128 devices in a mesh: dp: 16 (over x, y_lo, core), tensor: 8 (over y_hi, z).
Axes of the slice: x: 4, y: 4 (y_hi: 2, y_lo: 2; y = y_hi * 2 + y_lo), z: 4, core: 2. Of those that a mesh axis runs over, the one named last changes fastest.
Arguments:
- tokens: bfloat16 [24576, 1536], P(('dp', 'tensor')), may hold values from -6 to 6
- seq_lens: int32 [16, 4], P('dp'), may hold values from 0 to 1536, as said below
- query_key_value_weight: bfloat16 [1536, 3072], P(None, 'tensor'), may hold values from -0.15625 to 0.15625
- out_weight: bfloat16 [1536, 1536], P('tensor'), may hold values from -1 to 1
- gate_up_weight: bfloat16 [2, 1536, 4096], P(None, None, 'tensor'), may hold values from -0.15625 to 0.15625
- down_weight: bfloat16 [4096, 1536], P('tensor'), may hold values from -0.09375 to 0.09375
- norm_gains: float32 [2, 1536], replicated, may hold values from 0.5 to 1.5
- cotangent: bfloat16 [24576, 1536], P(('dp', 'tensor')), may hold values from -6 to 6
Outputs:
- mixed: bfloat16 [24576, 1536], P(('dp', 'tensor'))
- input_grad: float32 [24576, 1536], P(('dp', 'tensor'))
- qkv_grad: float32 [1536, 3072], P('dp', 'tensor')
- out_grad: float32 [1536, 1536], P('tensor', 'dp')
- gate_up_grad: float32 [2, 1536, 4096], P(None, 'dp', 'tensor')
- down_grad: float32 [4096, 1536], P('tensor', 'dp')
- gains_grad: float32 [2, 1536], P(None, 'dp')
The draws below stay inside these ranges and needn't reach their ends.
Inputs may be any that keep to these rules, and one draw needn't show every extreme that they name: `seq_lens`: row g lists the lengths of the sequences of data group g in slot order; each starts where the one before ends, rounded up to a multiple of 128 tokens, and all end within 1536 tokens; a zero is an empty slot. In every row the first or the second sequence begins within the group's first 192 token slots and ends within its last 192; in some row the first has exactly 1536 tokens.
All inputs are finite; a program needn't handle non-finite values.
Results may differ from the reference program's by a relative error of at most 0.028.
Values may be sent and summed in bfloat16 or wider, within the bound.
A program may use at most 192 MiB of HBM per device.

```python
import jax
import jax.numpy as jnp
from jax import lax

MODEL_WIDTH = 1536
HQ = 16
KEY_VALUE_HEADS = 8
HEAD_SIZE = 96
FF = 4096
BLOCK = 128
GROUPS = 16
GROUP_TOK = 1536
SHARD_TOK = 192
TOKENS = 24576


def round_up(values):
    return (values + BLOCK - 1) // BLOCK * BLOCK


def draw_seq_lens(key, part):
    key = jax.random.fold_in(key, 7)
    key_list = jax.random.split(key, 7)
    row_ids = jnp.arange(GROUPS, dtype=jnp.int32)
    front_room = (SHARD_TOK - 1) // BLOCK * BLOCK
    full_row = jax.random.randint(key_list[0], (), 0, GROUPS)
    is_full = row_ids == full_row
    leading = jax.random.randint(key_list[1], (GROUPS,), 0, 2)
    leading = jnp.where(is_full, 0, leading)
    before = jax.random.randint(key_list[2], (GROUPS,), 1, front_room + 1)
    before = jnp.where(leading == 1, before, 0)
    start = round_up(before)
    finish = jax.random.randint(key_list[3], (GROUPS,), GROUP_TOK - SHARD_TOK + 1, GROUP_TOK - BLOCK + 1)
    finish = jnp.where(is_full, GROUP_TOK, finish)
    spanning = finish - start
    room_left = GROUP_TOK - round_up(finish)
    raw_one = jax.random.randint(key_list[4], (GROUPS,), 0, 1 << 20)
    first_after = jnp.where(is_full, 0, 1 + raw_one % jnp.maximum(room_left, 1))
    room_left = room_left - round_up(first_after)
    raw_two = jax.random.randint(key_list[5], (GROUPS,), 0, 1 << 20)
    second_after = raw_two % (room_left + 1)
    room_left = room_left - round_up(second_after)
    raw_three = jax.random.randint(key_list[6], (GROUPS,), 0, 1 << 20)
    third_after = raw_three % (room_left + 1)
    has_front = leading == 1
    slot_zero = jnp.where(has_front, before, spanning)
    slot_one = jnp.where(has_front, spanning, first_after)
    slot_two = jnp.where(has_front, first_after, second_after)
    slot_three = jnp.where(has_front, second_after, third_after)
    return jnp.stack([slot_zero, slot_one, slot_two, slot_three], axis=1).astype(jnp.int32)


def shard_levels(stream_key, extent, shards, low, largest):
    def one(position, shards_of):
        heights = jax.random.uniform(jax.random.fold_in(jax.random.fold_in(stream_key, 6), position), (shards_of,), jnp.float32, low / len(shards), largest / len(shards))
        return jnp.repeat(jnp.exp(heights), extent[position] // shards_of).reshape((-1,) + (1,) * (len(extent) - position - 1))

    gain = one(*shards[0])
    for cut in shards[1:]:
        gain = gain * one(*cut)
    return gain


def scatter_about(rng, extent, deviation, most, shards=(), kind=jnp.bfloat16):
    values = jax.random.normal(rng, extent, jnp.float32) * deviation
    if len(shards) > 0:
        values = shard_levels(rng, extent, shards, -0.22, 0.18) * values
    return jnp.clip(values, min=-most, max=most).astype(kind)


def setup_inputs(seed: int = 0) -> dict:
    seeds = jax.random.split(jax.random.key(seed), 9)
    tokens = scatter_about(seeds[0], (TOKENS, MODEL_WIDTH), 1.0, 6.0, ((0, 128),))
    seq_lens = draw_seq_lens(jax.random.fold_in(seeds[8], 71), 0)
    query_key_value_weight = scatter_about(seeds[2], (MODEL_WIDTH, 4 * KEY_VALUE_HEADS * HEAD_SIZE), MODEL_WIDTH ** -0.5, 0.15625, ((1, 8),))
    out_weight = scatter_about(seeds[3], (HQ * HEAD_SIZE, MODEL_WIDTH), 32 ** -0.5, 1.0, ((0, 8),))
    gate_up_weight = scatter_about(seeds[4], (2, MODEL_WIDTH, FF), MODEL_WIDTH ** -0.5, 0.15625, ((2, 8),))
    down_weight = scatter_about(seeds[5], (FF, MODEL_WIDTH), FF ** -0.5, 0.09375, ((0, 8),))
    norm_gains = jnp.clip(1.0 + 0.1 * jax.random.normal(seeds[6], (2, MODEL_WIDTH), jnp.float32), 0.5, 1.5)
    cotangent = scatter_about(seeds[7], (TOKENS, MODEL_WIDTH), 1.0, 6.0, ((0, 128),))
    return dict(tokens=tokens, seq_lens=seq_lens, query_key_value_weight=query_key_value_weight, out_weight=out_weight, gate_up_weight=gate_up_weight, down_weight=down_weight, norm_gains=norm_gains, cotangent=cotangent)


EPSILON = 1e-05
THETA = 100000.0
HIGHEST = lax.Precision.HIGHEST

@jax.custom_vjp
def low(v):
    return lax.optimization_barrier(v.astype(jnp.bfloat16)).astype(jnp.float32)

@jax.custom_vjp
def low_back(v):
    return v

def low_keep(v):
    return (low(v), None)

def low_pass(kept, grad):
    return (grad,)

def back_keep(v):
    return (v, None)

def back_low(kept, grad):
    return (low(grad),)
low.defvjp(low_keep, low_pass)
low_back.defvjp(back_keep, back_low)

def layout(lengths, total_rows):
    padded_rows = (lengths + BLOCK - 1) // BLOCK * BLOCK
    starts = jnp.cumsum(padded_rows, dtype=jnp.int32) - padded_rows
    places = jnp.arange(total_rows, dtype=jnp.int32)[:, None]
    inside = (places >= starts[None, :]) & (places < (starts + lengths)[None, :])
    slot_ids = jnp.arange(lengths.shape[0], dtype=jnp.int32)
    segment = lax.optimization_barrier(jnp.sum(jnp.where(inside, slot_ids[None, :], 0), axis=1, dtype=jnp.int32))
    offset = lax.optimization_barrier(jnp.sum(jnp.where(inside, starts[None, :], 0), axis=1, dtype=jnp.int32))
    anywhere = jnp.any(inside, axis=1)
    positions = places[:, 0] - offset
    segment = jnp.where(anywhere, segment, lengths.shape[0] + places[:, 0])
    return (segment, positions)

def angles(positions):
    exponent = jnp.arange(0, HEAD_SIZE, 2, dtype=jnp.float32) / HEAD_SIZE
    inverse = jnp.power(THETA, -exponent)
    phases = positions.astype(jnp.float32)[:, None] * inverse[None, :]
    return (jnp.cos(phases), jnp.sin(phases))

def rotate(values, cos_part, sin_part):
    half_width = values.shape[-1] // 2
    first_half = values[..., :half_width]
    second_half = values[..., half_width:]
    return jnp.concatenate([first_half * cos_part - second_half * sin_part, second_half * cos_part + first_half * sin_part], axis=-1)

def attend_head(queries, keys_one, values_one, allowed):
    scores = jnp.einsum('tjd,kd->jtk', queries, keys_one, precision=HIGHEST) * HEAD_SIZE ** (-0.5)
    scores = low_back(scores)
    scores = jnp.where(allowed[None], scores, -1e+30)
    row_peak = lax.optimization_barrier(jnp.max(scores, axis=-1, keepdims=True))
    numerators = jnp.exp(scores - row_peak)
    softmax_weights = numerators / lax.optimization_barrier(jnp.sum(numerators, axis=-1, keepdims=True))
    return jnp.einsum('jtk,kd->tjd', low(softmax_weights), values_one, precision=HIGHEST)

def group_forward(hidden, segment, positions, query_key_value_weight, out_weight, gate_up_weight, down_weight, gain_values):
    count_of_rows = hidden.shape[0]
    scale_one = lax.rsqrt(lax.optimization_barrier(jnp.mean(hidden * hidden, axis=-1, keepdims=True)) + EPSILON)
    normed = low(hidden * scale_one * gain_values[0])
    projected_rows = low_back(jnp.dot(normed, query_key_value_weight, precision=HIGHEST, preferred_element_type=jnp.float32))
    projected_rows = projected_rows.reshape(count_of_rows, KEY_VALUE_HEADS, 4, HEAD_SIZE)
    cos_part, sin_part = angles(positions)
    queries = low(rotate(projected_rows[:, :, 0:2], cos_part[:, None, None], sin_part[:, None, None]))
    keys_all = low(rotate(projected_rows[:, :, 2], cos_part[:, None], sin_part[:, None]))
    values_all = low(projected_rows[:, :, 3])
    allowed = (segment[:, None] == segment[None, :]) & (positions[None, :] <= positions[:, None])
    attend = jax.checkpoint(lambda operands: attend_head(operands[0], operands[1], operands[2], allowed))
    head_outputs = lax.map(attend, (jnp.transpose(queries, (1, 0, 2, 3)), jnp.transpose(keys_all, (1, 0, 2)), jnp.transpose(values_all, (1, 0, 2))))
    mixed_heads = low(low_back(jnp.transpose(head_outputs, (1, 0, 2, 3)).reshape(count_of_rows, HQ * HEAD_SIZE)))
    branch = low_back(jnp.dot(mixed_heads, out_weight, precision=HIGHEST, preferred_element_type=jnp.float32))
    middle = hidden + branch
    scale_two = lax.rsqrt(lax.optimization_barrier(jnp.mean(middle * middle, axis=-1, keepdims=True)) + EPSILON)
    normed_two = low(middle * scale_two * gain_values[1])
    gate_up = low_back(jnp.einsum('td,cdf->ctf', normed_two, gate_up_weight, precision=HIGHEST))
    activated = low(jax.nn.silu(gate_up[0]) * gate_up[1])
    return middle + low_back(jnp.dot(activated, down_weight, precision=HIGHEST, preferred_element_type=jnp.float32))

def reference(tokens, seq_lens, query_key_value_weight, out_weight, gate_up_weight, down_weight, norm_gains, cotangent):
    segments, positions = jax.vmap(lambda lengths: layout(lengths, GROUP_TOK))(seq_lens)

    def forward(hidden, weight_qkv, weight_out, weight_gate_up, weight_down, gain_values):

        def one_group(operands):
            return group_forward(operands[0], operands[1], operands[2], weight_qkv, weight_out, weight_gate_up, weight_down, gain_values)
        grouped = lax.map(one_group, (hidden.reshape(GROUPS, GROUP_TOK, MODEL_WIDTH), segments, positions))
        return grouped.reshape(GROUPS * GROUP_TOK, MODEL_WIDTH)
    result, pullback = jax.vjp(forward, tokens.astype(jnp.float32), query_key_value_weight.astype(jnp.float32), out_weight.astype(jnp.float32), gate_up_weight.astype(jnp.float32), down_weight.astype(jnp.float32), norm_gains.astype(jnp.float32))
    gradients = pullback(cotangent.astype(jnp.float32))
    return (result.astype(jnp.bfloat16), gradients[0], gradients[1], gradients[2], gradients[3], gradients[4], gradients[5])
```

```python
import functools

import jax
import jax.numpy as jnp
import numpy as np
from jax import lax
from jax.experimental import pallas as pl
from jax.experimental.pallas import tpu as pltpu
from jax.sharding import Mesh
from jax.sharding import PartitionSpec as P

HEAD_SIZE = 96
BLOCK = 128
DP = ("x", "yl", "c")
TENSOR = ("yh", "z")
ALL = DP + TENSOR
SIZES = {"x": 4, "yl": 2, "c": 2, "yh": 2, "z": 4}
MESH = pl.DeviceIdType.MESH

EPSILON = 1e-05
THETA = 100000.0
masked_score = -1e30


def layout(lengths, total_rows):
    padded_rows = (lengths + BLOCK - 1) // BLOCK * BLOCK
    starts = jnp.cumsum(padded_rows, dtype=jnp.int32) - padded_rows
    places = jnp.arange(total_rows, dtype=jnp.int32)[:, None]
    inside = (places >= starts[None, :]) & (places < (starts + lengths)[None, :])
    slot_ids = jnp.arange(lengths.shape[0], dtype=jnp.int32)
    segment = jnp.sum(jnp.where(inside, slot_ids[None, :], 0), axis=1, dtype=jnp.int32)
    offset = jnp.sum(jnp.where(inside, starts[None, :], 0), axis=1, dtype=jnp.int32)
    anywhere = jnp.any(inside, axis=1)
    positions = places[:, 0] - offset
    segment = jnp.where(anywhere, segment, lengths.shape[0] + places[:, 0])
    return (segment, positions)


def angles(positions):
    exponent = jnp.arange(0, HEAD_SIZE, 2, dtype=jnp.float32) / HEAD_SIZE
    inverse = jnp.power(THETA, -exponent)
    phases = positions.astype(jnp.float32)[:, None] * inverse[None, :]
    return (jnp.cos(phases), jnp.sin(phases))


def rotate(values, cos_part, sin_part):
    half_width = values.shape[-1] // 2
    first_half = values[..., :half_width]
    second_half = values[..., half_width:]
    return jnp.concatenate(
        [
            first_half * cos_part - second_half * sin_part,
            second_half * cos_part + first_half * sin_part,
        ],
        axis=-1,
    )


def unrotate(values, cos_part, sin_part):
    return rotate(values, cos_part, -sin_part)


def times_transposed(left, right):
    return lax.dot_general(
        left, right, (((1,), (1,)), ((), ())), preferred_element_type=jnp.float32
    )


def transposed_times(left, right):
    return lax.dot_general(
        left, right, (((0,), (0,)), ((), ())), preferred_element_type=jnp.float32
    )


def normalize(values):
    scale = lax.rsqrt(jnp.mean(values * values, axis=-1, keepdims=True) + EPSILON)
    return (values * scale, scale)


def norm_back(grad_out, normalized, scale, gain_row):
    scaled = grad_out * gain_row
    return scale * (scaled - normalized * jnp.mean(scaled * normalized, axis=-1, keepdims=True))


def permutation(axes, move):
    shape = [SIZES[a] for a in axes]
    pairs = []
    for source in range(int(np.prod(shape))):
        place = dict(zip(axes, np.unravel_index(source, shape)))
        goal = move(place)
        pairs.append((source, int(np.ravel_multi_index([goal[a] for a in axes], shape))))
    return pairs


def to_other_core(value):
    return lax.ppermute(value, "c", [(0, 1), (1, 0)])


def to_cross(value):
    axes = ("yl", "yh")
    pairs = permutation(axes, lambda p: {"yl": 1 - p["yl"], "yh": 1 - p["yh"]})
    return lax.ppermute(value, axes, pairs)


def to_other_yl(value):
    return lax.ppermute(value, "yl", [(0, 1), (1, 0)])


def barrier_with(partners):
    barrier = pltpu.get_barrier_semaphore()
    for partner in partners:
        pl.semaphore_signal(barrier, inc=1, device_id=partner, device_id_type=MESH)
    pl.semaphore_wait(barrier, len(partners))


def gather_kernel(both, x_ref, o_ref, send_sem, recv_sem, local_sem):
    yh, z = lax.axis_index("yh"), lax.axis_index("z")
    after, before = lax.rem(z + 1, 4), lax.rem(z + 3, 4)
    other = 1 - yh
    right, left, across = {"z": after}, {"z": before}, {"yh": other}
    half = x_ref.shape[0] // 2
    lower, upper = pl.ds(0, half), pl.ds(half, half)
    whole = pl.ds(0, 2 * half)
    barrier_with([right, left, across] if both else [right, left])

    def place(block_yh, block_z, rows):
        if both:
            return o_ref.at[block_yh, block_z, rows]
        return o_ref.at[block_z, rows]

    def sent(slot, source, block_yh, block_z, rows, device):
        copy = pltpu.make_async_remote_copy(
            src_ref=source,
            dst_ref=place(block_yh, block_z, rows),
            send_sem=send_sem.at[slot],
            recv_sem=recv_sem.at[slot],
            device_id=device,
            device_id_type=MESH,
        )
        copy.start()
        return copy

    def passed(slot, block_yh, block_z, rows, device):
        return sent(slot, place(block_yh, block_z, rows), block_yh, block_z, rows, device)

    own = pltpu.make_async_copy(x_ref, place(yh, z, whole), local_sem)
    own.start()
    to_right = sent(0, x_ref, yh, z, whole, right)
    to_left = sent(1, x_ref, yh, z, whole, left)
    copies = [to_right, to_left]
    if both:
        to_across = sent(2, x_ref, yh, z, whole, across)
        copies.append(to_across)
    to_right.wait_recv()
    last = [passed(3, yh, before, lower, right)]
    to_left.wait_recv()
    last.append(passed(4, yh, after, upper, left))
    if both:
        to_across.wait_recv()
        far_right = passed(5, other, z, whole, right)
        far_left = passed(6, other, z, whole, left)
        copies += [far_right, far_left]
        far_right.wait_recv()
        last.append(passed(7, other, before, lower, right))
        far_left.wait_recv()
        last.append(passed(8, other, after, upper, left))
    for copy in last:
        copy.wait_recv()
    for copy in copies + last:
        copy.wait_send()
    own.wait()


def gathered(value, both, collective_id, name):
    blocks = (2, 4) if both else (4,)
    out = pl.pallas_call(
        functools.partial(gather_kernel, both),
        out_shape=jax.ShapeDtypeStruct((*blocks, *value.shape), value.dtype),
        in_specs=[pl.BlockSpec(memory_space=pl.ANY)],
        out_specs=pl.BlockSpec(memory_space=pl.ANY),
        scratch_shapes=[
            pltpu.SemaphoreType.DMA((9,)),
            pltpu.SemaphoreType.DMA((9,)),
            pltpu.SemaphoreType.DMA,
        ],
        compiler_params=pltpu.CompilerParams(collective_id=collective_id, has_side_effects=True),
        name=name,
    )(value)
    return out.reshape(-1, value.shape[-1])


def exchange_kernel(x_ref, o_ref, send_sem, recv_sem, local_sem):
    me = lax.axis_index("yh") * 4 + lax.axis_index("z")
    partners = []
    for step in range(1, 8):
        goal = lax.rem(me + step, 8)
        partners.append((goal, {"yh": lax.div(goal, 4), "z": lax.rem(goal, 4)}))
    barrier_with([device for _, device in partners])
    own = pltpu.make_async_copy(x_ref.at[me], o_ref.at[me], local_sem)
    own.start()
    copies = []
    for step, (goal, device) in enumerate(partners):
        copy = pltpu.make_async_remote_copy(
            src_ref=x_ref.at[goal],
            dst_ref=o_ref.at[me],
            send_sem=send_sem.at[step],
            recv_sem=recv_sem.at[step],
            device_id=device,
            device_id_type=MESH,
        )
        copy.start()
        copies.append(copy)
    for copy in copies:
        copy.wait()
    own.wait()


def exchanged(value, collective_id, name):
    return pl.pallas_call(
        exchange_kernel,
        out_shape=jax.ShapeDtypeStruct(value.shape, value.dtype),
        in_specs=[pl.BlockSpec(memory_space=pl.ANY)],
        out_specs=pl.BlockSpec(memory_space=pl.ANY),
        scratch_shapes=[
            pltpu.SemaphoreType.DMA((7,)),
            pltpu.SemaphoreType.DMA((7,)),
            pltpu.SemaphoreType.DMA,
        ],
        compiler_params=pltpu.CompilerParams(collective_id=collective_id, has_side_effects=True),
        name=name,
    )(value)


def core_slice(value, size, dim):
    return lax.dynamic_slice_in_dim(value, lax.axis_index("c") * size, size, dim)


def picked(value, index, dim):
    return lax.dynamic_index_in_dim(value, index, dim, keepdims=False)


def summed_over_cores(grad):
    core = lax.axis_index("c")
    parts = grad.reshape(*grad.shape[:-2], 8, 2, 96, grad.shape[-1])
    arrived = to_other_core(picked(parts, 1 - core, parts.ndim - 3))
    mine = picked(parts, core, parts.ndim - 3)
    return (mine.astype(jnp.float32) + arrived.astype(jnp.float32)).astype(jnp.bfloat16)


def summed_over_x(grad):
    lead = grad.shape[:-3]
    grad = grad.reshape(*lead, 4, 2 * 96, grad.shape[-1])
    out = lax.psum_scatter(grad, "x", scatter_dimension=len(lead), tiled=True)
    return out.reshape(*lead, 2, 96, grad.shape[-1])


def summed_over_yl(grad):
    yl = lax.axis_index("yl")
    arrived = to_other_yl(picked(grad, 1 - yl, grad.ndim - 3))
    return picked(grad, yl, grad.ndim - 3).astype(jnp.float32) + arrived.astype(jnp.float32)


def per_device(
    tokens,
    seq_lens,
    query_key_value_weight,
    out_weight,
    gate_up_weight,
    down_weight,
    norm_gains,
    cotangent,
):
    shard_rows = tokens.shape[0]
    group_rows = shard_rows * 8
    core, yh = lax.axis_index("c"), lax.axis_index("yh")
    block_rows = 512
    block_count = group_rows // block_rows
    scaling = HEAD_SIZE ** (-0.5)

    hidden = tokens.astype(jnp.float32)
    unit_one, scale_one = normalize(hidden)
    normed = (unit_one * norm_gains[0]).astype(jnp.bfloat16)

    gate_up_half = core_slice(gate_up_weight, 256, 2)
    down_half = core_slice(down_weight, 256, 0)
    gate_up_mine = to_cross(gate_up_half)
    down_mine = to_cross(down_half)
    gate_up_rest = to_other_core(gate_up_mine)
    down_rest = to_other_core(down_mine)
    out_half = core_slice(out_weight, 96, 0)
    out_halves = lax.all_gather(out_half, TENSOR, axis=0, tiled=True)
    out_all = lax.all_gather(out_halves, "c", axis=0, tiled=True)
    upstream_all = lax.all_gather(cotangent, "z", axis=0, tiled=True)

    normed_all = gathered(normed, True, 1, "gather_normed")
    projected_rows = jnp.dot(normed_all, query_key_value_weight, preferred_element_type=jnp.float32)
    projected_rows = projected_rows.reshape(group_rows, 4, HEAD_SIZE)
    segment, positions = layout(seq_lens[0], group_rows)
    cos_part, sin_part = angles(positions)
    queries = rotate(projected_rows[:, 0:2], cos_part[:, None], sin_part[:, None]).astype(
        jnp.bfloat16
    )
    keys_all = rotate(projected_rows[:, 2], cos_part, sin_part).astype(jnp.bfloat16)
    values_all = projected_rows[:, 3].astype(jnp.bfloat16)

    def block_scores(first_row):
        query_block = queries[first_row : first_row + block_rows]
        scores = (
            jnp.einsum("qjd,kd->jqk", query_block, keys_all, preferred_element_type=jnp.float32)
            * scaling
        )
        block_segment = segment[first_row : first_row + block_rows]
        block_positions = positions[first_row : first_row + block_rows]
        allowed = (block_segment[:, None] == segment[None, :]) & (
            positions[None, :] <= block_positions[:, None]
        )
        return (query_block, jnp.where(allowed[None], scores, masked_score))

    attended_list = []
    log_sums = []
    for block_index in range(block_count):
        scores = block_scores(block_index * block_rows)[1]
        row_peak = jnp.max(scores, axis=-1, keepdims=True)
        numerators = jnp.exp(scores - row_peak)
        totals = jnp.sum(numerators, axis=-1, keepdims=True)
        softmax_weights = (numerators / totals).astype(jnp.bfloat16)
        log_sums.append(row_peak + jnp.log(totals))
        attended = jnp.einsum(
            "jqk,kd->qjd", softmax_weights, values_all, preferred_element_type=jnp.float32
        )
        attended_list.append(attended.reshape(block_rows, 2 * HEAD_SIZE))
    mixed_heads = jnp.concatenate(attended_list, axis=0).astype(jnp.bfloat16)

    attended_here = exchanged(mixed_heads.reshape(8, shard_rows, 2 * HEAD_SIZE), 2, "exchange_out")
    attended_here = jnp.transpose(
        attended_here.reshape(8, shard_rows, 2, HEAD_SIZE), (1, 2, 0, 3)
    ).reshape(shard_rows, 16 * HEAD_SIZE)
    branch = jnp.dot(attended_here, out_all, preferred_element_type=jnp.float32)
    middle = hidden + branch
    unit_two, scale_two = normalize(middle)
    normed_two = (unit_two * norm_gains[1]).astype(jnp.bfloat16)
    normed_two_all = gathered(normed_two, False, 3, "gather_normed_two")

    in_order = core == 0
    gate_up_all = jnp.concatenate(
        [
            gate_up_weight,
            jnp.where(in_order, gate_up_mine, gate_up_rest),
            jnp.where(in_order, gate_up_rest, gate_up_mine),
        ],
        axis=2,
    )
    down_all = jnp.concatenate(
        [
            down_weight,
            jnp.where(in_order, down_mine, down_rest),
            jnp.where(in_order, down_rest, down_mine),
        ],
        axis=0,
    )
    gate_up = jnp.einsum(
        "td,cdf->ctf", normed_two_all, gate_up_all, preferred_element_type=jnp.float32
    )
    sigmoid_gate = jax.nn.sigmoid(gate_up[0])
    silu_gate = gate_up[0] * sigmoid_gate
    activated = (silu_gate * gate_up[1]).astype(jnp.bfloat16)
    upstream = cotangent.astype(jnp.float32)
    grad_act = times_transposed(upstream_all, down_all)
    grad_gate = grad_act * gate_up[1] * sigmoid_gate * (1.0 + gate_up[0] * (1.0 - sigmoid_gate))
    grad_upper = grad_act * silu_gate
    grad_gate_up = jnp.stack([grad_gate, grad_upper]).astype(jnp.bfloat16)
    normed_two_part = jnp.einsum(
        "ctf,cdf->td", grad_gate_up, gate_up_all, preferred_element_type=jnp.float32
    ).astype(jnp.bfloat16)
    grad_normed_two = lax.psum_scatter(
        normed_two_part, "z", scatter_dimension=0, tiled=True
    ).astype(jnp.float32)
    activated, normed_two_all, upstream_all, normed_two_part = lax.optimization_barrier(
        (activated, normed_two_all, upstream_all, normed_two_part)
    )
    ffn_out = lax.psum_scatter(
        jnp.dot(activated, down_all, preferred_element_type=jnp.float32).astype(jnp.bfloat16),
        "z",
        scatter_dimension=0,
        tiled=True,
    ).astype(jnp.float32)
    mixed = (middle + ffn_out).astype(jnp.bfloat16)
    down_grad = transposed_times(upstream_all, activated).astype(jnp.bfloat16)
    gate_up_grad = jnp.einsum(
        "td,ctf->cdf", normed_two_all, grad_gate_up, preferred_element_type=jnp.float32
    ).astype(jnp.bfloat16)
    ffn_grad = jnp.concatenate([gate_up_grad, down_grad[None]], axis=0)

    grad_middle = upstream + norm_back(grad_normed_two, unit_two, scale_two, norm_gains[1])
    grad_branch = grad_middle.astype(jnp.bfloat16)
    grad_heads = times_transposed(grad_branch, out_all).astype(jnp.bfloat16)
    grad_heads = jnp.transpose(
        grad_heads.reshape(shard_rows, 2, 8, HEAD_SIZE), (2, 0, 1, 3)
    ).reshape(8, shard_rows, 2 * HEAD_SIZE)
    grad_heads = exchanged(grad_heads, 4, "exchange_grad").reshape(group_rows, 2, HEAD_SIZE)
    out_grad = transposed_times(grad_branch, attended_here).astype(jnp.bfloat16)

    key_grad = jnp.zeros((group_rows, HEAD_SIZE), jnp.float32)
    value_grad = jnp.zeros((group_rows, HEAD_SIZE), jnp.float32)
    query_grads = []
    for block_index in range(block_count):
        first_row = block_index * block_rows
        query_block, scores = block_scores(first_row)
        softmax_weights = jnp.exp(scores - log_sums[block_index])
        soft_low = softmax_weights.astype(jnp.bfloat16)
        grad_block = grad_heads[first_row : first_row + block_rows]
        grad_weights = jnp.einsum(
            "qjd,kd->jqk", grad_block, values_all, preferred_element_type=jnp.float32
        )
        centered = jnp.sum(softmax_weights * grad_weights, axis=-1, keepdims=True)
        grad_scores = (softmax_weights * (grad_weights - centered)).astype(jnp.bfloat16)
        query_grads.append(
            jnp.einsum("jqk,kd->qjd", grad_scores, keys_all, preferred_element_type=jnp.float32)
            * scaling
        )
        key_grad = (
            key_grad
            + jnp.einsum("jqk,qjd->kd", grad_scores, query_block, preferred_element_type=jnp.float32)
            * scaling
        )
        value_grad = value_grad + jnp.einsum(
            "jqk,qjd->kd", soft_low, grad_block, preferred_element_type=jnp.float32
        )
    query_grad = unrotate(
        jnp.concatenate(query_grads, axis=0), cos_part[:, None], sin_part[:, None]
    )
    key_grad = unrotate(key_grad, cos_part, sin_part)
    grad_projected = jnp.concatenate(
        [query_grad, key_grad[:, None], value_grad[:, None]], axis=1
    )
    grad_projected = grad_projected.reshape(group_rows, 4 * HEAD_SIZE).astype(jnp.bfloat16)
    by_z = jnp.transpose(
        grad_projected.reshape(2, 4, shard_rows, 4 * HEAD_SIZE), (1, 0, 2, 3)
    ).reshape(group_rows, 4 * HEAD_SIZE)
    normed_part = times_transposed(by_z, query_key_value_weight).astype(jnp.bfloat16)
    grad_normed = lax.psum_scatter(normed_part, "z", scatter_dimension=0, tiled=True)
    grad_normed = lax.psum_scatter(grad_normed, "yh", scatter_dimension=0, tiled=True).astype(
        jnp.float32
    )
    grad_projected, normed_all, normed_part = lax.optimization_barrier(
        (grad_projected, normed_all, normed_part)
    )
    qkv_grad = transposed_times(normed_all, grad_projected).astype(jnp.bfloat16)
    input_grad = grad_middle + norm_back(grad_normed, unit_one, scale_one, norm_gains[0])

    ffn_grad = summed_over_x(summed_over_cores(ffn_grad))
    ffn_grad = (
        ffn_grad[..., :512].astype(jnp.float32) + to_cross(ffn_grad[..., 512:]).astype(jnp.float32)
    ).astype(jnp.bfloat16)
    ffn_grad = summed_over_yl(ffn_grad)
    out_grad = summed_over_x(summed_over_cores(out_grad))
    out_grad = jnp.transpose(out_grad.reshape(2, 96, 2, 2, 4, 96), (4, 3, 0, 1, 2, 5))
    out_grad = out_grad.reshape(4, 2, 2, 96, 192)
    out_grad = lax.psum_scatter(out_grad, "z", scatter_dimension=0, tiled=True)[0]
    out_grad = (
        picked(out_grad, yh, 0).astype(jnp.float32)
        + to_cross(picked(out_grad, 1 - yh, 0)).astype(jnp.float32)
    ).astype(jnp.bfloat16)
    out_grad = summed_over_yl(out_grad)
    qkv_grad = summed_over_yl(summed_over_x(summed_over_cores(qkv_grad)))

    first = ((lax.axis_index("x") * 2 + lax.axis_index("yl")) * 2 + core) * 96
    rows_one = lax.dynamic_slice_in_dim(query_key_value_weight, first, 96, 0).astype(jnp.float32)
    rows_two = lax.dynamic_slice_in_dim(gate_up_weight, first, 96, 1).astype(jnp.float32)
    gain_rows = lax.dynamic_slice_in_dim(norm_gains, first, 96, 1)
    gains_grad = jnp.stack(
        [
            jnp.sum(qkv_grad * rows_one, axis=1),
            jnp.sum(ffn_grad[0:2] * rows_two, axis=(0, 2)),
        ]
    )
    copies = jnp.broadcast_to(gains_grad, (8, *gains_grad.shape))
    copies = lax.all_to_all(copies, TENSOR, split_axis=0, concat_axis=0, tiled=True)
    gains_grad = jnp.sum(copies, axis=0) / gain_rows
    return (
        mixed,
        input_grad,
        qkv_grad,
        out_grad.T,
        ffn_grad[0:2],
        ffn_grad[2].T,
        gains_grad,
    )


def solution(mesh):
    split = Mesh(mesh.devices.reshape(4, 2, 2, 2, 4), ALL)
    placed = (
        P(ALL, None),
        P(DP, None),
        P(None, TENSOR),
        P(TENSOR, None),
        P(None, None, TENSOR),
        P(TENSOR, None),
        P(),
        P(ALL, None),
    )
    return jax.shard_map(
        per_device,
        mesh=split,
        in_specs=placed,
        out_specs=(
            P(ALL, None),
            P(ALL, None),
            P(DP, TENSOR),
            P(TENSOR, DP),
            P(None, DP, TENSOR),
            P(TENSOR, DP),
            P(None, DP),
        ),
        check_vma=False,
    )
```

```python
import functools

import jax
import jax.numpy as jnp
import numpy as np
from jax import lax
from jax.experimental import pallas as pl
from jax.experimental.pallas import tpu as pltpu
from jax.sharding import Mesh
from jax.sharding import PartitionSpec as P

HEAD_SIZE = 96
BLOCK = 128
DP = ("x", "yl", "c")
TENSOR = ("yh", "z")
ALL = DP + TENSOR
SIZES = {"x": 4, "yl": 2, "c": 2, "yh": 2, "z": 4}
MESH = pl.DeviceIdType.MESH

EPSILON = 1e-05
THETA = 100000.0
masked_score = -1e30


def layout(lengths, total_rows):
    padded_rows = (lengths + BLOCK - 1) // BLOCK * BLOCK
    starts = jnp.cumsum(padded_rows, dtype=jnp.int32) - padded_rows
    places = jnp.arange(total_rows, dtype=jnp.int32)[:, None]
    inside = (places >= starts[None, :]) & (places < (starts + lengths)[None, :])
    offset = jnp.sum(jnp.where(inside, starts[None, :], 0), axis=1, dtype=jnp.int32)
    anywhere = jnp.any(inside, axis=1)
    positions = places[:, 0] - offset
    first = jnp.where(anywhere, offset, places[:, 0])
    return (first, positions)


def angles(positions):
    exponent = jnp.arange(0, HEAD_SIZE, 2, dtype=jnp.float32) / HEAD_SIZE
    inverse = jnp.power(THETA, -exponent)
    phases = positions.astype(jnp.float32)[:, None] * inverse[None, :]
    return (jnp.cos(phases), jnp.sin(phases))


def spread_columns(weight):
    halves = weight.reshape(weight.shape[0], -1, HEAD_SIZE // 2)
    return jnp.pad(halves, ((0, 0), (0, 0), (0, 16))).reshape(weight.shape[0], -1)


def packed_columns(grad):
    return grad.reshape(grad.shape[0], -1, 64)[:, :, :48].reshape(grad.shape[0], -1)


def times_transposed(left, right):
    return lax.dot_general(
        left, right, (((1,), (1,)), ((), ())), preferred_element_type=jnp.float32
    )


def transposed_times(left, right):
    return lax.dot_general(
        left, right, (((0,), (0,)), ((), ())), preferred_element_type=jnp.float32
    )


def normalize(values):
    scale = lax.rsqrt(jnp.mean(values * values, axis=-1, keepdims=True) + EPSILON)
    return (values * scale, scale)


def norm_back(grad_out, normalized, scale, gain_row):
    scaled = grad_out * gain_row
    return scale * (scaled - normalized * jnp.mean(scaled * normalized, axis=-1, keepdims=True))


def permutation(axes, move):
    shape = [SIZES[a] for a in axes]
    pairs = []
    for source in range(int(np.prod(shape))):
        place = dict(zip(axes, np.unravel_index(source, shape)))
        goal = move(place)
        pairs.append((source, int(np.ravel_multi_index([goal[a] for a in axes], shape))))
    return pairs


def to_other_core(value):
    return lax.ppermute(value, "c", [(0, 1), (1, 0)])


def to_cross(value):
    axes = ("yl", "yh")
    pairs = permutation(axes, lambda p: {"yl": 1 - p["yl"], "yh": 1 - p["yh"]})
    return lax.ppermute(value, axes, pairs)


def to_other_yl(value):
    return lax.ppermute(value, "yl", [(0, 1), (1, 0)])


def barrier_with(partners):
    barrier = pltpu.get_barrier_semaphore()
    for partner in partners:
        pl.semaphore_signal(barrier, inc=1, device_id=partner, device_id_type=MESH)
    pl.semaphore_wait(barrier, len(partners))


def gather_kernel(both, x_ref, o_ref, send_sem, recv_sem, local_sem):
    yh, z = lax.axis_index("yh"), lax.axis_index("z")
    after, before = lax.rem(z + 1, 4), lax.rem(z + 3, 4)
    other = 1 - yh
    right, left, across = {"z": after}, {"z": before}, {"yh": other}
    half = x_ref.shape[0] // 2
    lower, upper = pl.ds(0, half), pl.ds(half, half)
    whole = pl.ds(0, 2 * half)
    barrier_with([right, left, across] if both else [right, left])

    def place(block_yh, block_z, rows):
        if both:
            return o_ref.at[block_yh, block_z, rows]
        return o_ref.at[block_z, rows]

    def sent(slot, source, block_yh, block_z, rows, device):
        copy = pltpu.make_async_remote_copy(
            src_ref=source,
            dst_ref=place(block_yh, block_z, rows),
            send_sem=send_sem.at[slot],
            recv_sem=recv_sem.at[slot],
            device_id=device,
            device_id_type=MESH,
        )
        copy.start()
        return copy

    def passed(slot, block_yh, block_z, rows, device):
        return sent(slot, place(block_yh, block_z, rows), block_yh, block_z, rows, device)

    own = pltpu.make_async_copy(x_ref, place(yh, z, whole), local_sem)
    own.start()
    to_right = sent(0, x_ref, yh, z, whole, right)
    to_left = sent(1, x_ref, yh, z, whole, left)
    copies = [to_right, to_left]
    if both:
        to_across = sent(2, x_ref, yh, z, whole, across)
        copies.append(to_across)
    to_right.wait_recv()
    last = [passed(3, yh, before, lower, right)]
    to_left.wait_recv()
    last.append(passed(4, yh, after, upper, left))
    if both:
        to_across.wait_recv()
        far_right = passed(5, other, z, whole, right)
        far_left = passed(6, other, z, whole, left)
        copies += [far_right, far_left]
        far_right.wait_recv()
        last.append(passed(7, other, before, lower, right))
        far_left.wait_recv()
        last.append(passed(8, other, after, upper, left))
    for copy in last:
        copy.wait_recv()
    for copy in copies + last:
        copy.wait_send()
    own.wait()


def gathered(value, both, collective_id, name):
    blocks = (2, 4) if both else (4,)
    out = pl.pallas_call(
        functools.partial(gather_kernel, both),
        out_shape=jax.ShapeDtypeStruct((*blocks, *value.shape), value.dtype),
        in_specs=[pl.BlockSpec(memory_space=pl.ANY)],
        out_specs=pl.BlockSpec(memory_space=pl.ANY),
        scratch_shapes=[
            pltpu.SemaphoreType.DMA((9,)),
            pltpu.SemaphoreType.DMA((9,)),
            pltpu.SemaphoreType.DMA,
        ],
        compiler_params=pltpu.CompilerParams(collective_id=collective_id, has_side_effects=True),
        name=name,
    )(value)
    return out.reshape(-1, value.shape[-1])


def kernel_copies(send_sem, recv_sem):
    def sent(slot, source, goal, device):
        copy = pltpu.make_async_remote_copy(
            src_ref=source,
            dst_ref=goal,
            send_sem=send_sem.at[slot],
            recv_sem=recv_sem.at[slot],
            device_id=device,
            device_id_type=MESH,
        )
        copy.start()
        return copy

    return sent


def tensor_partner(step):
    goal = lax.rem(lax.axis_index("yh") * 4 + lax.axis_index("z") + step, 8)
    return {"yh": lax.div(goal, 4), "z": lax.rem(goal, 4)}


def spread(values):
    gap = jnp.zeros((values.shape[0], 16), values.dtype)
    return jnp.concatenate([values[:, :48], gap, values[:, 48:], gap], axis=1)


def packed(values):
    return jnp.concatenate([values[:, :48], values[:, 64:112]], axis=1)


def score_block(key_block, query_block, first_row, key_start, query_start):
    scores = times_transposed(key_block, query_block) * (HEAD_SIZE ** (-0.5))
    keys = key_start + lax.broadcasted_iota(jnp.int32, scores.shape, 0)
    queries = lax.broadcasted_iota(jnp.int32, (1, scores.shape[1]), 1)
    queries = query_start + jnp.where(queries >= 192, queries - 192, queries)
    return scores, (keys >= first_row) & (keys <= queries)


KEYS = 256


def key_blocks(block):
    return lax.div(3 * block + 6, 4)


def attend_kernel(
    normed_ref,
    weight_ref,
    cos_ref,
    sin_ref,
    first_ref,
    out_weight_ref,
    gate_up_ref,
    down_ref,
    cotangent_ref,
    normed_all_ref,
    out_all_ref,
    gate_up_other_ref,
    down_other_ref,
    near_ref,
    here_ref,
    q_ref,
    k_ref,
    v_ref,
    o_ref,
    lse_ref,
    landed,
    scores,
    outgoing,
    send_sem,
    recv_sem,
    local_sem,
):
    x, yl, c = lax.axis_index("x"), lax.axis_index("yl"), lax.axis_index("c")
    yh, z = lax.axis_index("yh"), lax.axis_index("z")
    me = yh * 4 + z
    after, before, opposite = lax.rem(z + 1, 4), lax.rem(z + 3, 4), lax.rem(z + 2, 4)
    other = 1 - yh
    right, left, across = {"z": after}, {"z": before}, {"yh": other}
    x_after, x_before, x_far = lax.rem(x + 1, 4), lax.rem(x + 3, 4), lax.rem(x + 2, 4)
    x_right, x_left, core = {"x": x_after}, {"x": x_before}, {"c": 1 - c}

    def crossed(step):
        place = tensor_partner(step)
        return {**place, "yl": lax.rem(yl + yh + place["yh"], 2)}

    tensor_partners = [tensor_partner(step) for step in range(1, 8)]
    cross_partners = [{"yl": 1 - yl, "yh": other, "z": lax.rem(z + k, 4)} for k in range(4)]
    barrier_with(tensor_partners + cross_partners + [x_right, x_left, core])
    sent = kernel_copies(send_sem, recv_sem)

    lower, upper, whole = pl.ds(0, 96), pl.ds(96, 96), pl.ds(0, 192)

    def shard(slot, block_yh, block_z, rows, device):
        place = landed.at[block_yh, block_z, rows]
        return sent(slot, place, place, device)

    def gate_up_part(ref, quarter, half, part=pl.ds(0, 2)):
        rows = pl.ds(pl.multiple_of(quarter * 384, 16), 384)
        return ref.at[part, rows, pl.ds(pl.multiple_of(half * 256, 128), 256)]

    def down_part(ref, quarter, half, part=pl.ds(0, 128)):
        rows = pl.ds(pl.multiple_of(quarter * 128 + part.start, 16), part.size)
        return ref.at[rows, pl.ds(pl.multiple_of(half * 768, 128), 768)]

    def out_part(ref, quarter, half, part=pl.ds(1, 7)):
        rows = pl.ds(pl.multiple_of(quarter * 48, 16), 48)
        return ref.at[part, rows, pl.ds(pl.multiple_of(half * 768, 128), 768)]

    copies, awaited = [], []

    def keep(copy):
        copies.append(copy)
        return copy

    def await_later(copy):
        awaited.append(copy)
        return keep(copy)

    to_right = keep(sent(0, normed_ref, landed.at[yh, z], right))
    to_left = keep(sent(1, normed_ref, landed.at[yh, z], left))
    to_across = keep(sent(2, normed_ref, landed.at[yh, z], across))
    own = pltpu.make_async_copy(normed_ref, landed.at[yh, z], local_sem.at[0])
    own.start()
    own_out = pltpu.make_async_copy(out_weight_ref, out_all_ref.at[0], local_sem.at[1])
    own_out.start()
    near_own = pltpu.make_async_copy(cotangent_ref, near_ref.at[z], local_sem.at[2])
    near_own.start()
    gate_up_cross = keep(
        sent(9, gate_up_part(gate_up_ref, x, c), gate_up_part(gate_up_other_ref, x, c), crossed(4))
    )
    down_cross = keep(
        sent(10, down_part(down_ref, x, c), down_part(down_other_ref, x, c), crossed(4))
    )
    out_cross = []
    piece = out_weight_ref.at[
        pl.ds(pl.multiple_of(x * 48, 16), 48), pl.ds(pl.multiple_of(c * 768, 128), 768)
    ]
    for step in range(1, 8):
        goal = out_all_ref.at[
            8 - step, pl.ds(pl.multiple_of(x * 48, 16), 48), pl.ds(pl.multiple_of(c * 768, 128), 768)
        ]
        out_cross.append(keep(sent(10 + step, piece, goal, crossed(step))))
    own.wait()

    def project(block_yh, block_z):
        block = block_yh * 4 + block_z
        projected = jnp.dot(
            landed[block_yh, block_z], weight_ref[...], preferred_element_type=jnp.float32
        )
        rows = pl.ds(pl.multiple_of(block * 192, 16), 192)
        cos_part, sin_part = cos_ref[rows, :], sin_ref[rows, :]

        def turned(values):
            return (values * cos_part + pltpu.roll(values, 64, 1) * sin_part).astype(jnp.bfloat16)

        q_ref[block, 0:192, :] = turned(projected[:, 0:128])
        q_ref[block, 192:384, :] = turned(projected[:, 128:256])
        k_ref[rows, :] = turned(projected[:, 256:384])
        v_ref[rows, :] = projected[:, 384:512].astype(jnp.bfloat16)

    project(yh, z)
    to_right.wait_recv()
    last_right = keep(shard(3, yh, before, lower, right))
    to_left.wait_recv()
    last_left = keep(shard(4, yh, after, upper, left))
    project(yh, before)
    project(yh, after)

    def spread_out(base, part, ref, halves):
        goal = part(ref, x, c)
        return [
            keep(sent(base, goal, goal, x_right)),
            keep(sent(base + 1, goal, goal, x_left)),
            await_later(sent(base + 4, goal, goal, core)),
        ]

    def pass_on(base, part, ref, halves, arriving):
        arriving[0].wait_recv()
        first, second = part(ref, x_before, c), part(ref, x_before, c, halves[0])
        far = [keep(sent(base + 2, second, second, x_right))]
        await_later(sent(base + 5, first, first, core))
        arriving[1].wait_recv()
        first, second = part(ref, x_after, c), part(ref, x_after, c, halves[1])
        far.append(keep(sent(base + 3, second, second, x_left)))
        await_later(sent(base + 6, first, first, core))
        return far

    def finish(base, part, ref, halves, far):
        for k in range(2):
            far[k].wait_recv()
            goal = part(ref, x_far, c, halves[k])
            await_later(sent(base + 7 + k, goal, goal, core))

    gate_up_plan = (18, gate_up_part, gate_up_other_ref, (pl.ds(0, 1), pl.ds(1, 1)))
    down_plan = (27, down_part, down_other_ref, (pl.ds(0, 64), pl.ds(64, 64)))
    out_plan = (36, out_part, out_all_ref, (pl.ds(1, 4), pl.ds(5, 3)))

    gate_up_cross.wait_recv()
    gate_up_moves = spread_out(*gate_up_plan)
    down_cross.wait_recv()
    down_moves = spread_out(*down_plan)
    to_across.wait_recv()
    far_right = keep(shard(5, other, z, whole, right))
    far_left = keep(shard(6, other, z, whole, left))
    for copy in out_cross:
        copy.wait_recv()
    out_moves = spread_out(*out_plan)
    last_right.wait_recv()
    last_left.wait_recv()
    project(other, z)
    project(yh, opposite)
    far_right.wait_recv()
    far_last_right = keep(shard(7, other, before, lower, right))
    far_left.wait_recv()
    far_last_left = keep(shard(8, other, after, upper, left))
    await_later(sent(45, cotangent_ref, near_ref.at[z], right))
    await_later(sent(46, cotangent_ref, near_ref.at[z], left))
    project(other, before)
    project(other, after)
    gate_up_far = pass_on(*gate_up_plan, gate_up_moves)
    down_far = pass_on(*down_plan, down_moves)
    far_last_right.wait_recv()
    far_last_left.wait_recv()
    project(other, opposite)
    stored = pltpu.make_async_copy(landed, normed_all_ref, local_sem.at[3])
    stored.start()

    def outgoing_copy(block, step):
        return pltpu.make_async_remote_copy(
            src_ref=outgoing.at[block],
            dst_ref=here_ref.at[lax.rem(8 - step, 8)],
            send_sem=send_sem.at[47 + step],
            recv_sem=recv_sem.at[47 + step],
            device_id={"yh": lax.div(block, 4), "z": lax.rem(block, 4)},
            device_id_type=MESH,
        )

    def attend(block, carry):
        query_block = q_ref[block]
        first_row = first_ref[block]
        count = key_blocks(block)

        def score(j, peak):
            rows = pl.ds(pl.multiple_of(j * KEYS, KEYS), KEYS)
            block_scores, allowed = score_block(
                k_ref[rows, :], query_block, first_row, j * KEYS, block * 192
            )
            block_scores = jnp.where(allowed, block_scores, masked_score)
            scores[rows, :] = block_scores
            return jnp.maximum(peak, jnp.max(block_scores.reshape(KEYS // 8, 8, 384), axis=0))

        peak = lax.fori_loop(0, count, score, jnp.full((8, 384), masked_score, jnp.float32))
        peak = jnp.max(peak, axis=0, keepdims=True)

        def weigh(j, state):
            total, out = state
            rows = pl.ds(pl.multiple_of(j * KEYS, KEYS), KEYS)
            weights = jnp.exp(scores[rows, :] - peak)
            total = total + jnp.sum(weights.reshape(KEYS // 8, 8, 384), axis=0)
            out = out + transposed_times(weights.astype(jnp.bfloat16), v_ref[rows, :])
            return total, out

        total, out = lax.fori_loop(
            0,
            count,
            weigh,
            (jnp.zeros((8, 384), jnp.float32), jnp.zeros((384, 128), jnp.float32)),
        )
        total = jnp.sum(total, axis=0, keepdims=True)
        lse_ref[block] = peak + jnp.log(total)
        out = out * jnp.transpose(jnp.broadcast_to(1.0 / total, (128, 384)))
        o_ref[block] = out.astype(jnp.bfloat16)
        outgoing[block] = jnp.concatenate([packed(out[0:192]), packed(out[192:384])], axis=1).astype(
            jnp.bfloat16
        )
        step = lax.rem(block - me + 8, 8)

        @pl.when(step != 0)
        def _():
            outgoing_copy(block, step).start()

        @pl.when(step == 0)
        def _():
            pltpu.make_async_copy(outgoing.at[block], here_ref.at[0], local_sem.at[4]).start()

        return carry

    lax.fori_loop(0, 8, attend, 0)
    out_far = pass_on(*out_plan, out_moves)
    finish(*gate_up_plan, gate_up_far)
    finish(*down_plan, down_far)
    finish(*out_plan, out_far)
    for copy in awaited:
        copy.wait_recv()
    for copy in copies:
        copy.wait_send()
    for step in range(1, 8):
        outgoing_copy(lax.rem(me + step, 8), step).wait()
    pltpu.make_async_copy(outgoing.at[me], here_ref.at[0], local_sem.at[4]).wait()
    own_out.wait()
    near_own.wait()
    stored.wait()


ANY = pl.BlockSpec(memory_space=pl.ANY)
IN_VMEM = pl.BlockSpec(memory_space=pltpu.VMEM)


def attended(normed, weight, cos_part, sin_part, first, out_weight, gate_up, down, cotangent):
    def shape(dims, kind=jnp.bfloat16):
        return jax.ShapeDtypeStruct(dims, kind)

    return pl.pallas_call(
        attend_kernel,
        out_shape=(
            shape((2, 4, 192, 1536)),
            shape((8, 192, 1536)),
            shape((2, 1536, 512)),
            shape((512, 1536)),
            shape((4, 192, 1536)),
            shape((8, 192, 192)),
            shape((8, 384, 128)),
            shape((1536, 128)),
            shape((1536, 128)),
            shape((8, 384, 128)),
            shape((8, 1, 384), jnp.float32),
        ),
        in_specs=[IN_VMEM] * 5 + [ANY] * 4,
        out_specs=(ANY,) * 6 + (IN_VMEM,) * 5,
        scratch_shapes=[
            pltpu.VMEM((2, 4, 192, 1536), jnp.bfloat16),
            pltpu.VMEM((1536, 384), jnp.float32),
            pltpu.VMEM((8, 192, 192), jnp.bfloat16),
            pltpu.SemaphoreType.DMA((55,)),
            pltpu.SemaphoreType.DMA((55,)),
            pltpu.SemaphoreType.DMA((5,)),
        ],
        compiler_params=pltpu.CompilerParams(
            collective_id=1, has_side_effects=True, vmem_limit_bytes=48 * 2**20
        ),
        name="attend",
    )(normed, weight, cos_part, sin_part, first, out_weight, gate_up, down, cotangent)


def branch_kernel(tokens_ref, here_ref, out_ref, gain_ref, middle_ref, normed_ref):
    middle = tokens_ref[...].astype(jnp.float32)
    for k in range(8):
        middle += jnp.dot(here_ref[k], out_ref[k], preferred_element_type=jnp.float32)
    middle_ref[...] = middle
    scale = lax.rsqrt(jnp.mean(middle * middle, axis=1, keepdims=True) + EPSILON)
    normed_ref[...] = (middle * scale * gain_ref[...]).astype(jnp.bfloat16)


def branched(tokens, here, out_all, gain):
    return pl.pallas_call(
        branch_kernel,
        out_shape=(
            jax.ShapeDtypeStruct(tokens.shape, jnp.float32),
            jax.ShapeDtypeStruct(tokens.shape, jnp.bfloat16),
        ),
        compiler_params=pltpu.CompilerParams(vmem_limit_bytes=48 * 2**20),
        name="branch",
    )(tokens, here, out_all, gain)


def attend_back_kernel(
    dn_ref,
    middle_ref,
    gain_ref,
    cotangent_ref,
    out_ref,
    here_ref,
    q_ref,
    k_ref,
    v_ref,
    o_ref,
    lse_ref,
    first_ref,
    cos_ref,
    sin_ref,
    dh_ref,
    out_grad_ref,
    dp_ref,
    outgoing,
    landed,
    dk_sum,
    dv_sum,
    low,
    send_sem,
    recv_sem,
):
    me = lax.axis_index("yh") * 4 + lax.axis_index("z")
    barrier_with([tensor_partner(step) for step in range(1, 8)])

    middle = middle_ref[...]
    scale = lax.rsqrt(jnp.mean(middle * middle, axis=1, keepdims=True) + EPSILON)
    unit = middle * scale
    scaled = dn_ref[...].astype(jnp.float32) * gain_ref[...]
    dh = cotangent_ref[...].astype(jnp.float32) + scale * (
        scaled - unit * jnp.mean(scaled * unit, axis=1, keepdims=True)
    )
    dh_ref[...] = dh
    low[...] = dh.astype(jnp.bfloat16)
    copies = []
    sent = kernel_copies(send_sem, recv_sem)
    for step in range(1, 8):
        outgoing[step] = times_transposed(low[...], out_ref[step]).astype(jnp.bfloat16)
        copies.append(
            sent(step, outgoing.at[step], landed.at[8 - step], tensor_partner(step))
        )
    landed[0] = times_transposed(low[...], out_ref[0]).astype(jnp.bfloat16)
    for k in range(8):
        out_grad_ref[k] = transposed_times(here_ref[k], low[...]).astype(jnp.bfloat16)
    dk_sum[...] = jnp.zeros_like(dk_sum)
    dv_sum[...] = jnp.zeros_like(dv_sum)

    def unturned(values, rows):
        return values * cos_ref[rows, :] - pltpu.roll(values, 64, 1) * sin_ref[rows, :]

    def back(step, carry):
        block = lax.rem(me + step, 8)

        @pl.when(step != 0)
        def _():
            pltpu.make_async_remote_copy(
                src_ref=outgoing.at[step],
                dst_ref=landed.at[step],
                send_sem=send_sem.at[step],
                recv_sem=recv_sem.at[8 - step],
                device_id=tensor_partner(1),
                device_id_type=MESH,
            ).wait_recv()

        arrived = landed[step]
        grad_block = jnp.concatenate(
            [spread(arrived[:, 0:96]), spread(arrived[:, 96:192])], axis=0
        )
        query_block = q_ref[block]
        first_row, lse = first_ref[block], lse_ref[block]
        centered = grad_block.astype(jnp.float32) * o_ref[block].astype(jnp.float32)
        centered = jnp.sum(jnp.transpose(centered), axis=0, keepdims=True)

        def key_step(j, dq):
            rows = pl.ds(pl.multiple_of(j * KEYS, KEYS), KEYS)
            key_block, value_block = k_ref[rows, :], v_ref[rows, :]
            block_scores, allowed = score_block(
                key_block, query_block, first_row, j * KEYS, block * 192
            )
            weights = jnp.where(allowed, jnp.exp(block_scores - lse), 0.0)
            grad_weights = times_transposed(value_block, grad_block)
            grad_scores = (weights * (grad_weights - centered)).astype(jnp.bfloat16)
            dv_sum[rows, :] += jnp.dot(
                weights.astype(jnp.bfloat16), grad_block, preferred_element_type=jnp.float32
            )
            dk_sum[rows, :] += jnp.dot(
                grad_scores, query_block, preferred_element_type=jnp.float32
            )
            return dq + transposed_times(grad_scores, key_block)

        dq = lax.fori_loop(
            0, key_blocks(block), key_step, jnp.zeros((384, 128), jnp.float32)
        ) * (HEAD_SIZE ** (-0.5))
        rows = pl.ds(pl.multiple_of(block * 192, 16), 192)
        dp_ref[rows, 0:128] = unturned(dq[0:192], rows).astype(jnp.bfloat16)
        dp_ref[rows, 128:256] = unturned(dq[192:384], rows).astype(jnp.bfloat16)
        return carry

    lax.fori_loop(0, 8, back, 0)

    def finish(block, carry):
        rows = pl.ds(pl.multiple_of(block * 192, 16), 192)
        dk = dk_sum[rows, :] * (HEAD_SIZE ** (-0.5))
        dp_ref[rows, 256:384] = unturned(dk, rows).astype(jnp.bfloat16)
        dp_ref[rows, 384:512] = dv_sum[rows, :].astype(jnp.bfloat16)
        return carry

    lax.fori_loop(0, 8, finish, 0)
    for copy in copies:
        copy.wait_send()


def attended_back(*arguments):
    return pl.pallas_call(
        attend_back_kernel,
        out_shape=(
            jax.ShapeDtypeStruct((192, 1536), jnp.float32),
            jax.ShapeDtypeStruct((8, 192, 1536), jnp.bfloat16),
            jax.ShapeDtypeStruct((1536, 512), jnp.bfloat16),
        ),
        scratch_shapes=[
            pltpu.VMEM((8, 192, 192), jnp.bfloat16),
            pltpu.VMEM((8, 192, 192), jnp.bfloat16),
            pltpu.VMEM((1536, 128), jnp.float32),
            pltpu.VMEM((1536, 128), jnp.float32),
            pltpu.VMEM((192, 1536), jnp.bfloat16),
            pltpu.SemaphoreType.DMA((8,)),
            pltpu.SemaphoreType.DMA((8,)),
        ],
        compiler_params=pltpu.CompilerParams(
            collective_id=2, has_side_effects=True, vmem_limit_bytes=56 * 2**20
        ),
        name="attend_back",
    )(*arguments)


def picked(value, index, dim):
    return lax.dynamic_index_in_dim(value, index, dim, keepdims=False)


def added(one, two):
    return (one.astype(jnp.float32) + two.astype(jnp.float32)).astype(jnp.bfloat16)


def summed_over_cores(grad):
    core = lax.axis_index("c")
    count, _, columns = grad.shape
    parts = grad.reshape(count, 4, 2, 2, 96, columns)

    def chosen(which):
        part = picked(parts, which, 3).reshape(count, 4, 192, columns)
        return jnp.transpose(part, (1, 0, 2, 3))

    arrived = to_other_core(chosen(1 - core))
    return added(chosen(core), arrived)


def summed_over_x(grad):
    _, count, _, columns = grad.shape
    out = lax.psum_scatter(grad, "x", scatter_dimension=0, tiled=True)
    return jnp.transpose(out.reshape(count, 2, 96, columns), (1, 0, 2, 3))


def summed_over_yl(grad):
    yl = lax.axis_index("yl")
    arrived = to_other_yl(picked(grad, 1 - yl, 0))
    return picked(grad, yl, 0).astype(jnp.float32) + arrived.astype(jnp.float32)


def summed_out_grad(grad):
    core, yl, yh = lax.axis_index("c"), lax.axis_index("yl"), lax.axis_index("yh")
    me = yh * 4 + lax.axis_index("z")
    halves = grad.reshape(8, 2, 96, 4, 384)

    def chosen(which):
        return jnp.transpose(picked(halves, which, 1), (2, 0, 1, 3))

    grad = added(chosen(core), to_other_core(chosen(1 - core)))
    grad = lax.psum_scatter(grad, "x", scatter_dimension=0, tiled=True).reshape(8, 96, 384)
    grad = lax.dynamic_slice_in_dim(jnp.concatenate([grad, grad], axis=0), 8 - me, 8, 0)
    grad = jnp.transpose(grad.reshape(2, 4, 96, 384), (1, 0, 2, 3))
    grad = lax.psum_scatter(grad, "z", scatter_dimension=0, tiled=True).reshape(2, 96, 384)
    grad = added(picked(grad, yh, 0), to_cross(picked(grad, 1 - yh, 0)))
    grad = jnp.transpose(grad.reshape(96, 2, 192), (1, 0, 2))
    grad = added(picked(grad, yl, 0), to_other_yl(picked(grad, 1 - yl, 0)))
    grad = jnp.transpose(grad.reshape(96, 2, 96), (1, 0, 2))
    mine, theirs = picked(grad, core, 0), to_other_core(picked(grad, 1 - core, 0))
    in_order = core == 0
    return jnp.concatenate(
        [jnp.where(in_order, mine, theirs), jnp.where(in_order, theirs, mine)], axis=0
    ).astype(jnp.float32)


def per_device(
    tokens,
    seq_lens,
    query_key_value_weight,
    out_weight,
    gate_up_weight,
    down_weight,
    norm_gains,
    cotangent,
):
    shard_rows = tokens.shape[0]
    group_rows = shard_rows * 8
    core, yh = lax.axis_index("c"), lax.axis_index("yh")
    me = yh * 4 + lax.axis_index("z")

    hidden = tokens.astype(jnp.float32)
    unit_one, scale_one = normalize(hidden)
    normed = (unit_one * norm_gains[0]).astype(jnp.bfloat16)
    first, positions = layout(seq_lens[0], group_rows)
    cos_part, sin_part = angles(positions)
    gap = jnp.zeros((group_rows, 16), jnp.float32)
    cos_part = jnp.concatenate([cos_part, gap, cos_part, gap], axis=1)
    sin_part = jnp.concatenate([-sin_part, gap, sin_part, gap], axis=1)
    first = jnp.tile(first.reshape(8, 1, shard_rows), (1, 1, 2))
    weight_wide = spread_columns(query_key_value_weight)
    (
        normed_all,
        out_all,
        gate_up_other,
        down_other,
        upstream_near,
        attended_here,
        queries,
        keys_all,
        values_all,
        heads,
        log_sums,
    ) = attended(
        normed,
        weight_wide,
        cos_part,
        sin_part,
        first,
        out_weight,
        gate_up_weight,
        down_weight,
        cotangent,
    )
    normed_all = normed_all.reshape(group_rows, -1)

    middle, normed_two = branched(tokens, attended_here, out_all, norm_gains[1:2])
    normed_two_all = gathered(normed_two, False, 3, "gather_normed_two")
    upstream_all = gathered(cotangent, False, 4, "gather_upstream")
    gate_up_all = jnp.concatenate([gate_up_weight, gate_up_other], axis=2)
    down_all = jnp.concatenate([down_weight, down_other], axis=0)
    gate_up = jnp.einsum(
        "td,cdf->ctf", normed_two_all, gate_up_all, preferred_element_type=jnp.float32
    )
    sigmoid_gate = jax.nn.sigmoid(gate_up[0])
    silu_gate = gate_up[0] * sigmoid_gate
    activated = (silu_gate * gate_up[1]).astype(jnp.bfloat16)
    grad_act = times_transposed(upstream_all, down_all)
    grad_gate = grad_act * gate_up[1] * sigmoid_gate * (1.0 + gate_up[0] * (1.0 - sigmoid_gate))
    grad_upper = grad_act * silu_gate
    grad_gate_up = jnp.stack([grad_gate, grad_upper]).astype(jnp.bfloat16)
    normed_two_part = jnp.einsum(
        "ctf,cdf->td", grad_gate_up, gate_up_all, preferred_element_type=jnp.float32
    ).astype(jnp.bfloat16)
    grad_normed_two = lax.psum_scatter(normed_two_part, "z", scatter_dimension=0, tiled=True)
    activated, normed_two_all, upstream_all, normed_two_part = lax.optimization_barrier(
        (activated, normed_two_all, upstream_all, normed_two_part)
    )
    ffn_out = lax.psum_scatter(
        jnp.dot(activated, down_all, preferred_element_type=jnp.float32).astype(jnp.bfloat16),
        "z",
        scatter_dimension=0,
        tiled=True,
    ).astype(jnp.float32)
    mixed = (middle + ffn_out).astype(jnp.bfloat16)
    down_grad = transposed_times(upstream_all, activated).astype(jnp.bfloat16)
    gate_up_grad = jnp.einsum(
        "td,ctf->cdf", normed_two_all, grad_gate_up, preferred_element_type=jnp.float32
    ).astype(jnp.bfloat16)
    ffn_grad = jnp.concatenate([gate_up_grad, down_grad[None]], axis=0)

    grad_middle, out_grad, grad_projected = attended_back(
        grad_normed_two,
        middle,
        norm_gains[1:2],
        cotangent,
        out_all,
        attended_here,
        queries,
        keys_all,
        values_all,
        heads,
        log_sums,
        first,
        cos_part,
        sin_part,
    )
    by_z = jnp.transpose(
        grad_projected.reshape(2, 4, shard_rows, 512), (1, 0, 2, 3)
    ).reshape(group_rows, 512)
    normed_part = times_transposed(by_z, weight_wide).astype(jnp.bfloat16)
    grad_normed = lax.psum_scatter(normed_part, "z", scatter_dimension=0, tiled=True)
    grad_normed = lax.psum_scatter(grad_normed, "yh", scatter_dimension=0, tiled=True).astype(
        jnp.float32
    )
    grad_projected, normed_all, normed_part = lax.optimization_barrier(
        (grad_projected, normed_all, normed_part)
    )
    qkv_grad = transposed_times(normed_all, grad_projected).astype(jnp.bfloat16)
    qkv_grad = packed_columns(qkv_grad)
    input_grad = grad_middle + norm_back(grad_normed, unit_one, scale_one, norm_gains[0])

    ffn_grad = summed_over_x(summed_over_cores(ffn_grad))
    ffn_grad = (
        ffn_grad[..., :512].astype(jnp.float32) + to_cross(ffn_grad[..., 512:]).astype(jnp.float32)
    ).astype(jnp.bfloat16)
    ffn_grad = summed_over_yl(ffn_grad)
    qkv_grad = summed_over_yl(summed_over_x(summed_over_cores(qkv_grad[None])))[0]
    out_grad = summed_out_grad(out_grad)

    first = ((lax.axis_index("x") * 2 + lax.axis_index("yl")) * 2 + core) * 96
    rows_one = lax.dynamic_slice_in_dim(query_key_value_weight, first, 96, 0).astype(jnp.float32)
    rows_two = lax.dynamic_slice_in_dim(gate_up_weight, first, 96, 1).astype(jnp.float32)
    gain_rows = lax.dynamic_slice_in_dim(norm_gains, first, 96, 1)
    gains_grad = jnp.stack(
        [
            jnp.sum(qkv_grad * rows_one, axis=1),
            jnp.sum(ffn_grad[0:2] * rows_two, axis=(0, 2)),
        ]
    )
    copies = jnp.broadcast_to(gains_grad, (8, *gains_grad.shape))
    copies = lax.all_to_all(copies, TENSOR, split_axis=0, concat_axis=0, tiled=True)
    gains_grad = jnp.sum(copies, axis=0) / gain_rows
    return (
        mixed,
        input_grad,
        qkv_grad,
        out_grad,
        ffn_grad[0:2],
        ffn_grad[2].T,
        gains_grad,
    )


def solution(mesh):
    split = Mesh(mesh.devices.reshape(4, 2, 2, 2, 4), ALL)
    placed = (
        P(ALL, None),
        P(DP, None),
        P(None, TENSOR),
        P(TENSOR, None),
        P(None, None, TENSOR),
        P(TENSOR, None),
        P(),
        P(ALL, None),
    )
    return jax.shard_map(
        per_device,
        mesh=split,
        in_specs=placed,
        out_specs=(
            P(ALL, None),
            P(ALL, None),
            P(DP, TENSOR),
            P(TENSOR, DP),
            P(None, DP, TENSOR),
            P(TENSOR, DP),
            P(None, DP),
        ),
        check_vma=False,
    )
```

```python
import functools

import jax
import jax.numpy as jnp
import numpy as np
from jax import lax
from jax.experimental import pallas as pl
from jax.experimental.pallas import tpu as pltpu
from jax.sharding import Mesh
from jax.sharding import PartitionSpec as P

HEAD_SIZE = 96
BLOCK = 128
DP = ("x", "yl", "c")
TENSOR = ("yh", "z")
ALL = DP + TENSOR
SIZES = {"x": 4, "yl": 2, "c": 2, "yh": 2, "z": 4}
MESH = pl.DeviceIdType.MESH

EPSILON = 1e-05
THETA = 100000.0
masked_score = -1e30


def layout(lengths, total_rows):
    padded_rows = (lengths + BLOCK - 1) // BLOCK * BLOCK
    starts = jnp.cumsum(padded_rows, dtype=jnp.int32) - padded_rows
    places = jnp.arange(total_rows, dtype=jnp.int32)[:, None]
    inside = (places >= starts[None, :]) & (places < (starts + lengths)[None, :])
    offset = jnp.sum(jnp.where(inside, starts[None, :], 0), axis=1, dtype=jnp.int32)
    anywhere = jnp.any(inside, axis=1)
    positions = places[:, 0] - offset
    first = jnp.where(anywhere, offset, places[:, 0])
    return (first, positions)


def angles(positions):
    exponent = jnp.arange(0, HEAD_SIZE, 2, dtype=jnp.float32) / HEAD_SIZE
    inverse = jnp.power(THETA, -exponent)
    phases = positions.astype(jnp.float32)[:, None] * inverse[None, :]
    return (jnp.cos(phases), jnp.sin(phases))


def spread_columns(weight):
    halves = weight.reshape(weight.shape[0], -1, HEAD_SIZE // 2)
    return jnp.pad(halves, ((0, 0), (0, 0), (0, 16))).reshape(weight.shape[0], -1)


def packed_columns(grad):
    return grad.reshape(grad.shape[0], -1, 64)[:, :, :48].reshape(grad.shape[0], -1)


def times_transposed(left, right):
    return lax.dot_general(
        left, right, (((1,), (1,)), ((), ())), preferred_element_type=jnp.float32
    )


def transposed_times(left, right):
    return lax.dot_general(
        left, right, (((0,), (0,)), ((), ())), preferred_element_type=jnp.float32
    )


def normalize(values):
    scale = lax.rsqrt(jnp.mean(values * values, axis=-1, keepdims=True) + EPSILON)
    return (values * scale, scale)


def permutation(axes, move):
    shape = [SIZES[a] for a in axes]
    pairs = []
    for source in range(int(np.prod(shape))):
        place = dict(zip(axes, np.unravel_index(source, shape)))
        goal = move(place)
        pairs.append((source, int(np.ravel_multi_index([goal[a] for a in axes], shape))))
    return pairs


def to_other_core(value):
    return lax.ppermute(value, "c", [(0, 1), (1, 0)])


def to_cross(value):
    axes = ("yl", "yh")
    pairs = permutation(axes, lambda p: {"yl": 1 - p["yl"], "yh": 1 - p["yh"]})
    return lax.ppermute(value, axes, pairs)


def to_other_yl(value):
    return lax.ppermute(value, "yl", [(0, 1), (1, 0)])


def barrier_with(partners):
    barrier = pltpu.get_barrier_semaphore()
    for partner in partners:
        pl.semaphore_signal(barrier, inc=1, device_id=partner, device_id_type=MESH)
    pl.semaphore_wait(barrier, len(partners))


def gather_kernel(both, x_ref, o_ref, send_sem, recv_sem, local_sem):
    yh, z = lax.axis_index("yh"), lax.axis_index("z")
    after, before = lax.rem(z + 1, 4), lax.rem(z + 3, 4)
    other = 1 - yh
    right, left, across = {"z": after}, {"z": before}, {"yh": other}
    half = x_ref.shape[0] // 2
    lower, upper = pl.ds(0, half), pl.ds(half, half)
    whole = pl.ds(0, 2 * half)
    barrier_with([right, left, across] if both else [right, left])

    def place(block_yh, block_z, rows):
        if both:
            return o_ref.at[block_yh, block_z, rows]
        return o_ref.at[block_z, rows]

    def sent(slot, source, block_yh, block_z, rows, device):
        copy = pltpu.make_async_remote_copy(
            src_ref=source,
            dst_ref=place(block_yh, block_z, rows),
            send_sem=send_sem.at[slot],
            recv_sem=recv_sem.at[slot],
            device_id=device,
            device_id_type=MESH,
        )
        copy.start()
        return copy

    def passed(slot, block_yh, block_z, rows, device):
        return sent(slot, place(block_yh, block_z, rows), block_yh, block_z, rows, device)

    own = pltpu.make_async_copy(x_ref, place(yh, z, whole), local_sem)
    own.start()
    to_right = sent(0, x_ref, yh, z, whole, right)
    to_left = sent(1, x_ref, yh, z, whole, left)
    copies = [to_right, to_left]
    if both:
        to_across = sent(2, x_ref, yh, z, whole, across)
        copies.append(to_across)
    to_right.wait_recv()
    last = [passed(3, yh, before, lower, right)]
    to_left.wait_recv()
    last.append(passed(4, yh, after, upper, left))
    if both:
        to_across.wait_recv()
        far_right = passed(5, other, z, whole, right)
        far_left = passed(6, other, z, whole, left)
        copies += [far_right, far_left]
        far_right.wait_recv()
        last.append(passed(7, other, before, lower, right))
        far_left.wait_recv()
        last.append(passed(8, other, after, upper, left))
    for copy in last:
        copy.wait_recv()
    for copy in copies + last:
        copy.wait_send()
    own.wait()


def gathered(value, both, collective_id, name):
    blocks = (2, 4) if both else (4,)
    out = pl.pallas_call(
        functools.partial(gather_kernel, both),
        out_shape=jax.ShapeDtypeStruct((*blocks, *value.shape), value.dtype),
        in_specs=[pl.BlockSpec(memory_space=pl.ANY)],
        out_specs=pl.BlockSpec(memory_space=pl.ANY),
        scratch_shapes=[
            pltpu.SemaphoreType.DMA((9,)),
            pltpu.SemaphoreType.DMA((9,)),
            pltpu.SemaphoreType.DMA,
        ],
        compiler_params=pltpu.CompilerParams(collective_id=collective_id, has_side_effects=True),
        name=name,
    )(value)
    return out.reshape(-1, value.shape[-1])


def kernel_copies(send_sem, recv_sem):
    def sent(slot, source, goal, device):
        copy = pltpu.make_async_remote_copy(
            src_ref=source,
            dst_ref=goal,
            send_sem=send_sem.at[slot],
            recv_sem=recv_sem.at[slot],
            device_id=device,
            device_id_type=MESH,
        )
        copy.start()
        return copy

    return sent


def tensor_partner(step):
    goal = lax.rem(lax.axis_index("yh") * 4 + lax.axis_index("z") + step, 8)
    return {"yh": lax.div(goal, 4), "z": lax.rem(goal, 4)}


def spread(values):
    gap = jnp.zeros((values.shape[0], 16), values.dtype)
    return jnp.concatenate([values[:, :48], gap, values[:, 48:], gap], axis=1)


def packed(values):
    return jnp.concatenate([values[:, :48], values[:, 64:112]], axis=1)


KEYS = 256


def attend_kernel(
    normed_ref,
    weight_ref,
    cos_ref,
    sin_ref,
    first_ref,
    out_weight_ref,
    gate_up_ref,
    down_ref,
    cotangent_ref,
    normed_all_ref,
    out_all_ref,
    gate_up_other_ref,
    down_other_ref,
    near_ref,
    here_ref,
    q_ref,
    k_ref,
    v_ref,
    o_ref,
    lse_ref,
    landed,
    scores,
    outgoing,
    send_sem,
    recv_sem,
    local_sem,
):
    x, yl, c = lax.axis_index("x"), lax.axis_index("yl"), lax.axis_index("c")
    yh, z = lax.axis_index("yh"), lax.axis_index("z")
    me = yh * 4 + z
    after, before, opposite = lax.rem(z + 1, 4), lax.rem(z + 3, 4), lax.rem(z + 2, 4)
    other = 1 - yh
    right, left, across = {"z": after}, {"z": before}, {"yh": other}
    x_after, x_before, x_far = lax.rem(x + 1, 4), lax.rem(x + 3, 4), lax.rem(x + 2, 4)
    x_right, x_left, core = {"x": x_after}, {"x": x_before}, {"c": 1 - c}

    def crossed(step):
        place = tensor_partner(step)
        return {**place, "yl": lax.rem(yl + yh + place["yh"], 2)}

    tensor_partners = [tensor_partner(step) for step in range(1, 8)]
    cross_partners = [{"yl": 1 - yl, "yh": other, "z": lax.rem(z + k, 4)} for k in range(4)]
    barrier_with(tensor_partners + cross_partners + [x_right, x_left, core])
    sent = kernel_copies(send_sem, recv_sem)

    lower, upper, whole = pl.ds(0, 96), pl.ds(96, 96), pl.ds(0, 192)

    def shard(slot, block_yh, block_z, rows, device):
        place = landed.at[block_yh, block_z, rows]
        return sent(slot, place, place, device)

    def gate_up_part(ref, quarter, half, part=pl.ds(0, 2)):
        rows = pl.ds(pl.multiple_of(quarter * 384, 16), 384)
        return ref.at[part, rows, pl.ds(pl.multiple_of(half * 256, 128), 256)]

    def down_part(ref, quarter, half, part=pl.ds(0, 128)):
        rows = pl.ds(pl.multiple_of(quarter * 128 + part.start, 16), part.size)
        return ref.at[rows, pl.ds(pl.multiple_of(half * 768, 128), 768)]

    def out_part(ref, quarter, half, part=pl.ds(1, 7)):
        rows = pl.ds(pl.multiple_of(quarter * 48, 16), 48)
        return ref.at[part, rows, pl.ds(pl.multiple_of(half * 768, 128), 768)]

    copies, awaited = [], []

    def keep(copy):
        copies.append(copy)
        return copy

    def await_later(copy):
        awaited.append(copy)
        return keep(copy)

    to_right = keep(sent(0, normed_ref, landed.at[yh, z], right))
    to_left = keep(sent(1, normed_ref, landed.at[yh, z], left))
    to_across = keep(sent(2, normed_ref, landed.at[yh, z], across))
    own = pltpu.make_async_copy(normed_ref, landed.at[yh, z], local_sem.at[0])
    own.start()
    own_out = pltpu.make_async_copy(out_weight_ref, out_all_ref.at[0], local_sem.at[1])
    own_out.start()
    near_own = pltpu.make_async_copy(cotangent_ref, near_ref.at[z], local_sem.at[2])
    near_own.start()
    gate_up_cross = keep(
        sent(9, gate_up_part(gate_up_ref, x, c), gate_up_part(gate_up_other_ref, x, c), crossed(4))
    )
    down_cross = keep(
        sent(10, down_part(down_ref, x, c), down_part(down_other_ref, x, c), crossed(4))
    )
    out_cross = []
    piece = out_weight_ref.at[
        pl.ds(pl.multiple_of(x * 48, 16), 48), pl.ds(pl.multiple_of(c * 768, 128), 768)
    ]
    for step in range(1, 8):
        goal = out_all_ref.at[
            8 - step, pl.ds(pl.multiple_of(x * 48, 16), 48), pl.ds(pl.multiple_of(c * 768, 128), 768)
        ]
        out_cross.append(keep(sent(10 + step, piece, goal, crossed(step))))
    own.wait()

    def project(block_yh, block_z):
        block = block_yh * 4 + block_z
        projected = jnp.dot(
            landed[block_yh, block_z], weight_ref[...], preferred_element_type=jnp.float32
        )
        rows = pl.ds(pl.multiple_of(block * 192, 16), 192)
        cos_part, sin_part = cos_ref[rows, :], sin_ref[rows, :]

        def turned(values):
            return (values * cos_part + pltpu.roll(values, 64, 1) * sin_part).astype(jnp.bfloat16)

        q_ref[block, 0:192, :] = turned(projected[:, 0:128])
        q_ref[block, 192:384, :] = turned(projected[:, 128:256])
        k_ref[rows, :] = turned(projected[:, 256:384])
        v_ref[rows, :] = projected[:, 384:512].astype(jnp.bfloat16)

    project(yh, z)
    to_right.wait_recv()
    last_right = keep(shard(3, yh, before, lower, right))
    to_left.wait_recv()
    last_left = keep(shard(4, yh, after, upper, left))
    project(yh, before)
    project(yh, after)

    def spread_out(base, part, ref, halves):
        goal = part(ref, x, c)
        return [
            keep(sent(base, goal, goal, x_right)),
            keep(sent(base + 1, goal, goal, x_left)),
            await_later(sent(base + 4, goal, goal, core)),
        ]

    def pass_on(base, part, ref, halves, arriving):
        arriving[0].wait_recv()
        first, second = part(ref, x_before, c), part(ref, x_before, c, halves[0])
        far = [keep(sent(base + 2, second, second, x_right))]
        await_later(sent(base + 5, first, first, core))
        arriving[1].wait_recv()
        first, second = part(ref, x_after, c), part(ref, x_after, c, halves[1])
        far.append(keep(sent(base + 3, second, second, x_left)))
        await_later(sent(base + 6, first, first, core))
        return far

    def finish(base, part, ref, halves, far):
        for k in range(2):
            far[k].wait_recv()
            goal = part(ref, x_far, c, halves[k])
            await_later(sent(base + 7 + k, goal, goal, core))

    gate_up_plan = (18, gate_up_part, gate_up_other_ref, (pl.ds(0, 1), pl.ds(1, 1)))
    down_plan = (27, down_part, down_other_ref, (pl.ds(0, 64), pl.ds(64, 64)))
    out_plan = (36, out_part, out_all_ref, (pl.ds(1, 4), pl.ds(5, 3)))

    gate_up_cross.wait_recv()
    gate_up_moves = spread_out(*gate_up_plan)
    down_cross.wait_recv()
    down_moves = spread_out(*down_plan)
    to_across.wait_recv()
    far_right = keep(shard(5, other, z, whole, right))
    far_left = keep(shard(6, other, z, whole, left))
    for copy in out_cross:
        copy.wait_recv()
    out_moves = spread_out(*out_plan)
    last_right.wait_recv()
    last_left.wait_recv()
    project(other, z)
    project(yh, opposite)
    far_right.wait_recv()
    far_last_right = keep(shard(7, other, before, lower, right))
    far_left.wait_recv()
    far_last_left = keep(shard(8, other, after, upper, left))
    await_later(sent(45, cotangent_ref, near_ref.at[z], right))
    await_later(sent(46, cotangent_ref, near_ref.at[z], left))
    project(other, before)
    project(other, after)
    gate_up_far = pass_on(*gate_up_plan, gate_up_moves)
    down_far = pass_on(*down_plan, down_moves)
    far_last_right.wait_recv()
    far_last_left.wait_recv()
    project(other, opposite)
    stored = pltpu.make_async_copy(landed, normed_all_ref, local_sem.at[3])
    stored.start()

    def outgoing_copy(block, step):
        return pltpu.make_async_remote_copy(
            src_ref=outgoing.at[block],
            dst_ref=here_ref.at[8 - step],
            send_sem=send_sem.at[47 + step],
            recv_sem=recv_sem.at[47 + step],
            device_id={"yh": lax.div(block, 4), "z": lax.rem(block, 4)},
            device_id_type=MESH,
        )

    def attend(block):
        query_block = q_ref[block]
        first_row = first_ref[block]
        count = (192 * (block + 1) + KEYS - 1) // KEYS
        peak = jnp.full((8, 384), masked_score, jnp.float32)
        for j in range(count):
            rows = pl.ds(j * KEYS, KEYS)
            part, allowed = static_score(
                k_ref[rows, :], query_block, first_row, j * KEYS, block * 192
            )
            part = jnp.where(allowed, part, masked_score)
            scores[rows, :] = part
            peak = jnp.maximum(peak, jnp.max(part.reshape(KEYS // 8, 8, 384), axis=0))
        peak = jnp.max(peak, axis=0, keepdims=True)
        total = jnp.zeros((8, 384), jnp.float32)
        out = jnp.zeros((384, 128), jnp.float32)
        for j in range(count):
            rows = pl.ds(j * KEYS, KEYS)
            weights = jnp.exp(scores[rows, :] - peak)
            total = total + jnp.sum(weights.reshape(KEYS // 8, 8, 384), axis=0)
            out = out + transposed_times(low(weights), v_ref[rows, :])
        total = jnp.sum(total, axis=0, keepdims=True)
        lse_ref[block] = peak + jnp.log(total)
        out = out * jnp.transpose(jnp.broadcast_to(1.0 / total, (128, 384)))
        o_ref[block] = low(out)
        outgoing[block] = low(
            jnp.concatenate([packed(out[0:192]), packed(out[192:384])], axis=1)
        )
        step = lax.rem(block - me + 8, 8)

        @pl.when(step != 0)
        def _():
            outgoing_copy(block, step).start()

        @pl.when(step == 0)
        def _():
            pltpu.make_async_copy(outgoing.at[block], here_ref.at[0], local_sem.at[4]).start()

    for block in range(8):
        attend(block)
    out_far = pass_on(*out_plan, out_moves)
    finish(*gate_up_plan, gate_up_far)
    finish(*down_plan, down_far)
    finish(*out_plan, out_far)
    for copy in awaited:
        copy.wait_recv()
    for copy in copies:
        copy.wait_send()
    for step in range(1, 8):
        outgoing_copy(lax.rem(me + step, 8), step).wait()
    pltpu.make_async_copy(outgoing.at[me], here_ref.at[0], local_sem.at[4]).wait()
    own_out.wait()
    near_own.wait()
    stored.wait()


ANY = pl.BlockSpec(memory_space=pl.ANY)
IN_VMEM = pl.BlockSpec(memory_space=pltpu.VMEM)


def attended(normed, weight, cos_part, sin_part, first, out_weight, gate_up, down, cotangent):
    def shape(dims, kind=jnp.bfloat16):
        return jax.ShapeDtypeStruct(dims, kind)

    return pl.pallas_call(
        attend_kernel,
        out_shape=(
            shape((2, 4, 192, 1536)),
            shape((8, 192, 1536)),
            shape((2, 1536, 512)),
            shape((512, 1536)),
            shape((4, 192, 1536)),
            shape((8, 192, 192)),
            shape((8, 384, 128)),
            shape((1536, 128)),
            shape((1536, 128)),
            shape((8, 384, 128)),
            shape((8, 1, 384), jnp.float32),
        ),
        in_specs=[IN_VMEM] * 5 + [ANY] * 4,
        out_specs=(ANY,) * 6 + (IN_VMEM,) * 5,
        scratch_shapes=[
            pltpu.VMEM((2, 4, 192, 1536), jnp.bfloat16),
            pltpu.VMEM((1536, 384), jnp.float32),
            pltpu.VMEM((8, 192, 192), jnp.bfloat16),
            pltpu.SemaphoreType.DMA((55,)),
            pltpu.SemaphoreType.DMA((55,)),
            pltpu.SemaphoreType.DMA((5,)),
        ],
        compiler_params=pltpu.CompilerParams(
            collective_id=1, has_side_effects=True, vmem_limit_bytes=48 * 2**20
        ),
        name="attend",
    )(normed, weight, cos_part, sin_part, first, out_weight, gate_up, down, cotangent)


def branch_kernel(tokens_ref, here_ref, out_ref, gain_ref, middle_ref, normed_ref):
    middle = tokens_ref[...].astype(jnp.float32)
    for k in range(8):
        middle += jnp.dot(here_ref[k], out_ref[k], preferred_element_type=jnp.float32)
    middle_ref[...] = middle
    scale = lax.rsqrt(jnp.mean(middle * middle, axis=1, keepdims=True) + EPSILON)
    normed_ref[...] = (middle * scale * gain_ref[...]).astype(jnp.bfloat16)


def branched(tokens, here, out_all, gain):
    return pl.pallas_call(
        branch_kernel,
        out_shape=(
            jax.ShapeDtypeStruct(tokens.shape, jnp.float32),
            jax.ShapeDtypeStruct(tokens.shape, jnp.bfloat16),
        ),
        compiler_params=pltpu.CompilerParams(vmem_limit_bytes=48 * 2**20),
        name="branch",
    )(tokens, here, out_all, gain)


def static_score(key_block, query_block, first_row, key_start, query_start):
    scores = times_transposed(key_block, query_block) * (HEAD_SIZE ** (-0.5))
    keys = key_start + lax.broadcasted_iota(jnp.int32, scores.shape, 0)
    queries = lax.broadcasted_iota(jnp.int32, (1, scores.shape[1]), 1)
    queries = query_start + jnp.where(queries >= 192, queries - 192, queries)
    return scores, (keys >= first_row) & (keys <= queries)


def columns(start, size):
    return pl.ds(pl.multiple_of(start, 128), size)


def lines(start, size):
    return pl.ds(pl.multiple_of(start, 16), size)


def wide(value):
    return value.astype(jnp.float32)


def low(value):
    return value.astype(jnp.bfloat16)


def back_kernel(
    dn_ref,
    middle_ref,
    tokens_ref,
    gain_ref,
    cotangent_ref,
    out_ref,
    here_ref,
    q_ref,
    k_ref,
    v_ref,
    o_ref,
    lse_ref,
    first_ref,
    cos_ref,
    sin_ref,
    weight_ref,
    normed_ref,
    ffn_ref,
    gate_up_ref,
    input_grad_ref,
    qkv_grad_ref,
    out_grad_ref,
    ffn_grad_ref,
    gains_ref,
    outgoing,
    landed,
    dk_sum,
    dv_sum,
    dhb,
    dp,
    normed,
    ffn_right,
    ffn_left,
    ffn_own,
    ffn_far_a,
    ffn_far_b,
    ffn_from_left,
    ffn_from_right,
    ffn_cross,
    ffn_crossed,
    ffn_yl,
    ffn_yl_in,
    out_part,
    out_core,
    out_far_a,
    out_far_b,
    out_from_left,
    out_from_right,
    out_sum,
    out_shards,
    out_yl,
    out_yl_in,
    out_swap,
    out_swap_in,
    qkv_part,
    qkv_core,
    qkv_far_a,
    qkv_far_b,
    qkv_from_left,
    qkv_from_right,
    qkv_yl,
    qkv_yl_in,
    far_out,
    near_out,
    far_a,
    far_b,
    from_left,
    from_right,
    across_out,
    across_in,
    gain_out,
    gain_in,
    gate_up_rows,
    send_sem,
    recv_sem,
    local_sem,
):
    x, yl, c = lax.axis_index("x"), lax.axis_index("yl"), lax.axis_index("c")
    yh, z = lax.axis_index("yh"), lax.axis_index("z")
    me = yh * 4 + z
    place = (x * 2 + yl) * 2 + c
    after, before, opposite = lax.rem(z + 1, 4), lax.rem(z + 3, 4), lax.rem(z + 2, 4)
    x_after, x_before, x_far = lax.rem(x + 1, 4), lax.rem(x + 3, 4), lax.rem(x + 2, 4)
    right, left, across = {"z": after}, {"z": before}, {"yh": 1 - yh}
    x_right, x_left = {"x": x_after}, {"x": x_before}
    core, other_yl, cross = {"c": 1 - c}, {"yl": 1 - yl}, {"yl": 1 - yl, "yh": 1 - yh}
    barrier_with(
        [tensor_partner(step) for step in range(1, 8)] + [x_right, x_left, core, other_yl, cross]
    )
    raw_sent = kernel_copies(send_sem, recv_sem)
    copies = []
    slots = iter(range(SLOTS))

    def sent(source, goal, device):
        copy = raw_sent(next(slots), source, goal, device)
        copies.append(copy)
        return copy

    def arrived(pair):
        for copy in pair:
            copy.wait_recv()

    def fetched(slot, source, goal):
        copy = pltpu.make_async_copy(source, goal, local_sem.at[slot])
        copy.start()
        return copy

    ffn_first = [
        sent(ffn_ref.at[x_far, pl.ds(0, 288)], ffn_far_a, x_right),
        sent(ffn_ref.at[x_far, pl.ds(288, 288)], ffn_far_b, x_left),
    ]
    ffn_loads = [
        fetched(0, ffn_ref.at[x_after], ffn_right),
        fetched(1, ffn_ref.at[x_before], ffn_left),
        fetched(2, ffn_ref.at[x], ffn_own),
    ]
    normed_load = fetched(3, normed_ref, normed)
    rows_load = fetched(4, gate_up_ref.at[:, lines(place * 96, 96), :], gate_up_rows)

    middle = middle_ref[...]
    scale = lax.rsqrt(jnp.mean(middle * middle, axis=1, keepdims=True) + EPSILON)
    unit = middle * scale
    scaled = wide(dn_ref[...]) * gain_ref[1:2, :]
    dh = wide(cotangent_ref[...]) + scale * (
        scaled - unit * jnp.mean(scaled * unit, axis=1, keepdims=True)
    )
    input_grad_ref[...] = dh
    dhb[...] = low(dh)
    slot_base = [next(slots) for _ in range(8)][0]
    for step in range(1, 8):
        outgoing[step] = low(times_transposed(dhb[...], out_ref[step]))
        copies.append(
            raw_sent(
                slot_base + step, outgoing.at[step], landed.at[8 - step], tensor_partner(step)
            )
        )
    landed[0] = low(times_transposed(dhb[...], out_ref[0]))
    for k in range(8):
        out_part[k] = low(transposed_times(here_ref[k], dhb[...]))
    out_cored = sent(out_part.at[:, lines((1 - c) * 96, 96), :], out_core, core)
    dk_sum[...] = jnp.zeros_like(dk_sum)
    dv_sum[...] = jnp.zeros_like(dv_sum)

    def unturned(values, rows):
        return values * cos_ref[rows, :] - pltpu.roll(values, 64, 1) * sin_ref[rows, :]

    def await_block(step):
        pltpu.make_async_remote_copy(
            src_ref=outgoing.at[step],
            dst_ref=landed.at[step],
            send_sem=send_sem.at[slot_base + step],
            recv_sem=recv_sem.at[slot_base + 8 - step],
            device_id=tensor_partner(1),
            device_id_type=MESH,
        ).wait_recv()

    def back(block):
        step = lax.rem(block - me + 8, 8)

        @pl.when(step != 0)
        def _():
            await_block(step)

        grads = landed[step]
        grad_block = jnp.concatenate([spread(grads[:, 0:96]), spread(grads[:, 96:192])], axis=0)
        query_block = q_ref[block]
        first_row, lse = first_ref[block], lse_ref[block]
        centered = wide(grad_block) * wide(o_ref[block])
        centered = jnp.sum(jnp.transpose(centered), axis=0, keepdims=True)
        dq = jnp.zeros((384, 128), jnp.float32)
        for j in range((192 * (block + 1) + KEYS - 1) // KEYS):
            rows = pl.ds(j * KEYS, KEYS)
            key_block, value_block = k_ref[rows, :], v_ref[rows, :]
            scores, allowed = static_score(
                key_block, query_block, first_row, j * KEYS, block * 192
            )
            weights = jnp.where(allowed, jnp.exp(scores - lse), 0.0)
            grad_weights = times_transposed(value_block, grad_block)
            grad_scores = low(weights * (grad_weights - centered))
            dv_sum[rows, :] += jnp.dot(
                low(weights), grad_block, preferred_element_type=jnp.float32
            )
            dk_sum[rows, :] += jnp.dot(
                grad_scores, query_block, preferred_element_type=jnp.float32
            )
            dq = dq + transposed_times(grad_scores, key_block)
        dq = dq * (HEAD_SIZE ** (-0.5))
        rows = pl.ds(block * 192, 192)
        dp[rows, 0:128] = low(unturned(dq[0:192], rows))
        dp[rows, 128:256] = low(unturned(dq[192:384], rows))

    for block in range(4):
        back(block)
    out_cored.wait_recv()
    half = lines(c * 96, 96)
    for k in range(8):
        out_part[k, half, :] = low(wide(out_part[k, half, :]) + wide(out_core[k]))
    out_first = [
        sent(out_part.at[pl.ds(0, 4), half, columns(x_far * 384, 384)], out_far_a, x_right),
        sent(out_part.at[pl.ds(4, 4), half, columns(x_far * 384, 384)], out_far_b, x_left),
    ]
    for block in range(4, 7):
        back(block)
    arrived(ffn_first)
    for load in ffn_loads:
        load.wait()
    ffn_right[0:288] = low(wide(ffn_right[0:288]) + wide(ffn_far_a[...]))
    ffn_left[288:576] = low(wide(ffn_left[288:576]) + wide(ffn_far_b[...]))
    ffn_second = [
        sent(ffn_right, ffn_from_left, x_right),
        sent(ffn_left, ffn_from_right, x_left),
    ]
    back(7)
    for block in range(8):
        rows = pl.ds(block * 192, 192)
        dp[rows, 256:384] = low(unturned(dk_sum[rows, :] * (HEAD_SIZE ** (-0.5)), rows))
        dp[rows, 384:512] = low(dv_sum[rows, :])

    def partial(block_yh, block_z):
        rows = lines((block_yh * 4 + block_z) * 192, 192)
        return times_transposed(dp[rows, :], weight_ref[...])

    sides = (1 - yh, yh)
    far = []
    for k in range(2):
        far_out[k] = low(partial(sides[k], opposite))
        far.append(
            [
                sent(far_out.at[k, pl.ds(0, 96)], far_a.at[k], right),
                sent(far_out.at[k, pl.ds(96, 96)], far_b.at[k], left),
            ]
        )
    out_cols = [columns(place_x * 384, 384) for place_x in (x_after, x_before)]
    near = []
    for k in range(2):
        to_right, to_left = partial(sides[k], after), partial(sides[k], before)
        arrived(far[k])
        near_out[k, 0, 0:96] = low(to_right[0:96] + wide(far_a[k]))
        near_out[k, 0, 96:192] = low(to_right[96:192])
        near_out[k, 1, 0:96] = low(to_left[0:96])
        near_out[k, 1, 96:192] = low(to_left[96:192] + wide(far_b[k]))
        near.append(
            [
                sent(near_out.at[k, 0], from_left.at[k], right),
                sent(near_out.at[k, 1], from_right.at[k], left),
            ]
        )
    normed_load.wait()
    for part in range(4):
        features = pl.ds(part * 384, 384)
        grad = transposed_times(normed[:, features], dp[...])
        qkv_part[part * 2 : part * 2 + 2] = low(grad).reshape(2, 2, 96, 512)
    qkv_cored = sent(qkv_part.at[:, 1 - c], qkv_core, core)
    arrived(out_first)
    for k in range(4):
        out_part[k, half, out_cols[0]] = low(
            wide(out_part[k, half, out_cols[0]]) + wide(out_far_a[k])
        )
        out_part[4 + k, half, out_cols[1]] = low(
            wide(out_part[4 + k, half, out_cols[1]]) + wide(out_far_b[k])
        )
    out_second = [
        sent(out_part.at[:, half, out_cols[0]], out_from_left, x_right),
        sent(out_part.at[:, half, out_cols[1]], out_from_right, x_left),
    ]
    own = [partial(sides[k], z) for k in range(2)]
    qkv_cored.wait_recv()
    for k in range(8):
        qkv_part[k, c] = low(wide(qkv_part[k, c]) + wide(qkv_core[k]))
    qkv_first = [
        sent(qkv_part.at[x_far * 2, c], qkv_far_a, x_right),
        sent(qkv_part.at[x_far * 2 + 1, c], qkv_far_b, x_left),
    ]
    arrived(near[0])
    across_out[...] = low(own[0] + wide(from_left[0]) + wide(from_right[0]))
    crossing = sent(across_out, across_in, across)
    arrived(ffn_second)
    ffn_sum = wide(ffn_own[...]) + wide(ffn_from_left[...]) + wide(ffn_from_right[...])
    ffn_cross[...] = low(ffn_sum[:, 512:1024])
    ffn_own[:, 0:512] = low(ffn_sum[:, 0:512])
    ffn_crossing = sent(ffn_cross, ffn_crossed, cross)
    arrived(qkv_first)
    qkv_part[x_after * 2, c] = low(wide(qkv_part[x_after * 2, c]) + wide(qkv_far_a[...]))
    qkv_part[x_before * 2 + 1, c] = low(
        wide(qkv_part[x_before * 2 + 1, c]) + wide(qkv_far_b[...])
    )
    qkv_second = [
        sent(qkv_part.at[pl.ds(x_after * 2, 2), c], qkv_from_left, x_right),
        sent(qkv_part.at[pl.ds(x_before * 2, 2), c], qkv_from_right, x_left),
    ]
    arrived(out_second)
    own_cols = columns(x * 384, 384)
    for k in range(8):
        out_sum[k] = low(
            wide(out_part[k, half, own_cols]) + wide(out_from_left[k]) + wide(out_from_right[k])
        )
    out_shared = [
        sent(out_sum.at[step], out_shards.at[step - 1], tensor_partner(step))
        for step in range(1, 8)
    ]
    ffn_crossing.wait_recv()
    ffn_sum = wide(ffn_own[:, 0:512]) + wide(ffn_crossed[...])
    ffn_sum = ffn_sum.reshape(3, 2, 96, 512)
    keep_yl = jnp.where(yl == 0, ffn_sum[:, 0], ffn_sum[:, 1])
    ffn_yl[...] = low(jnp.where(yl == 0, ffn_sum[:, 1], ffn_sum[:, 0]))
    ffn_ending = sent(ffn_yl, ffn_yl_in, other_yl)
    ffn_grad_ref[...] = keep_yl
    arrived(qkv_second)
    qkv_sum = (
        wide(qkv_part[pl.ds(x * 2, 2), c]) + wide(qkv_from_left[...]) + wide(qkv_from_right[...])
    )
    qkv_grad_ref[...] = jnp.where(yl == 0, qkv_sum[0], qkv_sum[1])
    qkv_yl[...] = low(jnp.where(yl == 0, qkv_sum[1], qkv_sum[0]))
    qkv_ending = sent(qkv_yl, qkv_yl_in, other_yl)
    arrived(out_shared)
    total = wide(out_sum[0])
    for k in range(7):
        total = total + wide(out_shards[k])
    keep_out = jnp.where(yl == 0, total[:, 0:192], total[:, 192:384])
    out_yl[...] = low(jnp.where(yl == 0, total[:, 192:384], total[:, 0:192]))
    out_ending = sent(out_yl, out_yl_in, other_yl)
    ffn_ending.wait_recv()
    ffn_final = ffn_grad_ref[...] + wide(ffn_yl_in[...])
    ffn_grad_ref[...] = ffn_final
    qkv_ending.wait_recv()
    qkv_final = qkv_grad_ref[...] + wide(qkv_yl_in[...])
    qkv_grad_ref[...] = qkv_final
    rows_load.wait()
    gain_one = jnp.sum(
        qkv_final * wide(weight_ref[lines(place * 96, 96), :]), axis=1, keepdims=True
    )
    gain_two = jnp.sum(
        ffn_final[0] * wide(gate_up_rows[0]) + ffn_final[1] * wide(gate_up_rows[1]),
        axis=1,
        keepdims=True,
    )
    lanes = lax.broadcasted_iota(jnp.int32, (96, 128), 1)
    gain_out[...] = jnp.where(lanes == 0, gain_one, jnp.where(lanes == 1, gain_two, 0.0))
    gain_shared = [
        sent(gain_out, gain_in.at[step - 1], tensor_partner(step)) for step in range(1, 8)
    ]
    out_ending.wait_recv()
    out_final = keep_out + wide(out_yl_in[...])
    out_swap[...] = low(jnp.where(c == 0, out_final[:, 96:192], out_final[:, 0:96]))
    out_swapped = sent(out_swap, out_swap_in, core)
    out_mine = jnp.where(c == 0, out_final[:, 0:96], out_final[:, 96:192])
    out_grad_ref[half, :] = out_mine
    arrived(near[1])
    dn = own[1] + wide(from_left[1]) + wide(from_right[1])
    crossing.wait_recv()
    dn = dn + wide(across_in[...])
    hidden = wide(tokens_ref[...])
    scale = lax.rsqrt(jnp.mean(hidden * hidden, axis=1, keepdims=True) + EPSILON)
    unit = hidden * scale
    scaled = dn * gain_ref[0:1, :]
    input_grad_ref[...] += scale * (
        scaled - unit * jnp.mean(scaled * unit, axis=1, keepdims=True)
    )
    out_swapped.wait_recv()
    out_grad_ref[lines((1 - c) * 96, 96), :] = wide(out_swap_in[...])
    arrived(gain_shared)
    total = gain_out[...]
    for k in range(7):
        total = total + gain_in[k]
    gains_ref[...] = total
    for copy in copies:
        copy.wait_send()


SLOTS = 64


def finished_back(*arguments):
    def shape(dims, kind=jnp.float32):
        return jax.ShapeDtypeStruct(dims, kind)

    def room(*dims):
        return pltpu.VMEM(dims, jnp.bfloat16)

    return pl.pallas_call(
        back_kernel,
        out_shape=(
            shape((192, 1536)),
            shape((96, 512)),
            shape((192, 96)),
            shape((3, 96, 512)),
            shape((96, 128)),
        ),
        in_specs=[IN_VMEM] * 16 + [ANY] * 3,
        out_specs=(IN_VMEM,) * 5,
        scratch_shapes=[
            room(8, 192, 192),
            room(8, 192, 192),
            pltpu.VMEM((1536, 128), jnp.float32),
            pltpu.VMEM((1536, 128), jnp.float32),
            room(192, 1536),
            room(1536, 512),
            room(1536, 1536),
            room(576, 1024),
            room(576, 1024),
            room(576, 1024),
            room(288, 1024),
            room(288, 1024),
            room(576, 1024),
            room(576, 1024),
            room(576, 512),
            room(576, 512),
            room(3, 96, 512),
            room(3, 96, 512),
            room(8, 192, 1536),
            room(8, 96, 1536),
            room(4, 96, 384),
            room(4, 96, 384),
            room(8, 96, 384),
            room(8, 96, 384),
            room(8, 96, 384),
            room(7, 96, 384),
            room(96, 192),
            room(96, 192),
            room(96, 96),
            room(96, 96),
            room(8, 2, 96, 512),
            room(8, 96, 512),
            room(96, 512),
            room(96, 512),
            room(2, 96, 512),
            room(2, 96, 512),
            room(96, 512),
            room(96, 512),
            room(2, 192, 1536),
            room(2, 2, 192, 1536),
            room(2, 96, 1536),
            room(2, 96, 1536),
            room(2, 192, 1536),
            room(2, 192, 1536),
            room(192, 1536),
            room(192, 1536),
            pltpu.VMEM((96, 128), jnp.float32),
            pltpu.VMEM((7, 96, 128), jnp.float32),
            room(2, 96, 512),
            pltpu.SemaphoreType.DMA((SLOTS,)),
            pltpu.SemaphoreType.DMA((SLOTS,)),
            pltpu.SemaphoreType.DMA((5,)),
        ],
        compiler_params=pltpu.CompilerParams(
            collective_id=2, has_side_effects=True, vmem_limit_bytes=63 * 2**20
        ),
        name="back",
    )(*arguments)


def picked(value, index, dim):
    return lax.dynamic_index_in_dim(value, index, dim, keepdims=False)


def added(one, two):
    return (one.astype(jnp.float32) + two.astype(jnp.float32)).astype(jnp.bfloat16)


def summed_over_cores(grad):
    core = lax.axis_index("c")
    count, _, columns = grad.shape
    parts = grad.reshape(count, 4, 2, 2, 96, columns)

    def chosen(which):
        part = picked(parts, which, 3).reshape(count, 4, 192, columns)
        return jnp.transpose(part, (1, 0, 2, 3))

    arrived = to_other_core(chosen(1 - core))
    return added(chosen(core), arrived).reshape(4, -1, columns)


def per_device(
    tokens,
    seq_lens,
    query_key_value_weight,
    out_weight,
    gate_up_weight,
    down_weight,
    norm_gains,
    cotangent,
):
    shard_rows = tokens.shape[0]
    group_rows = shard_rows * 8

    normed = (normalize(tokens.astype(jnp.float32))[0] * norm_gains[0]).astype(jnp.bfloat16)
    first, positions = layout(seq_lens[0], group_rows)
    cos_part, sin_part = angles(positions)
    gap = jnp.zeros((group_rows, 16), jnp.float32)
    cos_part = jnp.concatenate([cos_part, gap, cos_part, gap], axis=1)
    sin_part = jnp.concatenate([-sin_part, gap, sin_part, gap], axis=1)
    first = jnp.tile(first.reshape(8, 1, shard_rows), (1, 1, 2))
    weight_wide = spread_columns(query_key_value_weight)
    (
        normed_all,
        out_all,
        gate_up_other,
        down_other,
        upstream_near,
        attended_here,
        queries,
        keys_all,
        values_all,
        heads,
        log_sums,
    ) = attended(
        normed,
        weight_wide,
        cos_part,
        sin_part,
        first,
        out_weight,
        gate_up_weight,
        down_weight,
        cotangent,
    )
    normed_all = normed_all.reshape(group_rows, -1)

    middle, normed_two = branched(tokens, attended_here, out_all, norm_gains[1:2])
    normed_two_all = gathered(normed_two, False, 3, "gather_normed_two")
    upstream_all = gathered(cotangent, False, 4, "gather_upstream")
    gate_up_all = jnp.concatenate([gate_up_weight, gate_up_other], axis=2)
    down_all = jnp.concatenate([down_weight, down_other], axis=0)
    gate_up = jnp.einsum(
        "td,cdf->ctf", normed_two_all, gate_up_all, preferred_element_type=jnp.float32
    )
    sigmoid_gate = jax.nn.sigmoid(gate_up[0])
    silu_gate = gate_up[0] * sigmoid_gate
    activated = (silu_gate * gate_up[1]).astype(jnp.bfloat16)
    grad_act = times_transposed(upstream_all, down_all)
    grad_gate = grad_act * gate_up[1] * sigmoid_gate * (1.0 + gate_up[0] * (1.0 - sigmoid_gate))
    grad_upper = grad_act * silu_gate
    grad_gate_up = jnp.stack([grad_gate, grad_upper]).astype(jnp.bfloat16)
    normed_two_part = jnp.einsum(
        "ctf,cdf->td", grad_gate_up, gate_up_all, preferred_element_type=jnp.float32
    ).astype(jnp.bfloat16)
    grad_normed_two = lax.psum_scatter(normed_two_part, "z", scatter_dimension=0, tiled=True)
    activated, normed_two_all, upstream_all, normed_two_part = lax.optimization_barrier(
        (activated, normed_two_all, upstream_all, normed_two_part)
    )
    ffn_out = lax.psum_scatter(
        jnp.dot(activated, down_all, preferred_element_type=jnp.float32).astype(jnp.bfloat16),
        "z",
        scatter_dimension=0,
        tiled=True,
    ).astype(jnp.float32)
    mixed = (middle + ffn_out).astype(jnp.bfloat16)
    down_grad = transposed_times(upstream_all, activated).astype(jnp.bfloat16)
    gate_up_grad = jnp.einsum(
        "td,ctf->cdf", normed_two_all, grad_gate_up, preferred_element_type=jnp.float32
    ).astype(jnp.bfloat16)
    ffn_grad = jnp.concatenate([gate_up_grad, down_grad[None]], axis=0)

    input_grad, qkv_grad, out_grad, ffn_grad, gains_grad = finished_back(
        grad_normed_two,
        middle,
        tokens,
        norm_gains,
        cotangent,
        out_all,
        attended_here,
        queries,
        keys_all,
        values_all,
        heads,
        log_sums,
        first,
        cos_part,
        sin_part,
        weight_wide,
        normed_all,
        summed_over_cores(ffn_grad),
        gate_up_weight,
    )
    first_gain = ((lax.axis_index("x") * 2 + lax.axis_index("yl")) * 2 + lax.axis_index("c")) * 96
    gain_rows = lax.dynamic_slice_in_dim(norm_gains, first_gain, 96, 1)
    return (
        mixed,
        input_grad,
        packed_columns(qkv_grad),
        out_grad,
        ffn_grad[0:2],
        ffn_grad[2].T,
        gains_grad[:, 0:2].T / gain_rows,
    )


def solution(mesh):
    split = Mesh(mesh.devices.reshape(4, 2, 2, 2, 4), ALL)
    placed = (
        P(ALL, None),
        P(DP, None),
        P(None, TENSOR),
        P(TENSOR, None),
        P(None, None, TENSOR),
        P(TENSOR, None),
        P(),
        P(ALL, None),
    )
    return jax.shard_map(
        per_device,
        mesh=split,
        in_specs=placed,
        out_specs=(
            P(ALL, None),
            P(ALL, None),
            P(DP, TENSOR),
            P(TENSOR, DP),
            P(None, DP, TENSOR),
            P(TENSOR, DP),
            P(None, DP),
        ),
        check_vma=False,
    )
```

```python
import functools

import jax
import jax.numpy as jnp
import numpy as np
from jax import lax
from jax.experimental import pallas as pl
from jax.experimental.pallas import tpu as pltpu
from jax.sharding import Mesh
from jax.sharding import PartitionSpec as P

HEAD_SIZE = 96
BLOCK = 128
DP = ("x", "yl", "c")
TENSOR = ("yh", "z")
ALL = DP + TENSOR
MESH = pl.DeviceIdType.MESH

EPSILON = 1e-05
THETA = 100000.0
masked_score = -1e30


def packed_columns(grad):
    return grad.reshape(grad.shape[0], -1, 64)[:, :, :48].reshape(grad.shape[0], -1)


def times_transposed(left, right):
    return lax.dot_general(
        left, right, (((1,), (1,)), ((), ())), preferred_element_type=jnp.float32
    )


def transposed_times(left, right):
    return lax.dot_general(
        left, right, (((0,), (0,)), ((), ())), preferred_element_type=jnp.float32
    )


def barrier_with(partners):
    barrier = pltpu.get_barrier_semaphore()
    for partner in partners:
        pl.semaphore_signal(barrier, inc=1, device_id=partner, device_id_type=MESH)
    pl.semaphore_wait(barrier, len(partners))


def kernel_copies(send_sem, recv_sem):
    def sent(slot, source, goal, device):
        copy = pltpu.make_async_remote_copy(
            src_ref=source,
            dst_ref=goal,
            send_sem=send_sem.at[slot],
            recv_sem=recv_sem.at[slot],
            device_id=device,
            device_id_type=MESH,
        )
        copy.start()
        return copy

    return sent


def tensor_partner(step):
    goal = lax.rem(lax.axis_index("yh") * 4 + lax.axis_index("z") + step, 8)
    return {"yh": lax.div(goal, 4), "z": lax.rem(goal, 4)}


def spread(values):
    gap = jnp.zeros((values.shape[0], 16), values.dtype)
    return jnp.concatenate([values[:, :48], gap, values[:, 48:], gap], axis=1)


def packed(values):
    return jnp.concatenate([values[:, :48], values[:, 64:112]], axis=1)


KEYS = 256


ANY = pl.BlockSpec(memory_space=pl.ANY)
IN_VMEM = pl.BlockSpec(memory_space=pltpu.VMEM)


def static_score(key_block, query_block, first_row, key_start, queries, query_start):
    scores = times_transposed(key_block, query_block) * (HEAD_SIZE ** (-0.5))
    keys = key_start + lax.broadcasted_iota(jnp.int32, scores.shape, 0)
    allowed = keys >= first_row
    if key_start + scores.shape[0] > query_start:
        allowed = allowed & (keys <= queries)
    return scores, allowed


def block_queries(block, starts, ends):
    queries = lax.broadcasted_iota(jnp.int32, (1, 384), 1)
    queries = block * 192 + jnp.where(queries >= 192, queries - 192, queries)
    first_row = queries
    for slot in range(4):
        within = (starts[slot] <= queries) & (queries < ends[slot])
        first_row = jnp.where(within, starts[slot], first_row)
    return queries, first_row


def sequences(lens_ref):
    starts, ends = [], []
    start = jnp.int32(0)
    for slot in range(4):
        length = lens_ref[0, slot]
        starts.append(start)
        ends.append(start + length)
        start = start + lax.div(length + (BLOCK - 1), BLOCK) * BLOCK
    return starts, ends


def columns(start, size):
    return pl.ds(pl.multiple_of(start, 128), size)


def lines(start, size):
    return pl.ds(pl.multiple_of(start, 16), size)


def wide(value):
    return value.astype(jnp.float32)


def low(value):
    return value.astype(jnp.bfloat16)


def front_kernel(
    tokens_ref,
    lens_ref,
    gain_ref,
    qkv_ref,
    out_weight_ref,
    gate_up_ref,
    down_ref,
    cotangent_ref,
    cos_table_ref,
    sin_table_ref,
    normed_ref,
    weight_out_ref,
    out_out_ref,
    gate_up_out_ref,
    down_out_ref,
    upstream_ref,
    normed_two_ref,
    act_ref,
    dgu_ref,
    middle_ref,
    here_ref,
    q_ref,
    k_ref,
    v_ref,
    o_ref,
    lse_ref,
    cos_ref,
    sin_ref,
    landed,
    raw,
    weight,
    tables,
    out_all,
    gate_up,
    down,
    upstream,
    normed_two,
    act,
    dgu,
    dact,
    scores,
    outgoing,
    send_sem,
    recv_sem,
    local_sem,
):
    x, yl, c = lax.axis_index("x"), lax.axis_index("yl"), lax.axis_index("c")
    yh, z = lax.axis_index("yh"), lax.axis_index("z")
    me = yh * 4 + z
    after, before, opposite = lax.rem(z + 1, 4), lax.rem(z + 3, 4), lax.rem(z + 2, 4)
    other = 1 - yh
    right, left, across = {"z": after}, {"z": before}, {"yh": other}
    x_after, x_before, x_far = lax.rem(x + 1, 4), lax.rem(x + 3, 4), lax.rem(x + 2, 4)
    x_right, x_left, core = {"x": x_after}, {"x": x_before}, {"c": 1 - c}

    def crossed(step):
        place = tensor_partner(step)
        return {**place, "yl": lax.rem(yl + yh + place["yh"], 2)}

    tensor_partners = [tensor_partner(step) for step in range(1, 8)]
    cross_partners = [{"yl": 1 - yl, "yh": other, "z": lax.rem(z + k, 4)} for k in range(4)]
    partners = tensor_partners + cross_partners + [x_right, x_left, core]
    barrier = pltpu.get_barrier_semaphore()
    for partner in partners:
        pl.semaphore_signal(barrier, inc=1, device_id=partner, device_id_type=MESH)

    stores = []
    local_slots = iter(range(FRONT_LOCALS))

    def moved(source, goal):
        copy = pltpu.make_async_copy(source, goal, local_sem.at[next(local_slots)])
        copy.start()
        return copy

    def stored(source, goal):
        stores.append(moved(source, goal))

    qkv_load = moved(qkv_ref, raw)
    cos_load = moved(cos_table_ref, tables.at[0])
    sin_load = moved(sin_table_ref, tables.at[1])
    hidden = wide(tokens_ref[...])
    scale = lax.rsqrt(jnp.mean(hidden * hidden, axis=1, keepdims=True) + EPSILON)
    landed[yh, z] = low(hidden * scale * gain_ref[0:1, :])
    pl.semaphore_wait(barrier, len(partners))

    raw_sent = kernel_copies(send_sem, recv_sem)
    copies = []
    slots = iter(range(FRONT_SLOTS))

    def sent(source, goal, device):
        copy = raw_sent(next(slots), source, goal, device)
        copies.append(copy)
        return copy

    lower, upper, whole = pl.ds(0, 96), pl.ds(96, 96), pl.ds(0, 192)

    def shard(block_yh, block_z, rows, device):
        spot = landed.at[block_yh, block_z, rows]
        return sent(spot, spot, device)

    def gate_up_part(quarter, half, part=pl.ds(0, 2)):
        rows = lines(quarter * 384, 384)
        return gate_up.at[1, part, rows, columns(half * 256, 256)]

    def down_part(quarter, half, part=pl.ds(0, 128)):
        rows = lines(quarter * 128 + part.start, part.size)
        return down.at[1, rows, columns(half * 768, 768)]

    def out_part(quarter, half, part=pl.ds(1, 7)):
        return out_all.at[part, lines(quarter * 48, 48), columns(half * 768, 768)]

    to_right = shard(yh, z, whole, right)
    to_left = shard(yh, z, whole, left)
    to_across = shard(yh, z, whole, across)
    out_cross = []
    piece = out_weight_ref.at[lines(x * 48, 48), columns(c * 768, 768)]
    for step in range(1, 8):
        goal = out_all.at[8 - step, lines(x * 48, 48), columns(c * 768, 768)]
        out_cross.append(sent(piece, goal, crossed(step)))
    gate_up_cross = sent(
        gate_up_ref.at[:, lines(x * 384, 384), columns(c * 256, 256)],
        gate_up_part(x, c),
        crossed(4),
    )
    down_cross = sent(
        down_ref.at[lines(x * 128, 128), columns(c * 768, 768)], down_part(x, c), crossed(4)
    )
    upstream_load = moved(cotangent_ref, upstream.at[z])
    out_load = moved(out_weight_ref, out_all.at[0])
    gate_up_load = moved(gate_up_ref, gate_up.at[0])
    down_load = moved(down_ref, down.at[0])

    starts, ends = sequences(lens_ref)
    cos_load.wait()
    sin_load.wait()
    for block in range(12):
        begin, end = jnp.int32(0), jnp.int32(0)
        for slot in range(4):
            within = (starts[slot] <= block * BLOCK) & (block * BLOCK < ends[slot])
            begin = jnp.where(within, starts[slot], begin)
            end = jnp.where(within, ends[slot], end)
        used = block - lax.div(begin, BLOCK)
        rows = pl.ds(block * BLOCK, BLOCK)
        token = block * BLOCK + lax.broadcasted_iota(jnp.int32, (BLOCK, 128), 0)
        cos_ref[rows, :] = jnp.where(token < end, tables[0, used], tables[0, block])
        sin_ref[rows, :] = jnp.where(token < end, tables[1, used], tables[1, block])
    qkv_load.wait()
    for head in range(4):
        weight[:, head * 128 : head * 128 + 128] = spread(raw[:, head * 96 : head * 96 + 96])
    stored(weight, weight_out_ref)

    def project(block_yh, block_z):
        block = block_yh * 4 + block_z
        projected = jnp.dot(
            landed[block_yh, block_z], weight[...], preferred_element_type=jnp.float32
        )
        rows = lines(block * 192, 192)
        cos_part, sin_part = cos_ref[rows, :], sin_ref[rows, :]

        def turned(values):
            return low(values * cos_part + pltpu.roll(values, 64, 1) * sin_part)

        q_ref[block, 0:192, :] = turned(projected[:, 0:128])
        q_ref[block, 192:384, :] = turned(projected[:, 128:256])
        k_ref[rows, :] = turned(projected[:, 256:384])
        v_ref[rows, :] = low(projected[:, 384:512])

    project(yh, z)
    to_right.wait_recv()
    last_right = shard(yh, before, lower, right)
    to_left.wait_recv()
    last_left = shard(yh, after, upper, left)
    project(yh, before)
    project(yh, after)
    to_across.wait_recv()
    far_right = shard(other, z, whole, right)
    far_left = shard(other, z, whole, left)
    project(other, z)

    def spread_out(part, halves, awaited):
        goal = part(x, c)
        awaited.append(sent(goal, goal, core))
        return [sent(goal, goal, x_right), sent(goal, goal, x_left)]

    def pass_on(part, halves, awaited, arriving):
        arriving[0].wait_recv()
        first, second = part(x_before, c), part(x_before, c, halves[0])
        far = [sent(second, second, x_right)]
        awaited.append(sent(first, first, core))
        arriving[1].wait_recv()
        first, second = part(x_after, c), part(x_after, c, halves[1])
        far.append(sent(second, second, x_left))
        awaited.append(sent(first, first, core))
        return far

    def finish(part, halves, awaited, far):
        for k in range(2):
            far[k].wait_recv()
            goal = part(x_far, c, halves[k])
            awaited.append(sent(goal, goal, core))
        for copy in awaited:
            copy.wait_recv()

    gate_up_plan = (gate_up_part, (pl.ds(0, 1), pl.ds(1, 1)), [])
    down_plan = (down_part, (pl.ds(0, 64), pl.ds(64, 64)), [])
    out_plan = (out_part, (pl.ds(1, 4), pl.ds(5, 3)), [])

    for copy in out_cross:
        copy.wait_recv()
    out_moves = spread_out(*out_plan)
    last_right.wait_recv()
    last_left.wait_recv()
    project(yh, opposite)
    gate_up_cross.wait_recv()
    gate_up_moves = spread_out(*gate_up_plan)
    down_cross.wait_recv()
    down_moves = spread_out(*down_plan)
    far_right.wait_recv()
    far_last_right = shard(other, before, lower, right)
    far_left.wait_recv()
    far_last_left = shard(other, after, upper, left)
    upstream_load.wait()
    upstream_right = sent(upstream.at[z], upstream.at[z], right)
    upstream_left = sent(upstream.at[z], upstream.at[z], left)
    project(other, before)
    project(other, after)
    far_last_right.wait_recv()
    far_last_left.wait_recv()
    project(other, opposite)
    stored(landed, normed_ref)

    def outgoing_copy(block, step):
        return pltpu.make_async_remote_copy(
            src_ref=outgoing.at[block],
            dst_ref=here_ref.at[8 - step],
            send_sem=send_sem.at[FRONT_SLOTS + step],
            recv_sem=recv_sem.at[FRONT_SLOTS + step],
            device_id={"yh": lax.div(block, 4), "z": lax.rem(block, 4)},
            device_id_type=MESH,
        )

    here_sem = local_sem.at[FRONT_LOCALS]

    def attend(block):
        query_block = q_ref[block]
        queries, first_row = block_queries(block, starts, ends)
        count = (192 * (block + 1) + KEYS - 1) // KEYS
        peak = jnp.full((8, 384), masked_score, jnp.float32)
        for j in range(count):
            rows = pl.ds(j * KEYS, KEYS)
            part, allowed = static_score(
                k_ref[rows, :], query_block, first_row, j * KEYS, queries, block * 192
            )
            part = jnp.where(allowed, part, masked_score)
            scores[rows, :] = part
            peak = jnp.maximum(peak, jnp.max(part.reshape(KEYS // 8, 8, 384), axis=0))
        peak = jnp.max(peak, axis=0, keepdims=True)
        total = jnp.zeros((8, 384), jnp.float32)
        out = jnp.zeros((384, 128), jnp.float32)
        for j in range(count):
            rows = pl.ds(j * KEYS, KEYS)
            weights = jnp.exp(scores[rows, :] - peak)
            total = total + jnp.sum(weights.reshape(KEYS // 8, 8, 384), axis=0)
            out = out + transposed_times(low(weights), v_ref[rows, :])
        total = jnp.sum(total, axis=0, keepdims=True)
        lse_ref[block] = peak + jnp.log(total)
        out = out * jnp.transpose(jnp.broadcast_to(1.0 / total, (128, 384)))
        o_ref[block] = low(out)
        outgoing[block] = low(
            jnp.concatenate([packed(out[0:192]), packed(out[192:384])], axis=1)
        )
        step = lax.rem(block - me + 8, 8)

        @pl.when(step != 0)
        def _():
            outgoing_copy(block, step).start()

        @pl.when(step == 0)
        def _():
            pltpu.make_async_copy(outgoing.at[block], here_ref.at[0], here_sem).start()

    for block in range(4):
        attend(block)
    out_far = pass_on(*out_plan, out_moves)
    for block in range(4, 7):
        attend(block)
    gate_up_far = pass_on(*gate_up_plan, gate_up_moves)
    down_far = pass_on(*down_plan, down_moves)
    attend(7)
    upstream_right.wait_recv()
    upstream_last = [sent(upstream.at[before, lower], upstream.at[before, lower], right)]
    upstream_left.wait_recv()
    upstream_last.append(sent(upstream.at[after, upper], upstream.at[after, upper], left))
    finish(*out_plan, out_far)
    out_load.wait()

    pltpu.make_async_copy(outgoing.at[me], here_ref.at[0], here_sem).wait()
    middle = wide(tokens_ref[...]) + jnp.dot(
        here_ref[0], out_all[0], preferred_element_type=jnp.float32
    )
    for step in range(7, 0, -1):
        outgoing_copy(lax.rem(me + step, 8), step).wait_recv()
        middle += jnp.dot(here_ref[8 - step], out_all[8 - step], preferred_element_type=jnp.float32)
    middle_ref[...] = middle
    scale = lax.rsqrt(jnp.mean(middle * middle, axis=1, keepdims=True) + EPSILON)
    normed_two[z] = low(middle * scale * gain_ref[1:2, :])
    two_right = sent(normed_two.at[z], normed_two.at[z], right)
    two_left = sent(normed_two.at[z], normed_two.at[z], left)
    stored(out_all, out_out_ref)
    finish(*down_plan, down_far)
    finish(*gate_up_plan, gate_up_far)
    stored(gate_up.at[1], gate_up_out_ref)
    stored(down.at[1], down_out_ref)
    gate_up_load.wait()
    down_load.wait()

    def act_back(block):
        for side in range(2):
            dact[block, side] = times_transposed(upstream[block], down[side])

    def feed(block):
        for side in range(2):
            cols = pl.ds(side * 512, 512)
            gate = jnp.dot(
                normed_two[block], gate_up[side, 0], preferred_element_type=jnp.float32
            )
            up = jnp.dot(normed_two[block], gate_up[side, 1], preferred_element_type=jnp.float32)
            sigmoid = 1.0 / (1.0 + jnp.exp(-gate))
            silu = gate * sigmoid
            act[block, :, cols] = low(silu * up)
            grad = dact[block, side]
            dgu[0, block, :, cols] = low(grad * up * sigmoid * (1.0 + gate * (1.0 - sigmoid)))
            dgu[1, block, :, cols] = low(grad * silu)

    act_back(z)
    feed(z)
    act_back(before)
    act_back(after)
    two_right.wait_recv()
    two_last = [sent(normed_two.at[before, lower], normed_two.at[before, lower], right)]
    two_left.wait_recv()
    two_last.append(sent(normed_two.at[after, upper], normed_two.at[after, upper], left))
    feed(before)
    feed(after)
    for copy in upstream_last:
        copy.wait_recv()
    stored(upstream, upstream_ref)
    act_back(opposite)
    for copy in two_last:
        copy.wait_recv()
    feed(opposite)
    stored(normed_two, normed_two_ref)
    stored(act, act_ref)
    stored(dgu, dgu_ref)
    for copy in copies:
        copy.wait_send()
    for step in range(1, 8):
        outgoing_copy(lax.rem(me + step, 8), step).wait_send()
    for copy in stores:
        copy.wait()


FRONT_SLOTS = 53
FRONT_LOCALS = 16


def rotation_tables():
    inverse = np.float32(THETA) ** (-np.arange(0, HEAD_SIZE, 2, dtype=np.float32) / HEAD_SIZE)
    phases = np.arange(1536, dtype=np.float32)[:, None] * inverse.astype(np.float32)[None, :]
    cosine, sine = np.zeros((1536, 128), np.float32), np.zeros((1536, 128), np.float32)
    cosine[:, 0:48] = cosine[:, 64:112] = np.cos(phases)
    sine[:, 64:112] = np.sin(phases)
    sine[:, 0:48] = -sine[:, 64:112]
    return cosine.reshape(12, BLOCK, 128), sine.reshape(12, BLOCK, 128)


def fronted(tokens, lens, gains, qkv, out_weight, gate_up, down, cotangent):
    def shape(dims, kind=jnp.bfloat16):
        return jax.ShapeDtypeStruct(dims, kind)

    def room(*dims):
        return pltpu.VMEM(dims, jnp.bfloat16)

    cosine, sine = rotation_tables()
    return pl.pallas_call(
        front_kernel,
        out_shape=(
            shape((2, 4, 192, 1536)),
            shape((1536, 512)),
            shape((8, 192, 1536)),
            shape((2, 1536, 512)),
            shape((512, 1536)),
            shape((4, 192, 1536)),
            shape((4, 192, 1536)),
            shape((4, 192, 1024)),
            shape((2, 4, 192, 1024)),
            shape((192, 1536), jnp.float32),
            shape((8, 192, 192)),
            shape((8, 384, 128)),
            shape((1536, 128)),
            shape((1536, 128)),
            shape((8, 384, 128)),
            shape((8, 1, 384), jnp.float32),
            shape((1536, 128), jnp.float32),
            shape((1536, 128), jnp.float32),
        ),
        in_specs=[IN_VMEM, pl.BlockSpec(memory_space=pltpu.SMEM), IN_VMEM] + [ANY] * 7,
        out_specs=(ANY,) * 9 + (IN_VMEM,) * 9,
        scratch_shapes=[
            room(2, 4, 192, 1536),
            room(1536, 384),
            room(1536, 512),
            pltpu.VMEM((2, 12, BLOCK, 128), jnp.float32),
            room(8, 192, 1536),
            room(2, 2, 1536, 512),
            room(2, 512, 1536),
            room(4, 192, 1536),
            room(4, 192, 1536),
            room(4, 192, 1024),
            room(2, 4, 192, 1024),
            pltpu.VMEM((4, 2, 192, 512), jnp.float32),
            pltpu.VMEM((1536, 384), jnp.float32),
            room(8, 192, 192),
            pltpu.SemaphoreType.DMA((FRONT_SLOTS + 8,)),
            pltpu.SemaphoreType.DMA((FRONT_SLOTS + 8,)),
            pltpu.SemaphoreType.DMA((FRONT_LOCALS + 1,)),
        ],
        compiler_params=pltpu.CompilerParams(
            collective_id=1, has_side_effects=True, vmem_limit_bytes=62 * 2**20
        ),
        name="front",
    )(
        tokens,
        lens,
        gains,
        qkv,
        out_weight,
        gate_up,
        down,
        cotangent,
        jnp.asarray(cosine),
        jnp.asarray(sine),
    )


def mid_kernel(
    dgu_ref,
    act_ref,
    normed_ref,
    upstream_ref,
    gate_up_ref,
    gate_up_other_ref,
    down_ref,
    down_other_ref,
    dn_ref,
    ffn_right_ref,
    ffn_left_ref,
    ffn_own_ref,
    feed_right_ref,
    feed_left_ref,
    feed_own_ref,
    dgu,
    act,
    normed,
    upstream,
    gate_up,
    down,
    turned,
    grads,
    grads_core,
    grads_a,
    grads_b,
    far_out,
    near_out,
    far_a,
    far_b,
    from_left,
    from_right,
    feeds,
    feed_a,
    feed_b,
    send_sem,
    recv_sem,
    local_sem,
):
    x, c = lax.axis_index("x"), lax.axis_index("c")
    z = lax.axis_index("z")
    after, before, opposite = lax.rem(z + 1, 4), lax.rem(z + 3, 4), lax.rem(z + 2, 4)
    x_after, x_before, x_far = lax.rem(x + 1, 4), lax.rem(x + 3, 4), lax.rem(x + 2, 4)
    right, left = {"z": after}, {"z": before}
    x_right, x_left, core = {"x": x_after}, {"x": x_before}, {"c": 1 - c}
    partners = [right, left, x_right, x_left, core]
    barrier = pltpu.get_barrier_semaphore()
    for partner in partners:
        pl.semaphore_signal(barrier, inc=1, device_id=partner, device_id_type=MESH)
    local_slots, slots = iter(range(MID_LOCALS)), iter(range(MID_SLOTS))
    stores, copies = [], []
    raw_sent = kernel_copies(send_sem, recv_sem)

    def moved(source, goal):
        copy = pltpu.make_async_copy(source, goal, local_sem.at[next(local_slots)])
        copy.start()
        return copy

    def stored(source, goal):
        stores.append(moved(source, goal))

    def sent(source, goal, device):
        copy = raw_sent(next(slots), source, goal, device)
        copies.append(copy)
        return copy

    def arrived(pair):
        for copy in pair:
            copy.wait_recv()

    first_loads = [
        moved(dgu_ref, dgu),
        moved(gate_up_ref, gate_up.at[0]),
        moved(gate_up_other_ref, gate_up.at[1]),
    ]
    normed_load = moved(normed_ref, normed)
    upstream_load = moved(upstream_ref, upstream)
    act_load = moved(act_ref, act)
    down_loads = [moved(down_ref, down.at[0]), moved(down_other_ref, down.at[1])]
    pl.semaphore_wait(barrier, len(partners))
    for load in first_loads:
        load.wait()

    def partial(block):
        total = jnp.zeros((192, 1536), jnp.float32)
        for kind in range(2):
            for side in range(2):
                total = total + times_transposed(
                    dgu[kind, block, :, pl.ds(side * 512, 512)], gate_up[side, kind]
                )
        return total

    far_out[...] = low(partial(opposite))
    far = [
        sent(far_out.at[pl.ds(0, 96)], far_a, right),
        sent(far_out.at[pl.ds(96, 96)], far_b, left),
    ]
    to_right, to_left = partial(after), partial(before)
    arrived(far)
    near_out[0, 0:96] = low(to_right[0:96] + wide(far_a[...]))
    near_out[0, 96:192] = low(to_right[96:192])
    near_out[1, 0:96] = low(to_left[0:96])
    near_out[1, 96:192] = low(to_left[96:192] + wide(far_b[...]))
    near = [
        sent(near_out.at[0], from_left, right),
        sent(near_out.at[1], from_right, left),
    ]
    dn_ref[...] = partial(z)

    def add_core(kind):
        cored[kind].wait_recv()
        for k in range(8):
            grads[kind, k, c] = low(wide(grads[kind, k, c]) + wide(grads_core[kind, k]))
        spot = grads.at[kind, pl.ds(x_far * 2, 2), c]
        return [
            sent(spot.at[:, :, pl.ds(0, 512)], grads_a.at[kind], x_right),
            sent(spot.at[:, :, pl.ds(512, 512)], grads_b.at[kind], x_left),
        ]

    def grad(kind, right_side):
        for side in range(2):
            cols = pl.ds(side * 512, 512)
            value = jnp.dot(turned[...], right_side(cols), preferred_element_type=jnp.float32)
            grads[kind, :, :, :, cols] = low(value).reshape(8, 2, 96, 512)
        cored.append(sent(grads.at[kind, :, 1 - c], grads_core.at[kind], core))

    cored = []
    normed_load.wait()
    turned[...] = jnp.transpose(normed[...].reshape(768, 1536))
    grad(0, lambda cols: dgu[0, :, :, cols].reshape(768, 512))
    grad(1, lambda cols: dgu[1, :, :, cols].reshape(768, 512))
    round_x = [add_core(0)]
    upstream_load.wait()
    act_load.wait()
    turned[...] = jnp.transpose(upstream[...].reshape(768, 1536))
    grad(2, lambda cols: act[:, :, cols].reshape(768, 512))
    round_x.append(add_core(1))

    for load in down_loads:
        load.wait()

    def feed(block):
        return jnp.dot(
            act[block, :, 0:512], down[0], preferred_element_type=jnp.float32
        ) + jnp.dot(act[block, :, 512:1024], down[1], preferred_element_type=jnp.float32)

    feeds[3] = low(feed(opposite))
    feed_far = [
        sent(feeds.at[3, pl.ds(0, 96)], feed_a, right),
        sent(feeds.at[3, pl.ds(96, 96)], feed_b, left),
    ]
    round_x.append(add_core(2))
    feeds[0], feeds[1], feeds[2] = low(feed(after)), low(feed(before)), low(feed(z))
    stored(feeds.at[2], feed_own_ref)
    stored(grads.at[:, pl.ds(x * 2, 2), c], ffn_own_ref)
    arrived(near)
    dn_ref[...] += wide(from_left[...]) + wide(from_right[...])
    for kind in range(3):
        arrived(round_x[kind])
        for k in range(2):
            spot = grads[kind, x_after * 2 + k, c, :, 0:512]
            grads[kind, x_after * 2 + k, c, :, 0:512] = low(wide(spot) + wide(grads_a[kind, k]))
            spot = grads[kind, x_before * 2 + k, c, :, 512:1024]
            grads[kind, x_before * 2 + k, c, :, 512:1024] = low(
                wide(spot) + wide(grads_b[kind, k])
            )
    stored(grads.at[:, pl.ds(x_after * 2, 2), c], ffn_right_ref)
    stored(grads.at[:, pl.ds(x_before * 2, 2), c], ffn_left_ref)
    arrived(feed_far)
    feeds[0, 0:96] = low(wide(feeds[0, 0:96]) + wide(feed_a[...]))
    feeds[1, 96:192] = low(wide(feeds[1, 96:192]) + wide(feed_b[...]))
    stored(feeds.at[0], feed_right_ref)
    stored(feeds.at[1], feed_left_ref)
    for copy in copies:
        copy.wait_send()
    for copy in stores:
        copy.wait()


MID_SLOTS = 15
MID_LOCALS = 14


def middled(*arguments):
    def shape(dims, kind=jnp.bfloat16):
        return jax.ShapeDtypeStruct(dims, kind)

    def room(*dims):
        return pltpu.VMEM(dims, jnp.bfloat16)

    return pl.pallas_call(
        mid_kernel,
        out_shape=(
            shape((192, 1536), jnp.float32),
            shape((3, 2, 96, 1024)),
            shape((3, 2, 96, 1024)),
            shape((3, 2, 96, 1024)),
            shape((192, 1536)),
            shape((192, 1536)),
            shape((192, 1536)),
        ),
        in_specs=[ANY] * 8,
        out_specs=(IN_VMEM,) + (ANY,) * 6,
        scratch_shapes=[
            room(2, 4, 192, 1024),
            room(4, 192, 1024),
            room(4, 192, 1536),
            room(4, 192, 1536),
            room(2, 2, 1536, 512),
            room(2, 512, 1536),
            room(1536, 768),
            room(3, 8, 2, 96, 1024),
            room(3, 8, 96, 1024),
            room(3, 2, 96, 512),
            room(3, 2, 96, 512),
            room(192, 1536),
            room(2, 192, 1536),
            room(96, 1536),
            room(96, 1536),
            room(192, 1536),
            room(192, 1536),
            room(4, 192, 1536),
            room(96, 1536),
            room(96, 1536),
            pltpu.SemaphoreType.DMA((MID_SLOTS,)),
            pltpu.SemaphoreType.DMA((MID_SLOTS,)),
            pltpu.SemaphoreType.DMA((MID_LOCALS,)),
        ],
        compiler_params=pltpu.CompilerParams(
            collective_id=3, has_side_effects=True, vmem_limit_bytes=62 * 2**20
        ),
        name="mid",
    )(*arguments)


def back_kernel(
    dn_ref,
    middle_ref,
    tokens_ref,
    gain_ref,
    cotangent_ref,
    out_ref,
    here_ref,
    q_ref,
    k_ref,
    v_ref,
    o_ref,
    lse_ref,
    lens_ref,
    cos_ref,
    sin_ref,
    weight_ref,
    normed_ref,
    ffn_right_ref,
    ffn_left_ref,
    ffn_own_ref,
    feed_right_ref,
    feed_left_ref,
    feed_own_ref,
    gate_up_ref,
    mixed_ref,
    input_grad_ref,
    qkv_grad_ref,
    out_grad_ref,
    ffn_grad_ref,
    gains_ref,
    outgoing,
    landed,
    dk_sum,
    dv_sum,
    dhb,
    dp,
    normed,
    ffn_own,
    feed_own,
    feed_from_left,
    feed_from_right,
    ffn_from_left,
    ffn_from_right,
    ffn_cross,
    ffn_crossed,
    ffn_yl,
    ffn_yl_in,
    out_part,
    out_core,
    out_far_a,
    out_far_b,
    out_from_left,
    out_from_right,
    out_sum,
    out_shards,
    out_yl,
    out_yl_in,
    out_swap,
    out_swap_in,
    qkv_part,
    qkv_core,
    qkv_far_a,
    qkv_far_b,
    qkv_from_left,
    qkv_from_right,
    qkv_yl,
    qkv_yl_in,
    far_out,
    near_out,
    far_a,
    far_b,
    from_left,
    from_right,
    across_out,
    across_in,
    gain_out,
    gain_in,
    gate_up_rows,
    send_sem,
    recv_sem,
    local_sem,
):
    x, yl, c = lax.axis_index("x"), lax.axis_index("yl"), lax.axis_index("c")
    yh, z = lax.axis_index("yh"), lax.axis_index("z")
    me = yh * 4 + z
    place = (x * 2 + yl) * 2 + c
    after, before, opposite = lax.rem(z + 1, 4), lax.rem(z + 3, 4), lax.rem(z + 2, 4)
    x_after, x_before, x_far = lax.rem(x + 1, 4), lax.rem(x + 3, 4), lax.rem(x + 2, 4)
    right, left, across = {"z": after}, {"z": before}, {"yh": 1 - yh}
    x_right, x_left = {"x": x_after}, {"x": x_before}
    core, other_yl, cross = {"c": 1 - c}, {"yl": 1 - yl}, {"yl": 1 - yl, "yh": 1 - yh}
    barrier_with(
        [tensor_partner(step) for step in range(1, 8)] + [x_right, x_left, core, other_yl, cross]
    )
    raw_sent = kernel_copies(send_sem, recv_sem)
    copies = []
    slots = iter(range(SLOTS))

    def sent(source, goal, device):
        copy = raw_sent(next(slots), source, goal, device)
        copies.append(copy)
        return copy

    def arrived(pair):
        for copy in pair:
            copy.wait_recv()

    def fetched(slot, source, goal):
        copy = pltpu.make_async_copy(source, goal, local_sem.at[slot])
        copy.start()
        return copy

    ffn_second = [
        sent(ffn_right_ref, ffn_from_left, x_right),
        sent(ffn_left_ref, ffn_from_right, x_left),
    ]
    ffn_load = fetched(0, ffn_own_ref, ffn_own)
    feed_load = fetched(1, feed_own_ref, feed_own)
    normed_load = fetched(3, normed_ref, normed)
    rows_load = fetched(4, gate_up_ref.at[:, lines(place * 96, 96), :], gate_up_rows)

    middle = middle_ref[...]
    scale = lax.rsqrt(jnp.mean(middle * middle, axis=1, keepdims=True) + EPSILON)
    unit = middle * scale
    scaled = wide(dn_ref[...]) * gain_ref[1:2, :]
    dh = wide(cotangent_ref[...]) + scale * (
        scaled - unit * jnp.mean(scaled * unit, axis=1, keepdims=True)
    )
    input_grad_ref[...] = dh
    dhb[...] = low(dh)
    slot_base = [next(slots) for _ in range(8)][0]
    for step in range(1, 8):
        outgoing[step] = low(times_transposed(dhb[...], out_ref[step]))
        copies.append(
            raw_sent(
                slot_base + step, outgoing.at[step], landed.at[8 - step], tensor_partner(step)
            )
        )
    landed[0] = low(times_transposed(dhb[...], out_ref[0]))
    feed_second = [
        sent(feed_right_ref, feed_from_left, right),
        sent(feed_left_ref, feed_from_right, left),
    ]
    for k in range(8):
        out_part[k] = low(transposed_times(here_ref[k], dhb[...]))
    out_cored = sent(out_part.at[:, lines((1 - c) * 96, 96), :], out_core, core)
    starts, ends = sequences(lens_ref)
    dk_sum[...] = jnp.zeros_like(dk_sum)
    dv_sum[...] = jnp.zeros_like(dv_sum)

    def unturned(values, rows):
        return values * cos_ref[rows, :] - pltpu.roll(values, 64, 1) * sin_ref[rows, :]

    def await_block(step):
        pltpu.make_async_remote_copy(
            src_ref=outgoing.at[step],
            dst_ref=landed.at[step],
            send_sem=send_sem.at[slot_base + step],
            recv_sem=recv_sem.at[slot_base + 8 - step],
            device_id=tensor_partner(1),
            device_id_type=MESH,
        ).wait_recv()

    def back(block):
        step = lax.rem(block - me + 8, 8)

        @pl.when(step != 0)
        def _():
            await_block(step)

        grads = landed[step]
        grad_block = jnp.concatenate([spread(grads[:, 0:96]), spread(grads[:, 96:192])], axis=0)
        query_block = q_ref[block]
        queries, first_row = block_queries(block, starts, ends)
        lse = lse_ref[block]
        centered = wide(grad_block) * wide(o_ref[block])
        centered = jnp.sum(jnp.transpose(centered), axis=0, keepdims=True)
        dq = jnp.zeros((384, 128), jnp.float32)
        for j in range((192 * (block + 1) + KEYS - 1) // KEYS):
            rows = pl.ds(j * KEYS, KEYS)
            key_block, value_block = k_ref[rows, :], v_ref[rows, :]
            scores, allowed = static_score(
                key_block, query_block, first_row, j * KEYS, queries, block * 192
            )
            weights = jnp.where(allowed, jnp.exp(scores - lse), 0.0)
            grad_weights = times_transposed(value_block, grad_block)
            grad_scores = low(weights * (grad_weights - centered))
            dv_sum[rows, :] += jnp.dot(
                low(weights), grad_block, preferred_element_type=jnp.float32
            )
            dk_sum[rows, :] += jnp.dot(
                grad_scores, query_block, preferred_element_type=jnp.float32
            )
            dq = dq + transposed_times(grad_scores, key_block)
        dq = dq * (HEAD_SIZE ** (-0.5))
        rows = pl.ds(block * 192, 192)
        dp[rows, 0:128] = low(unturned(dq[0:192], rows))
        dp[rows, 128:256] = low(unturned(dq[192:384], rows))

    for block in range(4):
        back(block)
    out_cored.wait_recv()
    half = lines(c * 96, 96)
    for k in range(8):
        out_part[k, half, :] = low(wide(out_part[k, half, :]) + wide(out_core[k]))
    out_first = [
        sent(out_part.at[pl.ds(0, 4), half, columns(x_far * 384, 384)], out_far_a, x_right),
        sent(out_part.at[pl.ds(4, 4), half, columns(x_far * 384, 384)], out_far_b, x_left),
    ]
    for block in range(4, 7):
        back(block)
    back(7)
    for block in range(8):
        rows = pl.ds(block * 192, 192)
        dp[rows, 256:384] = low(unturned(dk_sum[rows, :] * (HEAD_SIZE ** (-0.5)), rows))
        dp[rows, 384:512] = low(dv_sum[rows, :])

    def partial(block_yh, block_z):
        rows = lines((block_yh * 4 + block_z) * 192, 192)
        return times_transposed(dp[rows, :], weight_ref[...])

    sides = (1 - yh, yh)
    far = []
    for k in range(2):
        far_out[k] = low(partial(sides[k], opposite))
        far.append(
            [
                sent(far_out.at[k, pl.ds(0, 96)], far_a.at[k], right),
                sent(far_out.at[k, pl.ds(96, 96)], far_b.at[k], left),
            ]
        )
    out_cols = [columns(place_x * 384, 384) for place_x in (x_after, x_before)]
    near = []
    for k in range(2):
        to_right, to_left = partial(sides[k], after), partial(sides[k], before)
        arrived(far[k])
        near_out[k, 0, 0:96] = low(to_right[0:96] + wide(far_a[k]))
        near_out[k, 0, 96:192] = low(to_right[96:192])
        near_out[k, 1, 0:96] = low(to_left[0:96])
        near_out[k, 1, 96:192] = low(to_left[96:192] + wide(far_b[k]))
        near.append(
            [
                sent(near_out.at[k, 0], from_left.at[k], right),
                sent(near_out.at[k, 1], from_right.at[k], left),
            ]
        )
    normed_load.wait()
    for part in range(4):
        features = pl.ds(part * 384, 384)
        grad = transposed_times(normed[:, features], dp[...])
        qkv_part[part * 2 : part * 2 + 2] = low(grad).reshape(2, 2, 96, 512)
    qkv_cored = sent(qkv_part.at[:, 1 - c], qkv_core, core)
    arrived(out_first)
    for k in range(4):
        out_part[k, half, out_cols[0]] = low(
            wide(out_part[k, half, out_cols[0]]) + wide(out_far_a[k])
        )
        out_part[4 + k, half, out_cols[1]] = low(
            wide(out_part[4 + k, half, out_cols[1]]) + wide(out_far_b[k])
        )
    out_second = [
        sent(out_part.at[:, half, out_cols[0]], out_from_left, x_right),
        sent(out_part.at[:, half, out_cols[1]], out_from_right, x_left),
    ]
    own = [partial(sides[k], z) for k in range(2)]
    qkv_cored.wait_recv()
    for k in range(8):
        qkv_part[k, c] = low(wide(qkv_part[k, c]) + wide(qkv_core[k]))
    qkv_first = [
        sent(qkv_part.at[x_far * 2, c], qkv_far_a, x_right),
        sent(qkv_part.at[x_far * 2 + 1, c], qkv_far_b, x_left),
    ]
    arrived(near[0])
    across_out[...] = low(own[0] + wide(from_left[0]) + wide(from_right[0]))
    crossing = sent(across_out, across_in, across)
    arrived(ffn_second)
    ffn_load.wait()
    ffn_sum = wide(ffn_own[...]) + wide(ffn_from_left[...]) + wide(ffn_from_right[...])
    ffn_cross[...] = low(ffn_sum[..., 512:1024])
    ffn_own[:, :, :, 0:512] = low(ffn_sum[..., 0:512])
    ffn_crossing = sent(ffn_cross, ffn_crossed, cross)
    arrived(qkv_first)
    qkv_part[x_after * 2, c] = low(wide(qkv_part[x_after * 2, c]) + wide(qkv_far_a[...]))
    qkv_part[x_before * 2 + 1, c] = low(
        wide(qkv_part[x_before * 2 + 1, c]) + wide(qkv_far_b[...])
    )
    qkv_second = [
        sent(qkv_part.at[pl.ds(x_after * 2, 2), c], qkv_from_left, x_right),
        sent(qkv_part.at[pl.ds(x_before * 2, 2), c], qkv_from_right, x_left),
    ]
    arrived(out_second)
    own_cols = columns(x * 384, 384)
    for k in range(8):
        out_sum[k] = low(
            wide(out_part[k, half, own_cols]) + wide(out_from_left[k]) + wide(out_from_right[k])
        )
    out_shared = [
        sent(out_sum.at[step], out_shards.at[step - 1], tensor_partner(step))
        for step in range(1, 8)
    ]
    ffn_crossing.wait_recv()
    ffn_sum = wide(ffn_own[:, :, :, 0:512]) + wide(ffn_crossed[...])
    keep_yl = jnp.where(yl == 0, ffn_sum[:, 0], ffn_sum[:, 1])
    ffn_yl[...] = low(jnp.where(yl == 0, ffn_sum[:, 1], ffn_sum[:, 0]))
    ffn_ending = sent(ffn_yl, ffn_yl_in, other_yl)
    ffn_grad_ref[...] = keep_yl
    arrived(qkv_second)
    qkv_sum = (
        wide(qkv_part[pl.ds(x * 2, 2), c]) + wide(qkv_from_left[...]) + wide(qkv_from_right[...])
    )
    qkv_grad_ref[...] = jnp.where(yl == 0, qkv_sum[0], qkv_sum[1])
    qkv_yl[...] = low(jnp.where(yl == 0, qkv_sum[1], qkv_sum[0]))
    qkv_ending = sent(qkv_yl, qkv_yl_in, other_yl)
    arrived(out_shared)
    total = wide(out_sum[0])
    for k in range(7):
        total = total + wide(out_shards[k])
    keep_out = jnp.where(yl == 0, total[:, 0:192], total[:, 192:384])
    out_yl[...] = low(jnp.where(yl == 0, total[:, 192:384], total[:, 0:192]))
    out_ending = sent(out_yl, out_yl_in, other_yl)
    ffn_ending.wait_recv()
    ffn_final = ffn_grad_ref[...] + wide(ffn_yl_in[...])
    ffn_grad_ref[...] = ffn_final
    qkv_ending.wait_recv()
    qkv_final = qkv_grad_ref[...] + wide(qkv_yl_in[...])
    qkv_grad_ref[...] = qkv_final
    rows_load.wait()
    gain_one = jnp.sum(
        qkv_final * wide(weight_ref[lines(place * 96, 96), :]), axis=1, keepdims=True
    )
    gain_two = jnp.sum(
        ffn_final[0] * wide(gate_up_rows[0]) + ffn_final[1] * wide(gate_up_rows[1]),
        axis=1,
        keepdims=True,
    )
    lanes = lax.broadcasted_iota(jnp.int32, (96, 128), 1)
    gain_out[...] = jnp.where(lanes == 0, gain_one, jnp.where(lanes == 1, gain_two, 0.0))
    gain_shared = [
        sent(gain_out, gain_in.at[step - 1], tensor_partner(step)) for step in range(1, 8)
    ]
    out_ending.wait_recv()
    out_final = keep_out + wide(out_yl_in[...])
    out_swap[...] = low(jnp.where(c == 0, out_final[:, 96:192], out_final[:, 0:96]))
    out_swapped = sent(out_swap, out_swap_in, core)
    out_mine = jnp.where(c == 0, out_final[:, 0:96], out_final[:, 96:192])
    out_grad_ref[half, :] = out_mine
    arrived(near[1])
    dn = own[1] + wide(from_left[1]) + wide(from_right[1])
    crossing.wait_recv()
    dn = dn + wide(across_in[...])
    hidden = wide(tokens_ref[...])
    scale = lax.rsqrt(jnp.mean(hidden * hidden, axis=1, keepdims=True) + EPSILON)
    unit = hidden * scale
    scaled = dn * gain_ref[0:1, :]
    input_grad_ref[...] += scale * (
        scaled - unit * jnp.mean(scaled * unit, axis=1, keepdims=True)
    )
    arrived(feed_second)
    feed_load.wait()
    mixed_ref[...] = low(
        middle_ref[...] + wide(feed_own[...]) + wide(feed_from_left[...]) + wide(feed_from_right[...])
    )
    out_swapped.wait_recv()
    out_grad_ref[lines((1 - c) * 96, 96), :] = wide(out_swap_in[...])
    arrived(gain_shared)
    total = gain_out[...]
    for k in range(7):
        total = total + gain_in[k]
    gains_ref[...] = total
    for copy in copies:
        copy.wait_send()


SLOTS = 64


def finished_back(*arguments):
    def shape(dims, kind=jnp.float32):
        return jax.ShapeDtypeStruct(dims, kind)

    def room(*dims):
        return pltpu.VMEM(dims, jnp.bfloat16)

    return pl.pallas_call(
        back_kernel,
        out_shape=(
            shape((192, 1536), jnp.bfloat16),
            shape((192, 1536)),
            shape((96, 512)),
            shape((192, 96)),
            shape((3, 96, 512)),
            shape((96, 128)),
        ),
        in_specs=[IN_VMEM] * 12
        + [pl.BlockSpec(memory_space=pltpu.SMEM)]
        + [IN_VMEM] * 3
        + [ANY] * 8,
        out_specs=(IN_VMEM,) * 6,
        scratch_shapes=[
            room(8, 192, 192),
            room(8, 192, 192),
            pltpu.VMEM((1536, 128), jnp.float32),
            pltpu.VMEM((1536, 128), jnp.float32),
            room(192, 1536),
            room(1536, 512),
            room(1536, 1536),
            room(3, 2, 96, 1024),
            room(192, 1536),
            room(192, 1536),
            room(192, 1536),
            room(3, 2, 96, 1024),
            room(3, 2, 96, 1024),
            room(3, 2, 96, 512),
            room(3, 2, 96, 512),
            room(3, 96, 512),
            room(3, 96, 512),
            room(8, 192, 1536),
            room(8, 96, 1536),
            room(4, 96, 384),
            room(4, 96, 384),
            room(8, 96, 384),
            room(8, 96, 384),
            room(8, 96, 384),
            room(7, 96, 384),
            room(96, 192),
            room(96, 192),
            room(96, 96),
            room(96, 96),
            room(8, 2, 96, 512),
            room(8, 96, 512),
            room(96, 512),
            room(96, 512),
            room(2, 96, 512),
            room(2, 96, 512),
            room(96, 512),
            room(96, 512),
            room(2, 192, 1536),
            room(2, 2, 192, 1536),
            room(2, 96, 1536),
            room(2, 96, 1536),
            room(2, 192, 1536),
            room(2, 192, 1536),
            room(192, 1536),
            room(192, 1536),
            pltpu.VMEM((96, 128), jnp.float32),
            pltpu.VMEM((7, 96, 128), jnp.float32),
            room(2, 96, 512),
            pltpu.SemaphoreType.DMA((SLOTS,)),
            pltpu.SemaphoreType.DMA((SLOTS,)),
            pltpu.SemaphoreType.DMA((5,)),
        ],
        compiler_params=pltpu.CompilerParams(
            collective_id=2, has_side_effects=True, vmem_limit_bytes=63 * 2**20
        ),
        name="back",
    )(*arguments)


def per_device(
    tokens,
    seq_lens,
    query_key_value_weight,
    out_weight,
    gate_up_weight,
    down_weight,
    norm_gains,
    cotangent,
):
    (
        normed_all,
        weight_wide,
        out_all,
        gate_up_other,
        down_other,
        upstream_all,
        normed_two_all,
        activated,
        grad_gate_up,
        middle,
        attended_here,
        queries,
        keys_all,
        values_all,
        heads,
        log_sums,
        cos_part,
        sin_part,
    ) = fronted(
        tokens,
        seq_lens,
        norm_gains,
        query_key_value_weight,
        out_weight,
        gate_up_weight,
        down_weight,
        cotangent,
    )
    dn, ffn_right, ffn_left, ffn_own, feed_right, feed_left, feed_own = middled(
        grad_gate_up,
        activated,
        normed_two_all,
        upstream_all,
        gate_up_weight,
        gate_up_other,
        down_weight,
        down_other,
    )
    mixed, input_grad, qkv_grad, out_grad, ffn_grad, gains_grad = finished_back(
        dn,
        middle,
        tokens,
        norm_gains,
        cotangent,
        out_all,
        attended_here,
        queries,
        keys_all,
        values_all,
        heads,
        log_sums,
        seq_lens,
        cos_part,
        sin_part,
        weight_wide,
        normed_all.reshape(1536, 1536),
        ffn_right,
        ffn_left,
        ffn_own,
        feed_right,
        feed_left,
        feed_own,
        gate_up_weight,
    )
    first_gain = ((lax.axis_index("x") * 2 + lax.axis_index("yl")) * 2 + lax.axis_index("c")) * 96
    gain_rows = lax.dynamic_slice_in_dim(norm_gains, first_gain, 96, 1)
    return (
        mixed,
        input_grad,
        packed_columns(qkv_grad),
        out_grad,
        ffn_grad[0:2],
        ffn_grad[2].T,
        gains_grad[:, 0:2].T / gain_rows,
    )


def solution(mesh):
    split = Mesh(mesh.devices.reshape(4, 2, 2, 2, 4), ALL)
    placed = (
        P(ALL, None),
        P(DP, None),
        P(None, TENSOR),
        P(TENSOR, None),
        P(None, None, TENSOR),
        P(TENSOR, None),
        P(),
        P(ALL, None),
    )
    return jax.shard_map(
        per_device,
        mesh=split,
        in_specs=placed,
        out_specs=(
            P(ALL, None),
            P(ALL, None),
            P(DP, TENSOR),
            P(TENSOR, DP),
            P(None, DP, TENSOR),
            P(TENSOR, DP),
            P(None, DP),
        ),
        check_vma=False,
    )
```

```python
import functools

import jax
import jax.numpy as jnp
import numpy as np
from jax import lax
from jax.experimental import pallas as pl
from jax.experimental.pallas import tpu as pltpu
from jax.sharding import Mesh
from jax.sharding import PartitionSpec as P

HEAD_SIZE = 96
BLOCK = 128
DP = ("x", "yl", "c")
TENSOR = ("yh", "z")
ALL = DP + TENSOR
MESH = pl.DeviceIdType.MESH

EPSILON = 1e-05
THETA = 100000.0
masked_score = -1e30


def times_transposed(left, right):
    return lax.dot_general(
        left, right, (((1,), (1,)), ((), ())), preferred_element_type=jnp.float32
    )


def transposed_times(left, right):
    return lax.dot_general(
        left, right, (((0,), (0,)), ((), ())), preferred_element_type=jnp.float32
    )


def barrier_with(partners):
    barrier = pltpu.get_barrier_semaphore()
    for partner in partners:
        pl.semaphore_signal(barrier, inc=1, device_id=partner, device_id_type=MESH)
    pl.semaphore_wait(barrier, len(partners))


def kernel_copies(send_sem, recv_sem):
    def sent(slot, source, goal, device):
        copy = pltpu.make_async_remote_copy(
            src_ref=source,
            dst_ref=goal,
            send_sem=send_sem.at[slot],
            recv_sem=recv_sem.at[slot],
            device_id=device,
            device_id_type=MESH,
        )
        copy.start()
        return copy

    return sent


def tensor_partner(step):
    goal = lax.rem(lax.axis_index("yh") * 4 + lax.axis_index("z") + step, 8)
    return {"yh": lax.div(goal, 4), "z": lax.rem(goal, 4)}


def spread(values):
    gap = jnp.zeros((values.shape[0], 16), values.dtype)
    return jnp.concatenate([values[:, :48], gap, values[:, 48:], gap], axis=1)


def packed(values):
    return jnp.concatenate([values[:, :48], values[:, 64:112]], axis=1)


KEYS = 256


ANY = pl.BlockSpec(memory_space=pl.ANY)
IN_VMEM = pl.BlockSpec(memory_space=pltpu.VMEM)


def static_score(key_block, query_block, first_row, key_start, queries, query_start):
    scores = times_transposed(key_block, query_block) * (HEAD_SIZE ** (-0.5))
    keys = key_start + lax.broadcasted_iota(jnp.int32, scores.shape, 0)
    allowed = keys >= first_row
    if key_start + scores.shape[0] > query_start:
        allowed = allowed & (keys <= queries)
    return scores, allowed


def block_queries(block, starts, ends):
    queries = lax.broadcasted_iota(jnp.int32, (1, 384), 1)
    queries = block * 192 + jnp.where(queries >= 192, queries - 192, queries)
    first_row = queries
    for slot in range(4):
        within = (starts[slot] <= queries) & (queries < ends[slot])
        first_row = jnp.where(within, starts[slot], first_row)
    return queries, first_row


def sequences(lens_ref):
    starts, ends = [], []
    start = jnp.int32(0)
    for slot in range(4):
        length = lens_ref[0, slot]
        starts.append(start)
        ends.append(start + length)
        start = start + lax.div(length + (BLOCK - 1), BLOCK) * BLOCK
    return starts, ends


def columns(start, size):
    return pl.ds(pl.multiple_of(start, 128), size)


def lines(start, size):
    return pl.ds(pl.multiple_of(start, 16), size)


def wide(value):
    return value.astype(jnp.float32)


def low(value):
    return value.astype(jnp.bfloat16)


def front_kernel(
    tokens_ref,
    lens_ref,
    gain_ref,
    qkv_ref,
    out_weight_ref,
    gate_up_ref,
    down_ref,
    cotangent_ref,
    cos_table_ref,
    sin_table_ref,
    normed_ref,
    normed_other_ref,
    weight_out_ref,
    weight_other_out_ref,
    out_out_ref,
    gate_up_out_ref,
    down_out_ref,
    upstream_ref,
    normed_two_ref,
    act_ref,
    dgu_ref,
    middle_out_ref,
    here_out_ref,
    q_out_ref,
    k_out_ref,
    v_out_ref,
    o_out_ref,
    cos_out_ref,
    sin_out_ref,
    dn_out_ref,
    lse_ref,
    landed,
    raw,
    raw_other,
    weight,
    weight_other,
    projected_out,
    projected_in,
    tables,
    out_all,
    gate_up,
    down,
    upstream,
    normed_two,
    act,
    dgu,
    dact,
    scores,
    outgoing,
    middle_ref,
    here_ref,
    q_ref,
    k_ref,
    v_ref,
    o_ref,
    cos_ref,
    sin_ref,
    dn_parts,
    send_sem,
    recv_sem,
    local_sem,
):
    x, yl, c = lax.axis_index("x"), lax.axis_index("yl"), lax.axis_index("c")
    yh, z = lax.axis_index("yh"), lax.axis_index("z")
    me = yh * 4 + z
    after, before, opposite = lax.rem(z + 1, 4), lax.rem(z + 3, 4), lax.rem(z + 2, 4)
    other = 1 - yh
    right, left, across = {"z": after}, {"z": before}, {"yh": other}
    x_after, x_before, x_far = lax.rem(x + 1, 4), lax.rem(x + 3, 4), lax.rem(x + 2, 4)
    x_right, x_left, core = {"x": x_after}, {"x": x_before}, {"c": 1 - c}

    def crossed(step):
        place = tensor_partner(step)
        return {**place, "yl": lax.rem(yl + yh + place["yh"], 2)}

    tensor_partners = [tensor_partner(step) for step in range(1, 8)]
    cross_partners = [{"yl": 1 - yl, "yh": other, "z": lax.rem(z + k, 4)} for k in range(4)]
    partners = tensor_partners + cross_partners + [x_right, x_left, core]
    barrier = pltpu.get_barrier_semaphore()
    for partner in partners:
        pl.semaphore_signal(barrier, inc=1, device_id=partner, device_id_type=MESH)

    stores = []
    local_slots = iter(range(FRONT_LOCALS))

    def moved(source, goal):
        copy = pltpu.make_async_copy(source, goal, local_sem.at[next(local_slots)])
        copy.start()
        return copy

    def stored(source, goal):
        stores.append(moved(source, goal))

    qkv_load = moved(qkv_ref, raw)
    cos_load = moved(cos_table_ref, tables.at[0])
    sin_load = moved(sin_table_ref, tables.at[1])
    hidden = wide(tokens_ref[...])
    scale = lax.rsqrt(jnp.mean(hidden * hidden, axis=1, keepdims=True) + EPSILON)
    landed[z] = low(hidden * scale * gain_ref[0:1, :])
    pl.semaphore_wait(barrier, len(partners))

    raw_sent = kernel_copies(send_sem, recv_sem)
    copies = []
    slots = iter(range(FRONT_SLOTS))

    def sent(source, goal, device):
        copy = raw_sent(next(slots), source, goal, device)
        copies.append(copy)
        return copy

    lower, upper, whole = pl.ds(0, 96), pl.ds(96, 96), pl.ds(0, 192)

    def shard(block_z, rows, device):
        spot = landed.at[block_z, rows]
        return sent(spot, spot, device)

    def qkv_part(quarter, half, part=pl.ds(0, 192)):
        return raw_other.at[lines(quarter * 384 + half * 192 + part.start, part.size), :]

    def gate_up_part(quarter, half, part=pl.ds(0, 2)):
        rows = lines(quarter * 384, 384)
        return gate_up.at[1, part, rows, columns(half * 256, 256)]

    def down_part(quarter, half, part=pl.ds(0, 128)):
        rows = lines(quarter * 128 + part.start, part.size)
        return down.at[1, rows, columns(half * 768, 768)]

    def out_part(quarter, half, part=pl.ds(1, 7)):
        return out_all.at[part, lines(quarter * 48, 48), columns(half * 768, 768)]

    to_right = shard(z, whole, right)
    to_left = shard(z, whole, left)
    qkv_cross = sent(
        qkv_ref.at[lines(x * 384 + c * 192, 192), :], qkv_part(x, c), crossed(4)
    )
    out_cross = []
    piece = out_weight_ref.at[lines(x * 48, 48), columns(c * 768, 768)]
    for step in range(1, 8):
        goal = out_all.at[8 - step, lines(x * 48, 48), columns(c * 768, 768)]
        out_cross.append(sent(piece, goal, crossed(step)))
    gate_up_cross = sent(
        gate_up_ref.at[:, lines(x * 384, 384), columns(c * 256, 256)],
        gate_up_part(x, c),
        crossed(4),
    )
    down_cross = sent(
        down_ref.at[lines(x * 128, 128), columns(c * 768, 768)], down_part(x, c), crossed(4)
    )
    upstream_load = moved(cotangent_ref, upstream.at[z])
    out_load = moved(out_weight_ref, out_all.at[0])
    gate_up_load = moved(gate_up_ref, gate_up.at[0])
    down_load = moved(down_ref, down.at[0])

    starts, ends = sequences(lens_ref)
    cos_load.wait()
    sin_load.wait()
    for block in range(12):
        begin, end = jnp.int32(0), jnp.int32(0)
        for slot in range(4):
            within = (starts[slot] <= block * BLOCK) & (block * BLOCK < ends[slot])
            begin = jnp.where(within, starts[slot], begin)
            end = jnp.where(within, ends[slot], end)
        used = block - lax.div(begin, BLOCK)
        rows = pl.ds(block * BLOCK, BLOCK)
        token = block * BLOCK + lax.broadcasted_iota(jnp.int32, (BLOCK, 128), 0)
        cos_ref[rows, :] = jnp.where(token < end, tables[0, used], tables[0, block])
        sin_ref[rows, :] = jnp.where(token < end, tables[1, used], tables[1, block])
    qkv_load.wait()
    for head in range(4):
        weight[:, head * 128 : head * 128 + 128] = spread(raw[:, head * 96 : head * 96 + 96])
    stored(weight, weight_out_ref)
    stored(cos_ref, cos_out_ref)
    stored(sin_ref, sin_out_ref)

    def projected(block_z, weights):
        values = jnp.dot(landed[block_z], weights[...], preferred_element_type=jnp.float32)
        rows = lines((yh * 4 + block_z) * 192, 192)
        cos_part, sin_part = cos_ref[rows, :], sin_ref[rows, :]
        heads = [values[:, head * 128 : head * 128 + 128] for head in range(4)]
        for head in range(3):
            heads[head] = heads[head] * cos_part + pltpu.roll(heads[head], 64, 1) * sin_part
        return heads

    def kept(block, heads):
        rows = lines(block * 192, 192)
        q_ref[block, 0:192, :] = heads[0]
        q_ref[block, 192:384, :] = heads[1]
        k_ref[rows, :] = heads[2]
        v_ref[rows, :] = heads[3]

    def project_own(block_z):
        kept(yh * 4 + block_z, [low(head) for head in projected(block_z, weight)])

    exchanged = []

    def project_other(k, block_z):
        heads = [packed(head) for head in projected(block_z, weight_other)]
        projected_out[k] = low(jnp.concatenate(heads, axis=1))
        exchanged.append(sent(projected_out.at[k], projected_in.at[block_z], across))

    def spread_out(part, halves, awaited):
        goal = part(x, c)
        awaited.append(sent(goal, goal, core))
        return [sent(goal, goal, x_right), sent(goal, goal, x_left)]

    def pass_on(part, halves, awaited, arriving):
        arriving[0].wait_recv()
        first, second = part(x_before, c), part(x_before, c, halves[0])
        far = [sent(second, second, x_right)]
        awaited.append(sent(first, first, core))
        arriving[1].wait_recv()
        first, second = part(x_after, c), part(x_after, c, halves[1])
        far.append(sent(second, second, x_left))
        awaited.append(sent(first, first, core))
        return far

    def finish(part, halves, awaited, far):
        for k in range(2):
            far[k].wait_recv()
            goal = part(x_far, c, halves[k])
            awaited.append(sent(goal, goal, core))
        for copy in awaited:
            copy.wait_recv()

    gate_up_plan = (gate_up_part, (pl.ds(0, 1), pl.ds(1, 1)), [])
    down_plan = (down_part, (pl.ds(0, 64), pl.ds(64, 64)), [])
    out_plan = (out_part, (pl.ds(1, 4), pl.ds(5, 3)), [])
    qkv_plan = (qkv_part, (pl.ds(0, 96), pl.ds(96, 96)), [])

    project_own(z)
    qkv_cross.wait_recv()
    qkv_moves = spread_out(*qkv_plan)
    qkv_far = pass_on(*qkv_plan, qkv_moves)
    finish(*qkv_plan, qkv_far)
    for head in range(4):
        weight_other[:, head * 128 : head * 128 + 128] = spread(
            raw_other[:, head * 96 : head * 96 + 96]
        )
    stored(raw_other, weight_other_out_ref)
    to_right.wait_recv()
    last_right = shard(before, lower, right)
    to_left.wait_recv()
    last_left = shard(after, upper, left)
    project_other(0, z)
    project_other(1, before)
    project_other(2, after)
    project_own(before)
    project_own(after)
    for copy in out_cross:
        copy.wait_recv()
    out_moves = spread_out(*out_plan)
    last_right.wait_recv()
    last_left.wait_recv()
    project_other(3, opposite)
    project_own(opposite)
    upstream_load.wait()
    upstream_right = sent(upstream.at[z], upstream.at[z], right)
    upstream_left = sent(upstream.at[z], upstream.at[z], left)
    stored(landed, normed_ref)
    for copy in exchanged:
        copy.wait_recv()
    for block_z in range(4):
        arrived = projected_in[block_z]
        kept(
            other * 4 + block_z,
            [spread(arrived[:, head * 96 : head * 96 + 96]) for head in range(4)],
        )
    out_far = pass_on(*out_plan, out_moves)
    stored(q_ref, q_out_ref)
    stored(k_ref, k_out_ref)
    stored(v_ref, v_out_ref)

    def outgoing_copy(block, step):
        return pltpu.make_async_remote_copy(
            src_ref=outgoing.at[block],
            dst_ref=here_ref.at[8 - step],
            send_sem=send_sem.at[FRONT_SLOTS + step],
            recv_sem=recv_sem.at[FRONT_SLOTS + step],
            device_id={"yh": lax.div(block, 4), "z": lax.rem(block, 4)},
            device_id_type=MESH,
        )

    here_sem = local_sem.at[FRONT_LOCALS]

    def attend(block):
        query_block = q_ref[block]
        queries, first_row = block_queries(block, starts, ends)
        count = (192 * (block + 1) + KEYS - 1) // KEYS
        peak = jnp.full((8, 384), masked_score, jnp.float32)
        for j in range(count):
            rows = pl.ds(j * KEYS, KEYS)
            part, allowed = static_score(
                k_ref[rows, :], query_block, first_row, j * KEYS, queries, block * 192
            )
            part = jnp.where(allowed, part, masked_score)
            scores[rows, :] = part
            peak = jnp.maximum(peak, jnp.max(part.reshape(KEYS // 8, 8, 384), axis=0))
        peak = jnp.max(peak, axis=0, keepdims=True)
        total = jnp.zeros((8, 384), jnp.float32)
        out = jnp.zeros((384, 128), jnp.float32)
        for j in range(count):
            rows = pl.ds(j * KEYS, KEYS)
            weights = jnp.exp(scores[rows, :] - peak)
            total = total + jnp.sum(weights.reshape(KEYS // 8, 8, 384), axis=0)
            out = out + transposed_times(low(weights), v_ref[rows, :])
        total = jnp.sum(total, axis=0, keepdims=True)
        lse_ref[block] = peak + jnp.log(total)
        out = out * jnp.transpose(jnp.broadcast_to(1.0 / total, (128, 384)))
        o_ref[block] = low(out)
        outgoing[block] = low(
            jnp.concatenate([packed(out[0:192]), packed(out[192:384])], axis=1)
        )
        step = lax.rem(block - me + 8, 8)

        @pl.when(step != 0)
        def _():
            outgoing_copy(block, step).start()

        @pl.when(step == 0)
        def _():
            pltpu.make_async_copy(outgoing.at[block], here_ref.at[0], here_sem).start()

    for block in range(8):
        attend(block)
    gate_up_cross.wait_recv()
    gate_up_moves = spread_out(*gate_up_plan)
    down_cross.wait_recv()
    down_moves = spread_out(*down_plan)
    finish(*out_plan, out_far)
    out_load.wait()

    pltpu.make_async_copy(outgoing.at[me], here_ref.at[0], here_sem).wait()
    middle = wide(tokens_ref[...]) + jnp.dot(
        here_ref[0], out_all[0], preferred_element_type=jnp.float32
    )
    for step in range(7, 0, -1):
        outgoing_copy(lax.rem(me + step, 8), step).wait_recv()
        middle += jnp.dot(here_ref[8 - step], out_all[8 - step], preferred_element_type=jnp.float32)
    middle_ref[...] = middle
    stored(middle_ref, middle_out_ref)
    stored(here_ref, here_out_ref)
    stored(o_ref, o_out_ref)
    scale = lax.rsqrt(jnp.mean(middle * middle, axis=1, keepdims=True) + EPSILON)
    normed_two[z] = low(middle * scale * gain_ref[1:2, :])
    two_right = sent(normed_two.at[z], normed_two.at[z], right)
    two_left = sent(normed_two.at[z], normed_two.at[z], left)
    upstream_right.wait_recv()
    upstream_last = [sent(upstream.at[before, lower], upstream.at[before, lower], right)]
    upstream_left.wait_recv()
    upstream_last.append(sent(upstream.at[after, upper], upstream.at[after, upper], left))
    normed_across = [sent(landed.at[k], normed_other_ref.at[k], across) for k in range(2)]
    stored(out_all, out_out_ref)
    gate_up_load.wait()
    down_load.wait()

    def act_back(block, side):
        dact[block, side] = times_transposed(upstream[block], down[side])

    def feed(block, side):
        cols = pl.ds(side * 512, 512)
        gate = jnp.dot(normed_two[block], gate_up[side, 0], preferred_element_type=jnp.float32)
        up = jnp.dot(normed_two[block], gate_up[side, 1], preferred_element_type=jnp.float32)
        sigmoid = 1.0 / (1.0 + jnp.exp(-gate))
        silu = gate * sigmoid
        act[block, :, cols] = low(silu * up)
        grad = dact[block, side]
        dgu[0, block, :, cols] = low(grad * up * sigmoid * (1.0 + gate * (1.0 - sigmoid)))
        dgu[1, block, :, cols] = low(grad * silu)

    def partial(goal, block):
        total = jnp.zeros((192, 1536), jnp.float32)
        for kind in range(2):
            for side in range(2):
                total = total + times_transposed(
                    dgu[kind, block, :, pl.ds(side * 512, 512)], gate_up[side, kind]
                )
        dn_parts[goal] = low(total)

    act_back(z, 0)
    feed(z, 0)
    act_back(before, 0)
    act_back(after, 0)
    gate_up_far = pass_on(*gate_up_plan, gate_up_moves)
    down_far = pass_on(*down_plan, down_moves)
    two_right.wait_recv()
    two_last = [sent(normed_two.at[before, lower], normed_two.at[before, lower], right)]
    two_left.wait_recv()
    two_last.append(sent(normed_two.at[after, upper], normed_two.at[after, upper], left))
    feed(before, 0)
    feed(after, 0)
    for copy in upstream_last:
        copy.wait_recv()
    stored(upstream, upstream_ref)
    act_back(opposite, 0)
    finish(*down_plan, down_far)
    stored(down.at[1], down_out_ref)
    act_back(z, 1)
    act_back(before, 1)
    act_back(after, 1)
    finish(*gate_up_plan, gate_up_far)
    stored(gate_up.at[1], gate_up_out_ref)
    feed(z, 1)
    for copy in two_last:
        copy.wait_recv()
    stored(normed_two, normed_two_ref)
    act_back(opposite, 1)
    feed(opposite, 0)
    feed(opposite, 1)
    partial(1, opposite)
    feed(before, 1)
    feed(after, 1)
    stored(act, act_ref)
    stored(dgu, dgu_ref)
    partial(0, z)
    stored(dn_parts, dn_out_ref)
    for copy in normed_across:
        copy.wait_recv()
    for copy in copies:
        copy.wait_send()
    for step in range(1, 8):
        outgoing_copy(lax.rem(me + step, 8), step).wait_send()
    for copy in stores:
        copy.wait()


FRONT_SLOTS = 73
FRONT_LOCALS = 26


def rotation_tables():
    inverse = np.float32(THETA) ** (-np.arange(0, HEAD_SIZE, 2, dtype=np.float32) / HEAD_SIZE)
    phases = np.arange(1536, dtype=np.float32)[:, None] * inverse.astype(np.float32)[None, :]
    cosine, sine = np.zeros((1536, 128), np.float32), np.zeros((1536, 128), np.float32)
    cosine[:, 0:48] = cosine[:, 64:112] = np.cos(phases)
    sine[:, 64:112] = np.sin(phases)
    sine[:, 0:48] = -sine[:, 64:112]
    return cosine.reshape(12, BLOCK, 128), sine.reshape(12, BLOCK, 128)


def fronted(tokens, lens, gains, qkv, out_weight, gate_up, down, cotangent):
    def shape(dims, kind=jnp.bfloat16):
        return jax.ShapeDtypeStruct(dims, kind)

    def room(*dims):
        return pltpu.VMEM(dims, jnp.bfloat16)

    cosine, sine = rotation_tables()
    return pl.pallas_call(
        front_kernel,
        out_shape=(
            shape((4, 192, 1536)),
            shape((2, 192, 1536)),
            shape((1536, 512)),
            shape((1536, 384)),
            shape((8, 192, 1536)),
            shape((2, 1536, 512)),
            shape((512, 1536)),
            shape((4, 192, 1536)),
            shape((4, 192, 1536)),
            shape((4, 192, 1024)),
            shape((2, 4, 192, 1024)),
            shape((192, 1536), jnp.float32),
            shape((8, 192, 192)),
            shape((8, 384, 128)),
            shape((1536, 128)),
            shape((1536, 128)),
            shape((8, 384, 128)),
            shape((1536, 128), jnp.float32),
            shape((1536, 128), jnp.float32),
            shape((2, 192, 1536)),
            shape((8, 1, 384), jnp.float32),
        ),
        in_specs=[IN_VMEM, pl.BlockSpec(memory_space=pltpu.SMEM), IN_VMEM] + [ANY] * 7,
        out_specs=(ANY,) * 20 + (IN_VMEM,),
        scratch_shapes=[
            room(4, 192, 1536),
            room(1536, 384),
            room(1536, 384),
            room(1536, 512),
            room(1536, 512),
            room(4, 192, 384),
            room(4, 192, 384),
            pltpu.VMEM((2, 12, BLOCK, 128), jnp.float32),
            room(8, 192, 1536),
            room(2, 2, 1536, 512),
            room(2, 512, 1536),
            room(4, 192, 1536),
            room(4, 192, 1536),
            room(4, 192, 1024),
            room(2, 4, 192, 1024),
            pltpu.VMEM((4, 2, 192, 512), jnp.float32),
            pltpu.VMEM((1536, 384), jnp.float32),
            room(8, 192, 192),
            pltpu.VMEM((192, 1536), jnp.float32),
            room(8, 192, 192),
            room(8, 384, 128),
            room(1536, 128),
            room(1536, 128),
            room(8, 384, 128),
            pltpu.VMEM((1536, 128), jnp.float32),
            pltpu.VMEM((1536, 128), jnp.float32),
            room(2, 192, 1536),
            pltpu.SemaphoreType.DMA((FRONT_SLOTS + 8,)),
            pltpu.SemaphoreType.DMA((FRONT_SLOTS + 8,)),
            pltpu.SemaphoreType.DMA((FRONT_LOCALS + 1,)),
        ],
        compiler_params=pltpu.CompilerParams(
            collective_id=1, has_side_effects=True, vmem_limit_bytes=62 * 2**20
        ),
        name="front",
    )(
        tokens,
        lens,
        gains,
        qkv,
        out_weight,
        gate_up,
        down,
        cotangent,
        jnp.asarray(cosine),
        jnp.asarray(sine),
    )


def mid_kernel(
    dgu_ref,
    act_ref,
    normed_two_ref,
    upstream_ref,
    normed_ref,
    parts_ref,
    gate_up_ref,
    gate_up_other_ref,
    down_ref,
    down_other_ref,
    out_in_ref,
    here_in_ref,
    middle_in_ref,
    cotangent_in_ref,
    gain_ref,
    dh_ref,
    landed_ref,
    out_grad_ref,
    ffn_right_ref,
    ffn_left_ref,
    ffn_own_ref,
    gate_own_ref,
    feeds_ref,
    normed_other_ref,
    dgu,
    act,
    normed,
    upstream,
    parts,
    gate_up,
    down,
    turned,
    grads,
    grads_core,
    grads_a,
    grads_b,
    gate_left,
    gate_right,
    near_out,
    far_a,
    far_b,
    from_left,
    from_right,
    feeds,
    out_all,
    here,
    middle_room,
    cotangent,
    outgoing,
    landed,
    dhb,
    out_part,
    send_sem,
    recv_sem,
    local_sem,
):
    x, c = lax.axis_index("x"), lax.axis_index("c")
    z = lax.axis_index("z")
    after, before, opposite = lax.rem(z + 1, 4), lax.rem(z + 3, 4), lax.rem(z + 2, 4)
    x_after, x_before, x_far = lax.rem(x + 1, 4), lax.rem(x + 3, 4), lax.rem(x + 2, 4)
    right, left, across = {"z": after}, {"z": before}, {"yh": 1 - lax.axis_index("yh")}
    x_right, x_left, core = {"x": x_after}, {"x": x_before}, {"c": 1 - c}
    partners = [tensor_partner(step) for step in range(1, 8)] + [x_right, x_left, core]
    barrier = pltpu.get_barrier_semaphore()
    for partner in partners:
        pl.semaphore_signal(barrier, inc=1, device_id=partner, device_id_type=MESH)
    local_slots, slots = iter(range(MID_LOCALS)), iter(range(MID_SLOTS))
    stores, copies = [], []
    raw_sent = kernel_copies(send_sem, recv_sem)

    def moved(source, goal):
        copy = pltpu.make_async_copy(source, goal, local_sem.at[next(local_slots)])
        copy.start()
        return copy

    def stored(source, goal):
        stores.append(moved(source, goal))

    def sent(source, goal, device):
        copy = raw_sent(next(slots), source, goal, device)
        copies.append(copy)
        return copy

    def arrived(pair):
        for copy in pair:
            copy.wait_recv()

    dgu_load = moved(dgu_ref, dgu)
    gate_up_loads = [
        moved(gate_up_ref, gate_up.at[0]),
        moved(gate_up_other_ref, gate_up.at[1]),
    ]
    normed_load = moved(normed_two_ref, normed)
    parts_load = moved(parts_ref.at[0], parts)
    upstream_load = moved(upstream_ref, upstream)
    act_load = moved(act_ref, act)
    down_loads = [moved(down_ref, down.at[0]), moved(down_other_ref, down.at[1])]
    middle_load = moved(middle_in_ref, middle_room)
    cotangent_load = moved(cotangent_in_ref, cotangent)
    out_load = moved(out_in_ref, out_all)
    here_load = moved(here_in_ref, here)
    pl.semaphore_wait(barrier, len(partners))

    far = [
        sent(parts_ref.at[1, pl.ds(0, 96)], far_a, right),
        sent(parts_ref.at[1, pl.ds(96, 96)], far_b, left),
    ]
    normed_across = [
        sent(normed_ref.at[2 + k], normed_other_ref.at[k], across) for k in range(2)
    ]

    def add_core(kind):
        cored[kind].wait_recv()
        for k in range(8):
            grads[kind, k, c] = low(wide(grads[kind, k, c]) + wide(grads_core[kind, k]))
        spot = grads.at[kind, pl.ds(x_far * 2, 2), c]
        return [
            sent(spot.at[:, :, pl.ds(0, 512)], grads_a.at[kind], x_right),
            sent(spot.at[:, :, pl.ds(512, 512)], grads_b.at[kind], x_left),
        ]

    def grad(kind, right_side):
        for side in range(2):
            cols = pl.ds(side * 512, 512)
            value = jnp.dot(turned[...], right_side(cols), preferred_element_type=jnp.float32)
            grads[kind, :, :, :, cols] = low(value).reshape(8, 2, 96, 512)
        cored.append(sent(grads.at[kind, :, 1 - c], grads_core.at[kind], core))

    cored = []

    def add_x(kind):
        arrived(round_x[kind])
        for k in range(2):
            spot = grads[kind, x_after * 2 + k, c, :, 0:512]
            grads[kind, x_after * 2 + k, c, :, 0:512] = low(wide(spot) + wide(grads_a[kind, k]))
            spot = grads[kind, x_before * 2 + k, c, :, 512:1024]
            grads[kind, x_before * 2 + k, c, :, 512:1024] = low(
                wide(spot) + wide(grads_b[kind, k])
            )

    def partial(block):
        total = jnp.zeros((192, 1536), jnp.float32)
        for kind in range(2):
            for side in range(2):
                total = total + times_transposed(
                    dgu[kind, block, :, pl.ds(side * 512, 512)], gate_up[side, kind]
                )
        return total


    dgu_load.wait()
    for load in gate_up_loads:
        load.wait()
    to_right, to_left = partial(after), partial(before)
    normed_load.wait()
    turned[...] = jnp.transpose(normed[...].reshape(768, 1536))
    grad(0, lambda cols: dgu[0, :, :, cols].reshape(768, 512))
    arrived(far)
    near_out[0, 0:96] = low(to_right[0:96] + wide(far_a[...]))
    near_out[0, 96:192] = low(to_right[96:192])
    near_out[1, 0:96] = low(to_left[0:96])
    near_out[1, 96:192] = low(to_left[96:192] + wide(far_b[...]))
    near = [
        sent(near_out.at[0], from_left, right),
        sent(near_out.at[1], from_right, left),
    ]
    grad(1, lambda cols: dgu[1, :, :, cols].reshape(768, 512))
    round_x = [add_core(0)]
    upstream_load.wait()
    act_load.wait()
    turned[...] = jnp.transpose(upstream[...].reshape(768, 1536))
    grad(2, lambda cols: act[:, :, cols].reshape(768, 512))
    round_x.append(add_core(1))

    round_x.append(add_core(2))
    stored(grads.at[pl.ds(1, 2), pl.ds(x * 2, 2), c], ffn_own_ref)
    add_x(0)
    gate_second = [
        sent(grads.at[0, pl.ds(x_after * 2, 2), c], gate_left, x_right),
        sent(grads.at[0, pl.ds(x_before * 2, 2), c], gate_right, x_left),
    ]
    middle_load.wait()
    cotangent_load.wait()
    out_load.wait()
    middle = middle_room[...]
    scale = lax.rsqrt(jnp.mean(middle * middle, axis=1, keepdims=True) + EPSILON)
    unit = middle * scale
    parts_load.wait()
    arrived(near)
    dn = wide(parts[...]) + wide(from_left[...]) + wide(from_right[...])
    scaled = dn * gain_ref[1:2, :]
    dh = wide(cotangent[...]) + scale * (
        scaled - unit * jnp.mean(scaled * unit, axis=1, keepdims=True)
    )
    dh_ref[...] = dh
    dhb[...] = low(dh)
    do_moves = []
    for step in range(1, 8):
        outgoing[step] = low(times_transposed(dhb[...], out_all[step]))
        do_moves.append(sent(outgoing.at[step], landed.at[8 - step], tensor_partner(step)))
    landed[0] = low(times_transposed(dhb[...], out_all[0]))
    here_load.wait()
    for k in range(8):
        out_part[k] = low(transposed_times(here[k], dhb[...]))
    stored(out_part, out_grad_ref)
    for load in down_loads:
        load.wait()

    def feed(block):
        return jnp.dot(
            act[block, :, 0:512], down[0], preferred_element_type=jnp.float32
        ) + jnp.dot(act[block, :, 512:1024], down[1], preferred_element_type=jnp.float32)

    feeds[3] = low(feed(opposite))
    feeds[0], feeds[1], feeds[2] = low(feed(after)), low(feed(before)), low(feed(z))
    stored(feeds, feeds_ref)
    add_x(1)
    add_x(2)
    stored(grads.at[pl.ds(1, 2), pl.ds(x_after * 2, 2), c], ffn_right_ref)
    stored(grads.at[pl.ds(1, 2), pl.ds(x_before * 2, 2), c], ffn_left_ref)
    arrived(gate_second)
    for k in range(2):
        gate_left[k] = low(
            wide(grads[0, x * 2 + k, c]) + wide(gate_left[k]) + wide(gate_right[k])
        )
    stored(gate_left, gate_own_ref)
    arrived(do_moves)
    stored(landed, landed_ref)
    arrived(normed_across)
    for copy in copies:
        copy.wait_send()
    for copy in stores:
        copy.wait()


MID_SLOTS = 26
MID_LOCALS = 25


def middled(*arguments):
    def shape(dims, kind=jnp.bfloat16):
        return jax.ShapeDtypeStruct(dims, kind)

    def room(*dims):
        return pltpu.VMEM(dims, jnp.bfloat16)

    return pl.pallas_call(
        mid_kernel,
        out_shape=(
            shape((192, 1536), jnp.float32),
            shape((8, 192, 192)),
            shape((8, 192, 1536)),
            shape((2, 2, 96, 1024)),
            shape((2, 2, 96, 1024)),
            shape((2, 2, 96, 1024)),
            shape((2, 96, 1024)),
            shape((4, 192, 1536)),
            shape((2, 192, 1536)),
        ),
        in_specs=[ANY] * 14 + [IN_VMEM],
        out_specs=(IN_VMEM,) + (ANY,) * 8,
        scratch_shapes=[
            room(2, 4, 192, 1024),
            room(4, 192, 1024),
            room(4, 192, 1536),
            room(4, 192, 1536),
            room(192, 1536),
            room(2, 2, 1536, 512),
            room(2, 512, 1536),
            room(1536, 768),
            room(3, 8, 2, 96, 1024),
            room(3, 8, 96, 1024),
            room(3, 2, 96, 512),
            room(3, 2, 96, 512),
            room(2, 96, 1024),
            room(2, 96, 1024),
            room(2, 192, 1536),
            room(96, 1536),
            room(96, 1536),
            room(192, 1536),
            room(192, 1536),
            room(4, 192, 1536),
            room(8, 192, 1536),
            room(8, 192, 192),
            pltpu.VMEM((192, 1536), jnp.float32),
            room(192, 1536),
            room(8, 192, 192),
            room(8, 192, 192),
            room(192, 1536),
            room(8, 192, 1536),
            pltpu.SemaphoreType.DMA((MID_SLOTS,)),
            pltpu.SemaphoreType.DMA((MID_SLOTS,)),
            pltpu.SemaphoreType.DMA((MID_LOCALS,)),
        ],
        compiler_params=pltpu.CompilerParams(
            collective_id=3, has_side_effects=True, vmem_limit_bytes=62 * 2**20
        ),
        name="mid",
    )(*arguments)


def back_kernel(
    gain_ref,
    lse_ref,
    lens_ref,
    dh_in_ref,
    middle_in_ref,
    grads_in_ref,
    out_in_ref,
    q_in_ref,
    k_in_ref,
    v_in_ref,
    o_in_ref,
    cos_in_ref,
    sin_in_ref,
    weight_in_ref,
    weight_other_in_ref,
    tokens_in_ref,
    normed_ref,
    normed_first_ref,
    normed_second_ref,
    ffn_right_ref,
    ffn_left_ref,
    ffn_own_ref,
    gate_own_ref,
    feeds_ref,
    gate_up_ref,
    mixed_ref,
    input_grad_ref,
    qkv_grad_ref,
    out_grad_ref,
    ffn_grad_ref,
    gains_ref,
    landed,
    dk_sum,
    dv_sum,
    dp,
    normed,
    ffn_own,
    feeds,
    feed_a,
    feed_b,
    feed_from_left,
    feed_from_right,
    ffn_from_left,
    ffn_from_right,
    ffn_out,
    ffn_in,
    out_part,
    out_core,
    out_far_a,
    out_far_b,
    out_from_left,
    out_from_right,
    out_sum,
    out_shards,
    out_swap,
    out_swap_in,
    qkv_part,
    qkv_core,
    qkv_in,
    far_out,
    near_out,
    far_a,
    far_b,
    from_left,
    from_right,
    dq_out,
    dq_in,
    dkv_out,
    dkv_in,
    gain_out,
    gain_in,
    gate_up_rows,
    dh_ref,
    middle_ref,
    q_ref,
    k_ref,
    v_ref,
    o_ref,
    cos_ref,
    sin_ref,
    weight_ref,
    weight_other_ref,
    tokens_ref,
    send_sem,
    recv_sem,
    local_sem,
):
    x, yl, c = lax.axis_index("x"), lax.axis_index("yl"), lax.axis_index("c")
    yh, z = lax.axis_index("yh"), lax.axis_index("z")
    me = yh * 4 + z
    place = (x * 2 + yl) * 2 + c
    after, before, opposite = lax.rem(z + 1, 4), lax.rem(z + 3, 4), lax.rem(z + 2, 4)
    x_after, x_before, x_far = lax.rem(x + 1, 4), lax.rem(x + 3, 4), lax.rem(x + 2, 4)
    right, left, across = {"z": after}, {"z": before}, {"yh": 1 - yh}
    x_right, x_left = {"x": x_after}, {"x": x_before}
    core, other_yl, cross = {"c": 1 - c}, {"yl": 1 - yl}, {"yl": 1 - yl, "yh": 1 - yh}
    def dp_partner(step):
        goal = lax.rem(x * 2 + yl + step, 8)
        return {"x": lax.div(goal, 2), "yl": lax.rem(goal, 2)}, goal

    partners = [tensor_partner(step) for step in range(1, 8)]
    partners += [{**tensor_partner(step), "yl": 1 - yl} for step in range(1, 8)]
    partners += [core] + [dp_partner(step)[0] for step in range(1, 8)]
    barrier = pltpu.get_barrier_semaphore()
    for partner in partners:
        pl.semaphore_signal(barrier, inc=1, device_id=partner, device_id_type=MESH)
    raw_sent = kernel_copies(send_sem, recv_sem)
    copies = []
    slots = iter(range(SLOTS))

    def sent(source, goal, device):
        copy = raw_sent(next(slots), source, goal, device)
        copies.append(copy)
        return copy

    def arrived(pair):
        for copy in pair:
            copy.wait_recv()

    local_slots = iter(range(BACK_LOCALS))

    def fetched(source, goal):
        copy = pltpu.make_async_copy(source, goal, local_sem.at[next(local_slots)])
        copy.start()
        return copy

    attend_loads = [
        fetched(source, goal)
        for source, goal in (
            (grads_in_ref, landed),
            (q_in_ref, q_ref),
            (k_in_ref, k_ref),
            (v_in_ref, v_ref),
            (o_in_ref, o_ref),
            (cos_in_ref, cos_ref),
            (sin_in_ref, sin_ref),
        )
    ]
    out_load = fetched(out_in_ref.at[:, lines(c * 96, 96), :], out_part)
    weight_load = fetched(weight_in_ref, weight_ref)
    weight_other_load = fetched(weight_other_in_ref, weight_other_ref)
    normed_loads = [
        fetched(normed_ref, normed.at[lines(yh * 768, 768), :]),
        fetched(normed_first_ref, normed.at[lines((1 - yh) * 768, 384), :]),
        fetched(normed_second_ref, normed.at[lines((1 - yh) * 768 + 384, 384), :]),
    ]
    ffn_loads = [
        fetched(gate_own_ref, ffn_own.at[0]),
        fetched(ffn_own_ref, ffn_own.at[pl.ds(1, 2)]),
    ]
    feed_load = fetched(feeds_ref.at[pl.ds(0, 3)], feeds)
    tokens_load = fetched(tokens_in_ref, tokens_ref)
    middle_load = fetched(middle_in_ref, middle_ref)
    dh_load = fetched(dh_in_ref, dh_ref)
    rows_load = fetched(gate_up_ref.at[:, lines(place * 96, 96), :], gate_up_rows)

    pl.semaphore_wait(barrier, len(partners))
    out_cored = sent(out_in_ref.at[:, lines((1 - c) * 96, 96), :], out_core, core)
    ffn_second = [
        sent(ffn_right_ref, ffn_from_left, x_right),
        sent(ffn_left_ref, ffn_from_right, x_left),
    ]
    feed_far = [
        sent(feeds_ref.at[3, pl.ds(0, 96)], feed_a, right),
        sent(feeds_ref.at[3, pl.ds(96, 96)], feed_b, left),
    ]
    starts, ends = sequences(lens_ref)
    dk_sum[...] = jnp.zeros_like(dk_sum)
    dv_sum[...] = jnp.zeros_like(dv_sum)

    def unturned(values, rows):
        return values * cos_ref[rows, :] - pltpu.roll(values, 64, 1) * sin_ref[rows, :]

    dq_slot = [next(slots) for _ in range(4)][0]

    def dq_copy(block):
        return pltpu.make_async_remote_copy(
            src_ref=dq_out.at[block % 4],
            dst_ref=dq_in.at[block % 4],
            send_sem=send_sem.at[dq_slot + block % 4],
            recv_sem=recv_sem.at[dq_slot + block % 4],
            device_id=across,
            device_id_type=MESH,
        )

    def back(block):
        step = lax.rem(block - me + 8, 8)
        grads = landed[step]
        grad_block = jnp.concatenate([spread(grads[:, 0:96]), spread(grads[:, 96:192])], axis=0)
        query_block = q_ref[block]
        queries, first_row = block_queries(block, starts, ends)
        lse = lse_ref[block]
        centered = wide(grad_block) * wide(o_ref[block])
        centered = jnp.sum(jnp.transpose(centered), axis=0, keepdims=True)
        dq = jnp.zeros((384, 128), jnp.float32)
        for j in range((192 * (block + 1) + KEYS - 1) // KEYS):
            rows = pl.ds(j * KEYS, KEYS)
            key_block, value_block = k_ref[rows, :], v_ref[rows, :]
            scores, allowed = static_score(
                key_block, query_block, first_row, j * KEYS, queries, block * 192
            )
            weights = jnp.where(allowed, jnp.exp(scores - lse), 0.0)
            grad_weights = times_transposed(value_block, grad_block)
            grad_scores = low(weights * (grad_weights - centered))
            dv_sum[rows, :] += jnp.dot(
                low(weights), grad_block, preferred_element_type=jnp.float32
            )
            dk_sum[rows, :] += jnp.dot(
                grad_scores, query_block, preferred_element_type=jnp.float32
            )
            dq = dq + transposed_times(grad_scores, key_block)
        dq = dq * (HEAD_SIZE ** (-0.5))
        rows = pl.ds(block * 192, 192)
        first, second = unturned(dq[0:192], rows), unturned(dq[192:384], rows)
        dp[rows, 0:128] = low(first)
        dp[rows, 128:256] = low(second)

        @pl.when(yh != block // 4)
        def _():
            dq_out[block % 4] = low(jnp.concatenate([packed(first), packed(second)], axis=1))
            dq_copy(block).start()

    for load in attend_loads:
        load.wait()
    for block in range(4):
        back(block)
    out_load.wait()
    out_cored.wait_recv()
    for k in range(8):
        out_part[k] = low(wide(out_part[k]) + wide(out_core[k]))
    out_first = [
        sent(out_part.at[pl.ds(0, 4), :, columns(x_far * 384, 384)], out_far_a, x_right),
        sent(out_part.at[pl.ds(4, 4), :, columns(x_far * 384, 384)], out_far_b, x_left),
    ]
    for block in range(4, 6):
        back(block)
    arrived(feed_far)
    feed_load.wait()
    feeds[0, 0:96] = low(wide(feeds[0, 0:96]) + wide(feed_a[...]))
    feeds[1, 96:192] = low(wide(feeds[1, 96:192]) + wide(feed_b[...]))
    feed_second = [
        sent(feeds.at[0], feed_from_left, right),
        sent(feeds.at[1], feed_from_right, left),
    ]
    back(6)
    back(7)
    for block in range(8):
        rows = pl.ds(block * 192, 192)
        dp[rows, 256:384] = low(unturned(dk_sum[rows, :] * (HEAD_SIZE ** (-0.5)), rows))
        dp[rows, 384:512] = low(dv_sum[rows, :])

    mine = yh * 768
    for k in range(4):
        rows = lines((1 - yh) * 768 + k * 192, 192)
        dkv_out[k] = jnp.concatenate(
            [packed(dp[rows, 256:384]), packed(dp[rows, 384:512])], axis=1
        )
    exchanged = sent(dkv_out, dkv_in, across)
    for load in normed_loads:
        load.wait()
    for part in range(4):
        features = pl.ds(part * 384, 384)
        grad = transposed_times(normed[:, features], dp[...])
        qkv_part[part * 2 : part * 2 + 2] = low(grad).reshape(2, 2, 96, 512)
    qkv_cored = sent(qkv_part.at[:, 1 - c], qkv_core, core)
    for k in range(4):
        dq_copy(k).wait_recv()
    exchanged.wait_recv()
    weight_load.wait()
    weight_other_load.wait()

    def partial(block_z):
        theirs = jnp.concatenate([dq_in[block_z], dkv_in[block_z]], axis=1)
        return times_transposed(
            dp[lines(mine + block_z * 192, 192), :], weight_ref[...]
        ) + times_transposed(theirs, weight_other_ref[...])

    far_out[...] = low(partial(opposite))
    far = [
        sent(far_out.at[pl.ds(0, 96)], far_a, right),
        sent(far_out.at[pl.ds(96, 96)], far_b, left),
    ]
    arrived(ffn_second)
    for load in ffn_loads:
        load.wait()
    for kind in range(2):
        ffn_own[kind + 1] = low(
            wide(ffn_own[kind + 1]) + wide(ffn_from_left[kind]) + wide(ffn_from_right[kind])
        )
    ffn_sum = wide(ffn_own[...])
    flipped = jnp.where(yl == 0, ffn_sum[:, 1], ffn_sum[:, 0])
    kept = jnp.where(yl == 0, ffn_sum[:, 0], ffn_sum[:, 1])
    ffn_out[0] = low(flipped[..., 0:512])
    ffn_out[1] = low(flipped[..., 512:1024])
    ffn_out[2] = low(kept[..., 512:1024])
    ffn_moves = [
        sent(ffn_out.at[k], ffn_in.at[k], device)
        for k, device in enumerate((other_yl, cross, across))
    ]
    ffn_grad_ref[...] = kept[..., 0:512]
    to_right, to_left = partial(after), partial(before)
    out_cols = [columns(place_x * 384, 384) for place_x in (x_after, x_before)]
    arrived(out_first)
    for k in range(4):
        out_part[k, :, out_cols[0]] = low(wide(out_part[k, :, out_cols[0]]) + wide(out_far_a[k]))
        out_part[4 + k, :, out_cols[1]] = low(
            wide(out_part[4 + k, :, out_cols[1]]) + wide(out_far_b[k])
        )
    out_second = [
        sent(out_part.at[:, :, out_cols[0]], out_from_left, x_right),
        sent(out_part.at[:, :, out_cols[1]], out_from_right, x_left),
    ]
    qkv_cored.wait_recv()
    for k in range(8):
        qkv_part[k, c] = low(wide(qkv_part[k, c]) + wide(qkv_core[k]))
    qkv_moves = [
        sent(qkv_part.at[goal, c], qkv_in.at[step - 1], device)
        for step, (device, goal) in ((step, dp_partner(step)) for step in range(1, 8))
    ]
    arrived(far)
    near_out[0, 0:96] = low(to_right[0:96] + wide(far_a[...]))
    near_out[0, 96:192] = low(to_right[96:192])
    near_out[1, 0:96] = low(to_left[0:96])
    near_out[1, 96:192] = low(to_left[96:192] + wide(far_b[...]))
    near = [
        sent(near_out.at[0], from_left, right),
        sent(near_out.at[1], from_right, left),
    ]
    own = partial(z)
    arrived(out_second)
    own_cols = columns(x * 384, 384)
    for k in range(8):
        total = wide(out_part[k, :, own_cols]) + wide(out_from_left[k]) + wide(out_from_right[k])
        out_sum[k, 0] = low(total[:, 0:192])
        out_sum[k, 1] = low(total[:, 192:384])
    out_moves = []
    for step in range(8):
        place_yh = tensor_partner(step)
        for side in range(2):
            if step + side > 0:
                goal_yl = yl if side == 0 else 1 - yl
                out_moves.append(
                    sent(
                        out_sum.at[step, goal_yl],
                        out_shards.at[step * 2 + side - 1],
                        {**place_yh, "yl": goal_yl},
                    )
                )
    arrived(feed_second)
    middle_load.wait()
    mixed_ref[...] = low(
        middle_ref[...] + wide(feeds[2]) + wide(feed_from_left[...]) + wide(feed_from_right[...])
    )
    arrived(qkv_moves)
    qkv_final = wide(qkv_part[x * 2 + yl, c])
    for k in range(7):
        qkv_final = qkv_final + wide(qkv_in[k])
    qkv_grad_ref[...] = qkv_final
    arrived(ffn_moves)
    ffn_final = ffn_grad_ref[...]
    for k in range(3):
        ffn_final = ffn_final + wide(ffn_in[k])
    ffn_grad_ref[...] = ffn_final
    rows_load.wait()
    gain_one = jnp.sum(
        qkv_final * wide(weight_ref[lines(place * 96, 96), :]), axis=1, keepdims=True
    )
    gain_two = jnp.sum(
        ffn_final[0] * wide(gate_up_rows[0]) + ffn_final[1] * wide(gate_up_rows[1]),
        axis=1,
        keepdims=True,
    )
    lanes = lax.broadcasted_iota(jnp.int32, (96, 128), 1)
    gain_out[...] = jnp.where(lanes == 0, gain_one, jnp.where(lanes == 1, gain_two, 0.0))
    gain_shared = [
        sent(gain_out, gain_in.at[step - 1], tensor_partner(step)) for step in range(1, 8)
    ]
    arrived(out_moves)
    out_final = wide(out_sum[0, yl])
    for k in range(15):
        out_final = out_final + wide(out_shards[k])
    out_swap[...] = low(jnp.where(c == 0, out_final[:, 96:192], out_final[:, 0:96]))
    out_swapped = sent(out_swap, out_swap_in, core)
    out_mine = jnp.where(c == 0, out_final[:, 0:96], out_final[:, 96:192])
    out_grad_ref[lines(c * 96, 96), :] = out_mine
    arrived(near)
    dn = own + wide(from_left[...]) + wide(from_right[...])
    tokens_load.wait()
    hidden = wide(tokens_ref[...])
    scale = lax.rsqrt(jnp.mean(hidden * hidden, axis=1, keepdims=True) + EPSILON)
    unit = hidden * scale
    scaled = dn * gain_ref[0:1, :]
    dh_load.wait()
    input_grad_ref[...] = dh_ref[...] + scale * (
        scaled - unit * jnp.mean(scaled * unit, axis=1, keepdims=True)
    )
    out_swapped.wait_recv()
    out_grad_ref[lines((1 - c) * 96, 96), :] = wide(out_swap_in[...])
    arrived(gain_shared)
    total = gain_out[...]
    for k in range(7):
        total = total + gain_in[k]
    gains_ref[...] = total
    for copy in copies:
        copy.wait_send()
    for k in range(4):
        dq_copy(k).wait_send()


SLOTS = 72
BACK_LOCALS = 23


def finished_back(*arguments):
    def shape(dims, kind=jnp.float32):
        return jax.ShapeDtypeStruct(dims, kind)

    def room(*dims):
        return pltpu.VMEM(dims, jnp.bfloat16)

    return pl.pallas_call(
        back_kernel,
        out_shape=(
            shape((192, 1536), jnp.bfloat16),
            shape((192, 1536)),
            shape((96, 512)),
            shape((192, 96)),
            shape((3, 96, 512)),
            shape((96, 128)),
        ),
        in_specs=[IN_VMEM] * 2 + [pl.BlockSpec(memory_space=pltpu.SMEM)] + [ANY] * 22,
        out_specs=(IN_VMEM,) * 6,
        scratch_shapes=[
            room(8, 192, 192),
            pltpu.VMEM((1536, 128), jnp.float32),
            pltpu.VMEM((1536, 128), jnp.float32),
            room(1536, 512),
            room(1536, 1536),
            room(3, 2, 96, 1024),
            room(3, 192, 1536),
            room(96, 1536),
            room(96, 1536),
            room(192, 1536),
            room(192, 1536),
            room(2, 2, 96, 1024),
            room(2, 2, 96, 1024),
            room(3, 3, 96, 512),
            room(3, 3, 96, 512),
            room(8, 96, 1536),
            room(8, 96, 1536),
            room(4, 96, 384),
            room(4, 96, 384),
            room(8, 96, 384),
            room(8, 96, 384),
            room(8, 2, 96, 192),
            room(15, 96, 192),
            room(96, 96),
            room(96, 96),
            room(8, 2, 96, 512),
            room(8, 96, 512),
            room(7, 96, 512),
            room(192, 1536),
            room(2, 192, 1536),
            room(96, 1536),
            room(96, 1536),
            room(192, 1536),
            room(192, 1536),
            room(4, 192, 192),
            room(4, 192, 192),
            room(4, 192, 192),
            room(4, 192, 192),
            pltpu.VMEM((96, 128), jnp.float32),
            pltpu.VMEM((7, 96, 128), jnp.float32),
            room(2, 96, 512),
            pltpu.VMEM((192, 1536), jnp.float32),
            pltpu.VMEM((192, 1536), jnp.float32),
            room(8, 384, 128),
            room(1536, 128),
            room(1536, 128),
            room(8, 384, 128),
            pltpu.VMEM((1536, 128), jnp.float32),
            pltpu.VMEM((1536, 128), jnp.float32),
            room(1536, 512),
            room(1536, 384),
            room(192, 1536),
            pltpu.SemaphoreType.DMA((SLOTS,)),
            pltpu.SemaphoreType.DMA((SLOTS,)),
            pltpu.SemaphoreType.DMA((BACK_LOCALS,)),
        ],
        compiler_params=pltpu.CompilerParams(
            collective_id=2, has_side_effects=True, vmem_limit_bytes=63 * 2**20
        ),
        name="back",
    )(*arguments)


def finish_kernel(
    mixed_in,
    input_in,
    qkv_in,
    out_in,
    ffn_in,
    gains_in,
    gain_ref,
    mixed_ref,
    input_ref,
    qkv_ref,
    out_ref,
    gate_up_ref,
    down_ref,
    gains_ref,
    mixed_room,
    input_room,
    ffn_room,
    out_room,
    sem,
):
    rooms = (
        (mixed_in, mixed_room, ((mixed_room, mixed_ref),)),
        (input_in, input_room, ((input_room, input_ref),)),
        (
            ffn_in,
            ffn_room,
            ((ffn_room.at[pl.ds(0, 2)], gate_up_ref), (ffn_room.at[2], down_ref)),
        ),
        (out_in, out_room, ((out_room, out_ref),)),
    )
    arriving, copies = [], []
    for k, (source, room, _) in enumerate(rooms):
        arriving.append(pltpu.make_async_copy(source, room, sem.at[k]))
        arriving[-1].start()
    for arrival, (_, _, goals) in zip(arriving, rooms):
        arrival.wait()
        for source, goal in goals:
            copies.append(pltpu.make_async_copy(source, goal, sem.at[4 + len(copies)]))
            copies[-1].start()
    qkv_ref[...] = jnp.concatenate(
        [packed(qkv_in[:, head * 128 : head * 128 + 128]) for head in range(4)], axis=1
    )
    place = (lax.axis_index("x") * 2 + lax.axis_index("yl")) * 2 + lax.axis_index("c")
    gains = jnp.transpose(gains_in[...])[0:2]
    rows = jnp.zeros((2, 96), jnp.float32)
    for k in range(16):
        rows = jnp.where(place == k, gain_ref[:, k * 96 : k * 96 + 96], rows)
    gains_ref[...] = gains / rows
    for copy in copies:
        copy.wait()


def finished(*arguments):
    def shape(*dims):
        return jax.ShapeDtypeStruct(dims, jnp.float32)

    return pl.pallas_call(
        finish_kernel,
        out_shape=(
            jax.ShapeDtypeStruct((192, 1536), jnp.bfloat16),
            shape(192, 1536),
            shape(96, 384),
            shape(192, 96),
            shape(2, 96, 512),
            shape(96, 512),
            shape(2, 96),
        ),
        in_specs=[ANY, ANY, IN_VMEM, ANY, ANY, IN_VMEM, IN_VMEM],
        out_specs=(ANY, ANY, IN_VMEM, ANY, ANY, ANY, IN_VMEM),
        scratch_shapes=[
            pltpu.VMEM((192, 1536), jnp.bfloat16),
            pltpu.VMEM((192, 1536), jnp.float32),
            pltpu.VMEM((3, 96, 512), jnp.float32),
            pltpu.VMEM((192, 96), jnp.float32),
            pltpu.SemaphoreType.DMA((9,)),
        ],
        compiler_params=pltpu.CompilerParams(vmem_limit_bytes=63 * 2**20),
        name="finish",
    )(*arguments)


def per_device(
    tokens,
    seq_lens,
    query_key_value_weight,
    out_weight,
    gate_up_weight,
    down_weight,
    norm_gains,
    cotangent,
):
    (
        normed_half,
        normed_first,
        weight_wide,
        weight_other,
        out_all,
        gate_up_other,
        down_other,
        upstream_all,
        normed_two_all,
        activated,
        grad_gate_up,
        middle,
        attended_here,
        queries,
        keys_all,
        values_all,
        heads,
        cos_part,
        sin_part,
        dn_parts,
        log_sums,
    ) = fronted(
        tokens,
        seq_lens,
        norm_gains,
        query_key_value_weight,
        out_weight,
        gate_up_weight,
        down_weight,
        cotangent,
    )
    (
        grad_middle,
        grad_heads,
        out_half,
        ffn_right,
        ffn_left,
        ffn_own,
        gate_own,
        feeds,
        normed_second,
    ) = middled(
        grad_gate_up,
        activated,
        normed_two_all,
        upstream_all,
        normed_half,
        dn_parts,
        gate_up_weight,
        gate_up_other,
        down_weight,
        down_other,
        out_all,
        attended_here,
        middle,
        cotangent,
        norm_gains,
    )
    mixed, input_grad, qkv_grad, out_grad, ffn_grad, gains_grad = finished_back(
        norm_gains,
        log_sums,
        seq_lens,
        grad_middle,
        middle,
        grad_heads,
        out_half,
        queries,
        keys_all,
        values_all,
        heads,
        cos_part,
        sin_part,
        weight_wide,
        weight_other,
        tokens,
        normed_half.reshape(768, 1536),
        normed_first.reshape(384, 1536),
        normed_second.reshape(384, 1536),
        ffn_right,
        ffn_left,
        ffn_own,
        gate_own,
        feeds,
        gate_up_weight,
    )
    mixed, input_grad, qkv_grad, out_grad, gate_up_grad, down_grad, gains_grad = finished(
        mixed, input_grad, qkv_grad, out_grad, ffn_grad, gains_grad, norm_gains
    )
    return mixed, input_grad, qkv_grad, out_grad, gate_up_grad, down_grad.T, gains_grad


def solution(mesh):
    split = Mesh(mesh.devices.reshape(4, 2, 2, 2, 4), ALL)
    placed = (
        P(ALL, None),
        P(DP, None),
        P(None, TENSOR),
        P(TENSOR, None),
        P(None, None, TENSOR),
        P(TENSOR, None),
        P(),
        P(ALL, None),
    )
    return jax.shard_map(
        per_device,
        mesh=split,
        in_specs=placed,
        out_specs=(
            P(ALL, None),
            P(ALL, None),
            P(DP, TENSOR),
            P(TENSOR, DP),
            P(None, DP, TENSOR),
            P(TENSOR, DP),
            P(None, DP),
        ),
        check_vma=False,
    )
```

```python
import functools

import jax
import jax.numpy as jnp
import numpy as np
from jax import lax
from jax.experimental import pallas as pl
from jax.experimental.pallas import tpu as pltpu
from jax.sharding import Mesh
from jax.sharding import PartitionSpec as P

HEAD_SIZE = 96
BLOCK = 128
DP = ("x", "yl", "c")
TENSOR = ("yh", "z")
ALL = DP + TENSOR
MESH = pl.DeviceIdType.MESH

EPSILON = 1e-05
THETA = 100000.0
masked_score = -1e30


def times_transposed(left, right):
    return lax.dot_general(
        left, right, (((1,), (1,)), ((), ())), preferred_element_type=jnp.float32
    )


def transposed_times(left, right):
    return lax.dot_general(
        left, right, (((0,), (0,)), ((), ())), preferred_element_type=jnp.float32
    )


def barrier_with(partners):
    barrier = pltpu.get_barrier_semaphore()
    for partner in partners:
        pl.semaphore_signal(barrier, inc=1, device_id=partner, device_id_type=MESH)
    pl.semaphore_wait(barrier, len(partners))


def kernel_copies(send_sem, recv_sem):
    def sent(slot, source, goal, device):
        copy = pltpu.make_async_remote_copy(
            src_ref=source,
            dst_ref=goal,
            send_sem=send_sem.at[slot],
            recv_sem=recv_sem.at[slot],
            device_id=device,
            device_id_type=MESH,
        )
        copy.start()
        return copy

    return sent


def tensor_partner(step):
    goal = lax.rem(lax.axis_index("yh") * 4 + lax.axis_index("z") + step, 8)
    return {"yh": lax.div(goal, 4), "z": lax.rem(goal, 4)}


def spread(values):
    gap = jnp.zeros((values.shape[0], 16), values.dtype)
    return jnp.concatenate([values[:, :48], gap, values[:, 48:], gap], axis=1)


def packed(values):
    return jnp.concatenate([values[:, :48], values[:, 64:112]], axis=1)


KEYS = 256


ANY = pl.BlockSpec(memory_space=pl.ANY)
IN_VMEM = pl.BlockSpec(memory_space=pltpu.VMEM)


def static_score(key_block, query_block, first_row, key_start, queries, query_start):
    scores = times_transposed(key_block, query_block) * (HEAD_SIZE ** (-0.5))
    keys = key_start + lax.broadcasted_iota(jnp.int32, scores.shape, 0)
    allowed = keys >= first_row
    if key_start + scores.shape[0] > query_start:
        allowed = allowed & (keys <= queries)
    return scores, allowed


def block_queries(block, starts, ends):
    queries = lax.broadcasted_iota(jnp.int32, (1, 384), 1)
    queries = block * 192 + jnp.where(queries >= 192, queries - 192, queries)
    first_row = queries
    for slot in range(4):
        within = (starts[slot] <= queries) & (queries < ends[slot])
        first_row = jnp.where(within, starts[slot], first_row)
    return queries, first_row


def sequences(lens_ref):
    starts, ends = [], []
    start = jnp.int32(0)
    for slot in range(4):
        length = lens_ref[0, slot]
        starts.append(start)
        ends.append(start + length)
        start = start + lax.div(length + (BLOCK - 1), BLOCK) * BLOCK
    return starts, ends


def columns(start, size):
    return pl.ds(pl.multiple_of(start, 128), size)


def lines(start, size):
    return pl.ds(pl.multiple_of(start, 16), size)


def wide(value):
    return value.astype(jnp.float32)


def low(value):
    return value.astype(jnp.bfloat16)


def front_kernel(
    tokens_ref,
    lens_ref,
    gain_ref,
    qkv_ref,
    out_weight_ref,
    gate_up_ref,
    down_ref,
    cotangent_ref,
    cos_table_ref,
    sin_table_ref,
    normed_ref,
    normed_other_ref,
    weight_out_ref,
    weight_other_out_ref,
    out_out_ref,
    gate_up_out_ref,
    down_out_ref,
    upstream_ref,
    normed_two_ref,
    act_ref,
    dgu_ref,
    middle_out_ref,
    here_out_ref,
    q_out_ref,
    k_out_ref,
    v_out_ref,
    o_out_ref,
    cos_out_ref,
    sin_out_ref,
    dn_out_ref,
    lse_ref,
    landed,
    raw,
    raw_other,
    weight,
    weight_other,
    projected_out,
    projected_in,
    tables,
    out_all,
    gate_up,
    down,
    upstream,
    normed_two,
    act,
    dgu,
    dact,
    scores,
    outgoing,
    middle_ref,
    here_ref,
    q_ref,
    k_ref,
    v_ref,
    o_ref,
    cos_ref,
    sin_ref,
    dn_part,
    send_sem,
    recv_sem,
    local_sem,
):
    x, yl, c = lax.axis_index("x"), lax.axis_index("yl"), lax.axis_index("c")
    yh, z = lax.axis_index("yh"), lax.axis_index("z")
    me = yh * 4 + z
    after, before, opposite = lax.rem(z + 1, 4), lax.rem(z + 3, 4), lax.rem(z + 2, 4)
    other = 1 - yh
    right, left, across = {"z": after}, {"z": before}, {"yh": other}
    x_after, x_before, x_far = lax.rem(x + 1, 4), lax.rem(x + 3, 4), lax.rem(x + 2, 4)
    x_right, x_left, core = {"x": x_after}, {"x": x_before}, {"c": 1 - c}

    def crossed(step):
        place = tensor_partner(step)
        return {**place, "yl": lax.rem(yl + yh + place["yh"], 2)}

    tensor_partners = [tensor_partner(step) for step in range(1, 8)]
    cross_partners = [{"yl": 1 - yl, "yh": other, "z": lax.rem(z + k, 4)} for k in range(4)]
    partners = tensor_partners + cross_partners + [x_right, x_left, core]
    barrier = pltpu.get_barrier_semaphore()
    for partner in partners:
        pl.semaphore_signal(barrier, inc=1, device_id=partner, device_id_type=MESH)

    stores = []
    local_slots = iter(range(FRONT_LOCALS))

    def moved(source, goal):
        copy = pltpu.make_async_copy(source, goal, local_sem.at[next(local_slots)])
        copy.start()
        return copy

    def stored(source, goal):
        stores.append(moved(source, goal))

    qkv_load = moved(qkv_ref, raw)
    cos_load = moved(cos_table_ref, tables.at[0])
    sin_load = moved(sin_table_ref, tables.at[1])
    hidden = wide(tokens_ref[...])
    scale = lax.rsqrt(jnp.mean(hidden * hidden, axis=1, keepdims=True) + EPSILON)
    landed[z] = low(hidden * scale * gain_ref[0:1, :])
    pl.semaphore_wait(barrier, len(partners))

    raw_sent = kernel_copies(send_sem, recv_sem)
    copies = []
    slots = iter(range(FRONT_SLOTS))

    def sent(source, goal, device):
        copy = raw_sent(next(slots), source, goal, device)
        copies.append(copy)
        return copy

    lower, upper, whole = pl.ds(0, 96), pl.ds(96, 96), pl.ds(0, 192)

    def shard(block_z, rows, device):
        spot = landed.at[block_z, rows]
        return sent(spot, spot, device)

    def qkv_part(quarter, half, part=pl.ds(0, 192)):
        return raw_other.at[lines(quarter * 384 + half * 192 + part.start, part.size), :]

    def gate_up_part(quarter, half, part=pl.ds(0, 2)):
        rows = lines(quarter * 384, 384)
        return gate_up.at[1, part, rows, columns(half * 256, 256)]

    def down_part(quarter, half, part=pl.ds(0, 128)):
        rows = lines(quarter * 128 + part.start, part.size)
        return down.at[1, rows, columns(half * 768, 768)]

    def out_part(quarter, half, part=pl.ds(1, 7)):
        return out_all.at[part, lines(quarter * 48, 48), columns(half * 768, 768)]

    to_right = shard(z, whole, right)
    to_left = shard(z, whole, left)
    qkv_cross = sent(
        qkv_ref.at[lines(x * 384 + c * 192, 192), :], qkv_part(x, c), crossed(4)
    )
    out_cross = []
    piece = out_weight_ref.at[lines(x * 48, 48), columns(c * 768, 768)]
    for step in range(1, 8):
        goal = out_all.at[8 - step, lines(x * 48, 48), columns(c * 768, 768)]
        out_cross.append(sent(piece, goal, crossed(step)))
    gate_up_cross = sent(
        gate_up_ref.at[:, lines(x * 384, 384), columns(c * 256, 256)],
        gate_up_part(x, c),
        crossed(4),
    )
    down_cross = sent(
        down_ref.at[lines(x * 128, 128), columns(c * 768, 768)], down_part(x, c), crossed(4)
    )
    upstream_load = moved(cotangent_ref, upstream.at[z])
    out_load = moved(out_weight_ref, out_all.at[0])
    gate_up_load = moved(gate_up_ref, gate_up.at[0])
    down_load = moved(down_ref, down.at[0])

    starts, ends = sequences(lens_ref)
    cos_load.wait()
    sin_load.wait()
    for block in range(12):
        begin, end = jnp.int32(0), jnp.int32(0)
        for slot in range(4):
            within = (starts[slot] <= block * BLOCK) & (block * BLOCK < ends[slot])
            begin = jnp.where(within, starts[slot], begin)
            end = jnp.where(within, ends[slot], end)
        used = block - lax.div(begin, BLOCK)
        rows = pl.ds(block * BLOCK, BLOCK)
        token = block * BLOCK + lax.broadcasted_iota(jnp.int32, (BLOCK, 128), 0)
        cos_ref[rows, :] = jnp.where(token < end, tables[0, used], tables[0, block])
        sin_ref[rows, :] = jnp.where(token < end, tables[1, used], tables[1, block])
    qkv_load.wait()
    for head in range(4):
        weight[:, head * 128 : head * 128 + 128] = spread(raw[:, head * 96 : head * 96 + 96])
    stored(weight, weight_out_ref)
    stored(cos_ref, cos_out_ref)
    stored(sin_ref, sin_out_ref)

    def projected(block_z, weights):
        values = jnp.dot(landed[block_z], weights[...], preferred_element_type=jnp.float32)
        rows = lines((yh * 4 + block_z) * 192, 192)
        cos_part, sin_part = cos_ref[rows, :], sin_ref[rows, :]
        heads = [values[:, head * 128 : head * 128 + 128] for head in range(4)]
        for head in range(3):
            heads[head] = heads[head] * cos_part + pltpu.roll(heads[head], 64, 1) * sin_part
        return heads

    def kept(block, heads):
        rows = lines(block * 192, 192)
        q_ref[block, 0:192, :] = heads[0]
        q_ref[block, 192:384, :] = heads[1]
        k_ref[rows, :] = heads[2]
        v_ref[rows, :] = heads[3]

    def project_own(block_z):
        kept(yh * 4 + block_z, [low(head) for head in projected(block_z, weight)])

    exchanged = []

    def project_other(k, block_z):
        heads = [packed(head) for head in projected(block_z, weight_other)]
        projected_out[k] = low(jnp.concatenate(heads, axis=1))
        exchanged.append(sent(projected_out.at[k], projected_in.at[block_z], across))

    def spread_out(part, halves, awaited):
        goal = part(x, c)
        awaited.append(sent(goal, goal, core))
        return [sent(goal, goal, x_right), sent(goal, goal, x_left)]

    def pass_on(part, halves, awaited, arriving):
        arriving[0].wait_recv()
        first, second = part(x_before, c), part(x_before, c, halves[0])
        far = [sent(second, second, x_right)]
        awaited.append(sent(first, first, core))
        arriving[1].wait_recv()
        first, second = part(x_after, c), part(x_after, c, halves[1])
        far.append(sent(second, second, x_left))
        awaited.append(sent(first, first, core))
        return far

    def forward(part, halves, awaited, far):
        for k in range(2):
            far[k].wait_recv()
            goal = part(x_far, c, halves[k])
            awaited.append(sent(goal, goal, core))

    def settle(part, halves, awaited):
        for copy in awaited:
            copy.wait_recv()

    gate_up_plan = (gate_up_part, (pl.ds(0, 1), pl.ds(1, 1)), [])
    down_plan = (down_part, (pl.ds(0, 64), pl.ds(64, 64)), [])
    out_plan = (out_part, (pl.ds(1, 4), pl.ds(5, 3)), [])
    qkv_plan = (qkv_part, (pl.ds(0, 96), pl.ds(96, 96)), [])

    project_own(z)
    qkv_cross.wait_recv()
    qkv_moves = spread_out(*qkv_plan)
    qkv_far = pass_on(*qkv_plan, qkv_moves)
    forward(*qkv_plan, qkv_far)
    settle(*qkv_plan)
    for head in range(4):
        weight_other[:, head * 128 : head * 128 + 128] = spread(
            raw_other[:, head * 96 : head * 96 + 96]
        )
    stored(raw_other, weight_other_out_ref)
    to_right.wait_recv()
    last_right = shard(before, lower, right)
    to_left.wait_recv()
    last_left = shard(after, upper, left)
    project_other(0, z)
    project_other(1, before)
    project_other(2, after)
    project_own(before)
    project_own(after)
    for copy in out_cross:
        copy.wait_recv()
    out_moves = spread_out(*out_plan)
    last_right.wait_recv()
    last_left.wait_recv()
    project_other(3, opposite)
    project_own(opposite)
    upstream_load.wait()
    upstream_right = sent(upstream.at[z], upstream.at[z], right)
    upstream_left = sent(upstream.at[z], upstream.at[z], left)
    stored(landed, normed_ref)
    for copy in exchanged:
        copy.wait_recv()
    for block_z in range(4):
        arrived = projected_in[block_z]
        kept(
            other * 4 + block_z,
            [spread(arrived[:, head * 96 : head * 96 + 96]) for head in range(4)],
        )
    out_far = pass_on(*out_plan, out_moves)
    gate_up_cross.wait_recv()
    gate_up_moves = spread_out(*gate_up_plan)
    down_cross.wait_recv()
    down_moves = spread_out(*down_plan)
    stored(q_ref, q_out_ref)
    stored(k_ref, k_out_ref)
    stored(v_ref, v_out_ref)

    def outgoing_copy(block, step):
        return pltpu.make_async_remote_copy(
            src_ref=outgoing.at[block],
            dst_ref=here_ref.at[8 - step],
            send_sem=send_sem.at[FRONT_SLOTS + step],
            recv_sem=recv_sem.at[FRONT_SLOTS + step],
            device_id={"yh": lax.div(block, 4), "z": lax.rem(block, 4)},
            device_id_type=MESH,
        )

    here_sem = local_sem.at[FRONT_LOCALS]

    def attend(block):
        query_block = q_ref[block]
        queries, first_row = block_queries(block, starts, ends)
        count = (192 * (block + 1) + KEYS - 1) // KEYS
        peak = jnp.full((8, 384), masked_score, jnp.float32)
        for j in range(count):
            rows = pl.ds(j * KEYS, KEYS)
            part, allowed = static_score(
                k_ref[rows, :], query_block, first_row, j * KEYS, queries, block * 192
            )
            part = jnp.where(allowed, part, masked_score)
            scores[rows, :] = part
            peak = jnp.maximum(peak, jnp.max(part.reshape(KEYS // 8, 8, 384), axis=0))
        peak = jnp.max(peak, axis=0, keepdims=True)
        total = jnp.zeros((8, 384), jnp.float32)
        out = jnp.zeros((384, 128), jnp.float32)
        for j in range(count):
            rows = pl.ds(j * KEYS, KEYS)
            weights = jnp.exp(scores[rows, :] - peak)
            total = total + jnp.sum(weights.reshape(KEYS // 8, 8, 384), axis=0)
            out = out + transposed_times(low(weights), v_ref[rows, :])
        total = jnp.sum(total, axis=0, keepdims=True)
        lse_ref[block] = peak + jnp.log(total)
        out = out * jnp.transpose(jnp.broadcast_to(1.0 / total, (128, 384)))
        o_ref[block] = low(out)
        outgoing[block] = low(
            jnp.concatenate([packed(out[0:192]), packed(out[192:384])], axis=1)
        )
        step = lax.rem(block - me + 8, 8)

        @pl.when(step != 0)
        def _():
            outgoing_copy(block, step).start()

        @pl.when(step == 0)
        def _():
            pltpu.make_async_copy(outgoing.at[block], here_ref.at[0], here_sem).start()

    for block in range(6):
        attend(block)
    forward(*out_plan, out_far)
    for block in range(6, 8):
        attend(block)
    settle(*out_plan)
    upstream_right.wait_recv()
    upstream_last = [sent(upstream.at[before, lower], upstream.at[before, lower], right)]
    upstream_left.wait_recv()
    upstream_last.append(sent(upstream.at[after, upper], upstream.at[after, upper], left))
    out_load.wait()

    pltpu.make_async_copy(outgoing.at[me], here_ref.at[0], here_sem).wait()
    middle = wide(tokens_ref[...]) + jnp.dot(
        here_ref[0], out_all[0], preferred_element_type=jnp.float32
    )
    for step in range(7, 0, -1):
        outgoing_copy(lax.rem(me + step, 8), step).wait_recv()
        middle += jnp.dot(here_ref[8 - step], out_all[8 - step], preferred_element_type=jnp.float32)
    middle_ref[...] = middle
    stored(middle_ref, middle_out_ref)
    stored(here_ref, here_out_ref)
    stored(o_ref, o_out_ref)
    scale = lax.rsqrt(jnp.mean(middle * middle, axis=1, keepdims=True) + EPSILON)
    normed_two[z] = low(middle * scale * gain_ref[1:2, :])
    two_right = sent(normed_two.at[z], normed_two.at[z], right)
    two_left = sent(normed_two.at[z], normed_two.at[z], left)
    normed_across = [sent(landed.at[k], normed_other_ref.at[k], across) for k in range(2)]
    stored(out_all, out_out_ref)
    gate_up_load.wait()
    down_load.wait()

    def act_back(block, side):
        dact[block, side] = times_transposed(upstream[block], down[side])

    def feed(block, side):
        cols = pl.ds(side * 512, 512)
        gate = jnp.dot(normed_two[block], gate_up[side, 0], preferred_element_type=jnp.float32)
        up = jnp.dot(normed_two[block], gate_up[side, 1], preferred_element_type=jnp.float32)
        sigmoid = 1.0 / (1.0 + jnp.exp(-gate))
        silu = gate * sigmoid
        act[block, :, cols] = low(silu * up)
        grad = dact[block, side]
        dgu[0, block, :, cols] = low(grad * up * sigmoid * (1.0 + gate * (1.0 - sigmoid)))
        dgu[1, block, :, cols] = low(grad * silu)

    def partial(block):
        total = jnp.zeros((192, 1536), jnp.float32)
        for kind in range(2):
            for side in range(2):
                total = total + times_transposed(
                    dgu[kind, block, :, pl.ds(side * 512, 512)], gate_up[side, kind]
                )
        dn_part[...] = low(total)

    act_back(z, 0)
    feed(z, 0)
    act_back(before, 0)
    act_back(after, 0)
    gate_up_far = pass_on(*gate_up_plan, gate_up_moves)
    down_far = pass_on(*down_plan, down_moves)
    forward(*down_plan, down_far)
    settle(*down_plan)
    stored(down.at[1], down_out_ref)
    act_back(z, 1)
    act_back(before, 1)
    act_back(after, 1)
    forward(*gate_up_plan, gate_up_far)
    two_right.wait_recv()
    two_last = [sent(normed_two.at[before, lower], normed_two.at[before, lower], right)]
    two_left.wait_recv()
    two_last.append(sent(normed_two.at[after, upper], normed_two.at[after, upper], left))
    feed(before, 0)
    feed(after, 0)
    settle(*gate_up_plan)
    stored(gate_up.at[1], gate_up_out_ref)
    feed(z, 1)
    feed(before, 1)
    feed(after, 1)
    for copy in upstream_last:
        copy.wait_recv()
    stored(upstream, upstream_ref)
    act_back(opposite, 0)
    act_back(opposite, 1)
    for copy in two_last:
        copy.wait_recv()
    stored(normed_two, normed_two_ref)
    feed(opposite, 0)
    feed(opposite, 1)
    stored(act, act_ref)
    stored(dgu, dgu_ref)
    partial(opposite)
    stored(dn_part, dn_out_ref)
    for copy in normed_across:
        copy.wait_recv()
    for copy in copies:
        copy.wait_send()
    for step in range(1, 8):
        outgoing_copy(lax.rem(me + step, 8), step).wait_send()
    for copy in stores:
        copy.wait()


FRONT_SLOTS = 73
FRONT_LOCALS = 26


def rotation_tables():
    inverse = np.float32(THETA) ** (-np.arange(0, HEAD_SIZE, 2, dtype=np.float32) / HEAD_SIZE)
    phases = np.arange(1536, dtype=np.float32)[:, None] * inverse.astype(np.float32)[None, :]
    cosine, sine = np.zeros((1536, 128), np.float32), np.zeros((1536, 128), np.float32)
    cosine[:, 0:48] = cosine[:, 64:112] = np.cos(phases)
    sine[:, 64:112] = np.sin(phases)
    sine[:, 0:48] = -sine[:, 64:112]
    return cosine.reshape(12, BLOCK, 128), sine.reshape(12, BLOCK, 128)


def fronted(tokens, lens, gains, qkv, out_weight, gate_up, down, cotangent):
    def shape(dims, kind=jnp.bfloat16):
        return jax.ShapeDtypeStruct(dims, kind)

    def room(*dims):
        return pltpu.VMEM(dims, jnp.bfloat16)

    cosine, sine = rotation_tables()
    return pl.pallas_call(
        front_kernel,
        out_shape=(
            shape((4, 192, 1536)),
            shape((2, 192, 1536)),
            shape((1536, 512)),
            shape((1536, 384)),
            shape((8, 192, 1536)),
            shape((2, 1536, 512)),
            shape((512, 1536)),
            shape((4, 192, 1536)),
            shape((4, 192, 1536)),
            shape((4, 192, 1024)),
            shape((2, 4, 192, 1024)),
            shape((192, 1536), jnp.float32),
            shape((8, 192, 192)),
            shape((8, 384, 128)),
            shape((1536, 128)),
            shape((1536, 128)),
            shape((8, 384, 128)),
            shape((1536, 128), jnp.float32),
            shape((1536, 128), jnp.float32),
            shape((192, 1536)),
            shape((8, 1, 384), jnp.float32),
        ),
        in_specs=[IN_VMEM, pl.BlockSpec(memory_space=pltpu.SMEM), IN_VMEM] + [ANY] * 7,
        out_specs=(ANY,) * 20 + (IN_VMEM,),
        scratch_shapes=[
            room(4, 192, 1536),
            room(1536, 384),
            room(1536, 384),
            room(1536, 512),
            room(1536, 512),
            room(4, 192, 384),
            room(4, 192, 384),
            pltpu.VMEM((2, 12, BLOCK, 128), jnp.float32),
            room(8, 192, 1536),
            room(2, 2, 1536, 512),
            room(2, 512, 1536),
            room(4, 192, 1536),
            room(4, 192, 1536),
            room(4, 192, 1024),
            room(2, 4, 192, 1024),
            pltpu.VMEM((4, 2, 192, 512), jnp.float32),
            pltpu.VMEM((1536, 384), jnp.float32),
            room(8, 192, 192),
            pltpu.VMEM((192, 1536), jnp.float32),
            room(8, 192, 192),
            room(8, 384, 128),
            room(1536, 128),
            room(1536, 128),
            room(8, 384, 128),
            pltpu.VMEM((1536, 128), jnp.float32),
            pltpu.VMEM((1536, 128), jnp.float32),
            room(192, 1536),
            pltpu.SemaphoreType.DMA((FRONT_SLOTS + 8,)),
            pltpu.SemaphoreType.DMA((FRONT_SLOTS + 8,)),
            pltpu.SemaphoreType.DMA((FRONT_LOCALS + 1,)),
        ],
        compiler_params=pltpu.CompilerParams(
            collective_id=1, has_side_effects=True, vmem_limit_bytes=62 * 2**20
        ),
        name="front",
    )(
        tokens,
        lens,
        gains,
        qkv,
        out_weight,
        gate_up,
        down,
        cotangent,
        jnp.asarray(cosine),
        jnp.asarray(sine),
    )


def mid_kernel(
    dgu_ref,
    act_ref,
    normed_two_ref,
    upstream_ref,
    normed_ref,
    part_ref,
    gate_up_ref,
    gate_up_other_ref,
    down_ref,
    down_other_ref,
    out_in_ref,
    here_in_ref,
    middle_in_ref,
    cotangent_in_ref,
    gain_ref,
    dh_ref,
    landed_ref,
    out_grad_ref,
    ffn_right_ref,
    ffn_left_ref,
    ffn_own_ref,
    gate_own_ref,
    feeds_ref,
    normed_other_ref,
    dgu,
    act,
    normed,
    upstream,
    own,
    gate_up,
    down,
    turned,
    grads,
    grads_core,
    grads_a,
    grads_b,
    gate_left,
    gate_right,
    near_out,
    far_a,
    far_b,
    from_left,
    from_right,
    feeds,
    out_all,
    here,
    middle_room,
    cotangent,
    outgoing,
    landed,
    dhb,
    out_part,
    send_sem,
    recv_sem,
    local_sem,
):
    x, c = lax.axis_index("x"), lax.axis_index("c")
    z = lax.axis_index("z")
    after, before, opposite = lax.rem(z + 1, 4), lax.rem(z + 3, 4), lax.rem(z + 2, 4)
    x_after, x_before, x_far = lax.rem(x + 1, 4), lax.rem(x + 3, 4), lax.rem(x + 2, 4)
    right, left, across = {"z": after}, {"z": before}, {"yh": 1 - lax.axis_index("yh")}
    x_right, x_left, core = {"x": x_after}, {"x": x_before}, {"c": 1 - c}
    partners = [tensor_partner(step) for step in range(1, 8)] + [x_right, x_left, core]
    barrier = pltpu.get_barrier_semaphore()
    for partner in partners:
        pl.semaphore_signal(barrier, inc=1, device_id=partner, device_id_type=MESH)
    local_slots, slots = iter(range(MID_LOCALS)), iter(range(MID_SLOTS))
    stores, copies = [], []
    raw_sent = kernel_copies(send_sem, recv_sem)

    def moved(source, goal):
        copy = pltpu.make_async_copy(source, goal, local_sem.at[next(local_slots)])
        copy.start()
        return copy

    def stored(source, goal):
        stores.append(moved(source, goal))

    def sent(source, goal, device):
        copy = raw_sent(next(slots), source, goal, device)
        copies.append(copy)
        return copy

    def arrived(pair):
        for copy in pair:
            copy.wait_recv()

    dgu_load = moved(dgu_ref, dgu)
    gate_up_loads = [
        moved(gate_up_ref, gate_up.at[0]),
        moved(gate_up_other_ref, gate_up.at[1]),
    ]
    normed_load = moved(normed_two_ref, normed)
    upstream_load = moved(upstream_ref, upstream)
    act_load = moved(act_ref, act)
    down_loads = [moved(down_ref, down.at[0]), moved(down_other_ref, down.at[1])]
    middle_load = moved(middle_in_ref, middle_room)
    cotangent_load = moved(cotangent_in_ref, cotangent)
    out_load = moved(out_in_ref, out_all)
    here_load = moved(here_in_ref, here)
    pl.semaphore_wait(barrier, len(partners))

    far = [
        sent(part_ref.at[pl.ds(0, 96)], far_a, right),
        sent(part_ref.at[pl.ds(96, 96)], far_b, left),
    ]
    normed_across = [
        sent(normed_ref.at[2 + k], normed_other_ref.at[k], across) for k in range(2)
    ]

    def add_core(kind):
        cored[kind].wait_recv()
        for k in range(8):
            grads[kind, k, c] = low(wide(grads[kind, k, c]) + wide(grads_core[kind, k]))
        spot = grads.at[kind, pl.ds(x_far * 2, 2), c]
        return [
            sent(spot.at[:, :, pl.ds(0, 512)], grads_a.at[kind], x_right),
            sent(spot.at[:, :, pl.ds(512, 512)], grads_b.at[kind], x_left),
        ]

    def grad(kind, right_side):
        for side in range(2):
            cols = pl.ds(side * 512, 512)
            value = jnp.dot(turned[...], right_side(cols), preferred_element_type=jnp.float32)
            grads[kind, :, :, :, cols] = low(value).reshape(8, 2, 96, 512)
        cored.append(sent(grads.at[kind, :, 1 - c], grads_core.at[kind], core))

    cored = []

    def add_x(kind):
        arrived(round_x[kind])
        for k in range(2):
            spot = grads[kind, x_after * 2 + k, c, :, 0:512]
            grads[kind, x_after * 2 + k, c, :, 0:512] = low(wide(spot) + wide(grads_a[kind, k]))
            spot = grads[kind, x_before * 2 + k, c, :, 512:1024]
            grads[kind, x_before * 2 + k, c, :, 512:1024] = low(
                wide(spot) + wide(grads_b[kind, k])
            )

    def partial(block):
        total = jnp.zeros((192, 1536), jnp.float32)
        for kind in range(2):
            for side in range(2):
                total = total + times_transposed(
                    dgu[kind, block, :, pl.ds(side * 512, 512)], gate_up[side, kind]
                )
        return total


    dgu_load.wait()
    for load in gate_up_loads:
        load.wait()
    to_right, to_left = partial(after), partial(before)
    normed_load.wait()
    turned[...] = jnp.transpose(normed[...].reshape(768, 1536))
    grad(0, lambda cols: dgu[0, :, :, cols].reshape(768, 512))
    arrived(far)
    near_out[0, 0:96] = low(to_right[0:96] + wide(far_a[...]))
    near_out[0, 96:192] = low(to_right[96:192])
    near_out[1, 0:96] = low(to_left[0:96])
    near_out[1, 96:192] = low(to_left[96:192] + wide(far_b[...]))
    near = [
        sent(near_out.at[0], from_left, right),
        sent(near_out.at[1], from_right, left),
    ]
    grad(1, lambda cols: dgu[1, :, :, cols].reshape(768, 512))
    round_x = [add_core(0)]
    upstream_load.wait()
    act_load.wait()
    turned[...] = jnp.transpose(upstream[...].reshape(768, 1536))
    grad(2, lambda cols: act[:, :, cols].reshape(768, 512))
    round_x.append(add_core(1))

    round_x.append(add_core(2))
    stored(grads.at[pl.ds(1, 2), pl.ds(x * 2, 2), c], ffn_own_ref)
    own[...] = partial(z)
    add_x(0)
    gate_second = [
        sent(grads.at[0, pl.ds(x_after * 2, 2), c], gate_left, x_right),
        sent(grads.at[0, pl.ds(x_before * 2, 2), c], gate_right, x_left),
    ]
    middle_load.wait()
    cotangent_load.wait()
    out_load.wait()
    middle = middle_room[...]
    scale = lax.rsqrt(jnp.mean(middle * middle, axis=1, keepdims=True) + EPSILON)
    unit = middle * scale
    arrived(near)
    dn = own[...] + wide(from_left[...]) + wide(from_right[...])
    scaled = dn * gain_ref[1:2, :]
    dh = wide(cotangent[...]) + scale * (
        scaled - unit * jnp.mean(scaled * unit, axis=1, keepdims=True)
    )
    dh_ref[...] = dh
    dhb[...] = low(dh)
    do_moves = []
    for step in range(1, 8):
        outgoing[step] = low(times_transposed(dhb[...], out_all[step]))
        do_moves.append(sent(outgoing.at[step], landed.at[8 - step], tensor_partner(step)))
    landed[0] = low(times_transposed(dhb[...], out_all[0]))
    here_load.wait()
    for k in range(8):
        out_part[k] = low(transposed_times(here[k], dhb[...]))
    stored(out_part, out_grad_ref)
    for load in down_loads:
        load.wait()

    def feed(block):
        return jnp.dot(
            act[block, :, 0:512], down[0], preferred_element_type=jnp.float32
        ) + jnp.dot(act[block, :, 512:1024], down[1], preferred_element_type=jnp.float32)

    feeds[3] = low(feed(opposite))
    feeds[0], feeds[1], feeds[2] = low(feed(after)), low(feed(before)), low(feed(z))
    stored(feeds, feeds_ref)
    add_x(1)
    add_x(2)
    stored(grads.at[pl.ds(1, 2), pl.ds(x_after * 2, 2), c], ffn_right_ref)
    stored(grads.at[pl.ds(1, 2), pl.ds(x_before * 2, 2), c], ffn_left_ref)
    arrived(gate_second)
    for k in range(2):
        gate_left[k] = low(
            wide(grads[0, x * 2 + k, c]) + wide(gate_left[k]) + wide(gate_right[k])
        )
    stored(gate_left, gate_own_ref)
    arrived(do_moves)
    stored(landed, landed_ref)
    arrived(normed_across)
    for copy in copies:
        copy.wait_send()
    for copy in stores:
        copy.wait()


MID_SLOTS = 26
MID_LOCALS = 25


def middled(*arguments):
    def shape(dims, kind=jnp.bfloat16):
        return jax.ShapeDtypeStruct(dims, kind)

    def room(*dims):
        return pltpu.VMEM(dims, jnp.bfloat16)

    return pl.pallas_call(
        mid_kernel,
        out_shape=(
            shape((192, 1536), jnp.float32),
            shape((8, 192, 192)),
            shape((8, 192, 1536)),
            shape((2, 2, 96, 1024)),
            shape((2, 2, 96, 1024)),
            shape((2, 2, 96, 1024)),
            shape((2, 96, 1024)),
            shape((4, 192, 1536)),
            shape((2, 192, 1536)),
        ),
        in_specs=[ANY] * 14 + [IN_VMEM],
        out_specs=(IN_VMEM,) + (ANY,) * 8,
        scratch_shapes=[
            room(2, 4, 192, 1024),
            room(4, 192, 1024),
            room(4, 192, 1536),
            room(4, 192, 1536),
            pltpu.VMEM((192, 1536), jnp.float32),
            room(2, 2, 1536, 512),
            room(2, 512, 1536),
            room(1536, 768),
            room(3, 8, 2, 96, 1024),
            room(3, 8, 96, 1024),
            room(3, 2, 96, 512),
            room(3, 2, 96, 512),
            room(2, 96, 1024),
            room(2, 96, 1024),
            room(2, 192, 1536),
            room(96, 1536),
            room(96, 1536),
            room(192, 1536),
            room(192, 1536),
            room(4, 192, 1536),
            room(8, 192, 1536),
            room(8, 192, 192),
            pltpu.VMEM((192, 1536), jnp.float32),
            room(192, 1536),
            room(8, 192, 192),
            room(8, 192, 192),
            room(192, 1536),
            room(8, 192, 1536),
            pltpu.SemaphoreType.DMA((MID_SLOTS,)),
            pltpu.SemaphoreType.DMA((MID_SLOTS,)),
            pltpu.SemaphoreType.DMA((MID_LOCALS,)),
        ],
        compiler_params=pltpu.CompilerParams(
            collective_id=3, has_side_effects=True, vmem_limit_bytes=62 * 2**20
        ),
        name="mid",
    )(*arguments)


def back_kernel(
    gain_ref,
    lse_ref,
    lens_ref,
    dh_in_ref,
    middle_in_ref,
    grads_in_ref,
    out_in_ref,
    q_in_ref,
    k_in_ref,
    v_in_ref,
    o_in_ref,
    cos_in_ref,
    sin_in_ref,
    weight_in_ref,
    weight_other_in_ref,
    tokens_in_ref,
    normed_ref,
    normed_first_ref,
    normed_second_ref,
    ffn_right_ref,
    ffn_left_ref,
    ffn_own_ref,
    gate_own_ref,
    feeds_ref,
    gate_up_ref,
    mixed_ref,
    input_grad_ref,
    qkv_grad_ref,
    out_grad_ref,
    ffn_grad_ref,
    gains_ref,
    landed,
    dk_sum,
    dv_sum,
    dp,
    normed,
    ffn_own,
    feeds,
    feed_a,
    feed_b,
    feed_from_left,
    feed_from_right,
    ffn_from_left,
    ffn_from_right,
    ffn_out,
    ffn_in,
    out_part,
    out_core,
    out_far_a,
    out_far_b,
    out_from_left,
    out_from_right,
    out_sum,
    out_shards,
    out_swap,
    out_swap_in,
    qkv_part,
    qkv_core,
    qkv_in,
    far_out,
    near_out,
    far_a,
    far_b,
    from_left,
    from_right,
    dq_out,
    dq_in,
    dkv_out,
    dkv_in,
    gain_out,
    gain_in,
    gate_up_rows,
    dh_ref,
    middle_ref,
    q_ref,
    k_ref,
    v_ref,
    o_ref,
    cos_ref,
    sin_ref,
    weight_ref,
    weight_other_ref,
    tokens_ref,
    send_sem,
    recv_sem,
    local_sem,
):
    x, yl, c = lax.axis_index("x"), lax.axis_index("yl"), lax.axis_index("c")
    yh, z = lax.axis_index("yh"), lax.axis_index("z")
    me = yh * 4 + z
    place = (x * 2 + yl) * 2 + c
    after, before, opposite = lax.rem(z + 1, 4), lax.rem(z + 3, 4), lax.rem(z + 2, 4)
    x_after, x_before, x_far = lax.rem(x + 1, 4), lax.rem(x + 3, 4), lax.rem(x + 2, 4)
    right, left, across = {"z": after}, {"z": before}, {"yh": 1 - yh}
    x_right, x_left = {"x": x_after}, {"x": x_before}
    core, other_yl, cross = {"c": 1 - c}, {"yl": 1 - yl}, {"yl": 1 - yl, "yh": 1 - yh}
    def dp_partner(step):
        goal = lax.rem(x * 2 + yl + step, 8)
        return {"x": lax.div(goal, 2), "yl": lax.rem(goal, 2)}, goal

    partners = [tensor_partner(step) for step in range(1, 8)]
    partners += [{**tensor_partner(step), "yl": 1 - yl} for step in range(1, 8)]
    partners += [core] + [dp_partner(step)[0] for step in range(1, 8)]
    barrier = pltpu.get_barrier_semaphore()
    for partner in partners:
        pl.semaphore_signal(barrier, inc=1, device_id=partner, device_id_type=MESH)
    raw_sent = kernel_copies(send_sem, recv_sem)
    copies = []
    slots = iter(range(SLOTS))

    def sent(source, goal, device):
        copy = raw_sent(next(slots), source, goal, device)
        copies.append(copy)
        return copy

    def arrived(pair):
        for copy in pair:
            copy.wait_recv()

    local_slots = iter(range(BACK_LOCALS))

    def fetched(source, goal):
        copy = pltpu.make_async_copy(source, goal, local_sem.at[next(local_slots)])
        copy.start()
        return copy

    attend_loads = [
        fetched(source, goal)
        for source, goal in (
            (grads_in_ref, landed),
            (q_in_ref, q_ref),
            (k_in_ref, k_ref),
            (v_in_ref, v_ref),
            (o_in_ref, o_ref),
            (cos_in_ref, cos_ref),
            (sin_in_ref, sin_ref),
        )
    ]
    out_load = fetched(out_in_ref.at[:, lines(c * 96, 96), :], out_part)
    weight_load = fetched(weight_in_ref, weight_ref)
    weight_other_load = fetched(weight_other_in_ref, weight_other_ref)
    normed_loads = [
        fetched(normed_ref, normed.at[lines(yh * 768, 768), :]),
        fetched(normed_first_ref, normed.at[lines((1 - yh) * 768, 384), :]),
        fetched(normed_second_ref, normed.at[lines((1 - yh) * 768 + 384, 384), :]),
    ]
    ffn_loads = [
        fetched(gate_own_ref, ffn_own.at[0]),
        fetched(ffn_own_ref, ffn_own.at[pl.ds(1, 2)]),
    ]
    feed_load = fetched(feeds_ref.at[pl.ds(0, 3)], feeds)
    tokens_load = fetched(tokens_in_ref, tokens_ref)
    middle_load = fetched(middle_in_ref, middle_ref)
    dh_load = fetched(dh_in_ref, dh_ref)
    rows_load = fetched(gate_up_ref.at[:, lines(place * 96, 96), :], gate_up_rows)

    pl.semaphore_wait(barrier, len(partners))
    out_cored = sent(out_in_ref.at[:, lines((1 - c) * 96, 96), :], out_core, core)
    ffn_second = [
        sent(ffn_right_ref, ffn_from_left, x_right),
        sent(ffn_left_ref, ffn_from_right, x_left),
    ]
    feed_far = [
        sent(feeds_ref.at[3, pl.ds(0, 96)], feed_a, right),
        sent(feeds_ref.at[3, pl.ds(96, 96)], feed_b, left),
    ]
    starts, ends = sequences(lens_ref)
    dk_sum[...] = jnp.zeros_like(dk_sum)
    dv_sum[...] = jnp.zeros_like(dv_sum)

    def unturned(values, rows):
        return values * cos_ref[rows, :] - pltpu.roll(values, 64, 1) * sin_ref[rows, :]

    dq_slot = [next(slots) for _ in range(4)][0]

    def dq_copy(block):
        return pltpu.make_async_remote_copy(
            src_ref=dq_out.at[block % 4],
            dst_ref=dq_in.at[block % 4],
            send_sem=send_sem.at[dq_slot + block % 4],
            recv_sem=recv_sem.at[dq_slot + block % 4],
            device_id=across,
            device_id_type=MESH,
        )

    def back(block):
        step = lax.rem(block - me + 8, 8)
        grads = landed[step]
        grad_block = jnp.concatenate([spread(grads[:, 0:96]), spread(grads[:, 96:192])], axis=0)
        query_block = q_ref[block]
        queries, first_row = block_queries(block, starts, ends)
        lse = lse_ref[block]
        centered = wide(grad_block) * wide(o_ref[block])
        centered = jnp.sum(jnp.transpose(centered), axis=0, keepdims=True)
        dq = jnp.zeros((384, 128), jnp.float32)
        for j in range((192 * (block + 1) + KEYS - 1) // KEYS):
            rows = pl.ds(j * KEYS, KEYS)
            key_block, value_block = k_ref[rows, :], v_ref[rows, :]
            scores, allowed = static_score(
                key_block, query_block, first_row, j * KEYS, queries, block * 192
            )
            weights = jnp.where(allowed, jnp.exp(scores - lse), 0.0)
            grad_weights = times_transposed(value_block, grad_block)
            grad_scores = low(weights * (grad_weights - centered))
            dv_sum[rows, :] += jnp.dot(
                low(weights), grad_block, preferred_element_type=jnp.float32
            )
            dk_sum[rows, :] += jnp.dot(
                grad_scores, query_block, preferred_element_type=jnp.float32
            )
            dq = dq + transposed_times(grad_scores, key_block)
        dq = dq * (HEAD_SIZE ** (-0.5))
        rows = pl.ds(block * 192, 192)
        first, second = unturned(dq[0:192], rows), unturned(dq[192:384], rows)
        dp[rows, 0:128] = low(first)
        dp[rows, 128:256] = low(second)

        @pl.when(yh != block // 4)
        def _():
            dq_out[block % 4] = low(jnp.concatenate([packed(first), packed(second)], axis=1))
            dq_copy(block).start()

    for load in attend_loads:
        load.wait()
    for block in range(4):
        back(block)
    out_load.wait()
    out_cored.wait_recv()
    for k in range(8):
        out_part[k] = low(wide(out_part[k]) + wide(out_core[k]))
    out_first = [
        sent(out_part.at[pl.ds(0, 4), :, columns(x_far * 384, 384)], out_far_a, x_right),
        sent(out_part.at[pl.ds(4, 4), :, columns(x_far * 384, 384)], out_far_b, x_left),
    ]
    for block in range(4, 6):
        back(block)
    arrived(feed_far)
    feed_load.wait()
    feeds[0, 0:96] = low(wide(feeds[0, 0:96]) + wide(feed_a[...]))
    feeds[1, 96:192] = low(wide(feeds[1, 96:192]) + wide(feed_b[...]))
    feed_second = [
        sent(feeds.at[0], feed_from_left, right),
        sent(feeds.at[1], feed_from_right, left),
    ]
    back(6)
    back(7)
    for block in range(8):
        rows = pl.ds(block * 192, 192)
        dp[rows, 256:384] = low(unturned(dk_sum[rows, :] * (HEAD_SIZE ** (-0.5)), rows))
        dp[rows, 384:512] = low(dv_sum[rows, :])

    mine = yh * 768
    for k in range(4):
        rows = lines((1 - yh) * 768 + k * 192, 192)
        dkv_out[k] = jnp.concatenate(
            [packed(dp[rows, 256:384]), packed(dp[rows, 384:512])], axis=1
        )
    exchanged = sent(dkv_out, dkv_in, across)
    for load in normed_loads:
        load.wait()
    for part in range(4):
        features = pl.ds(part * 384, 384)
        grad = transposed_times(normed[:, features], dp[...])
        qkv_part[part * 2 : part * 2 + 2] = low(grad).reshape(2, 2, 96, 512)
    qkv_cored = sent(qkv_part.at[:, 1 - c], qkv_core, core)
    arrived(ffn_second)
    for load in ffn_loads:
        load.wait()
    for kind in range(2):
        ffn_own[kind + 1] = low(
            wide(ffn_own[kind + 1]) + wide(ffn_from_left[kind]) + wide(ffn_from_right[kind])
        )
    ffn_sum = wide(ffn_own[...])
    flipped = jnp.where(yl == 0, ffn_sum[:, 1], ffn_sum[:, 0])
    kept = jnp.where(yl == 0, ffn_sum[:, 0], ffn_sum[:, 1])
    ffn_out[0] = low(flipped[..., 0:512])
    ffn_out[1] = low(flipped[..., 512:1024])
    ffn_out[2] = low(kept[..., 512:1024])
    ffn_moves = [
        sent(ffn_out.at[k], ffn_in.at[k], device)
        for k, device in enumerate((other_yl, cross, across))
    ]
    ffn_grad_ref[...] = kept[..., 0:512]
    out_cols = [columns(place_x * 384, 384) for place_x in (x_after, x_before)]
    arrived(out_first)
    for k in range(4):
        out_part[k, :, out_cols[0]] = low(wide(out_part[k, :, out_cols[0]]) + wide(out_far_a[k]))
        out_part[4 + k, :, out_cols[1]] = low(
            wide(out_part[4 + k, :, out_cols[1]]) + wide(out_far_b[k])
        )
    out_second = [
        sent(out_part.at[:, :, out_cols[0]], out_from_left, x_right),
        sent(out_part.at[:, :, out_cols[1]], out_from_right, x_left),
    ]
    qkv_cored.wait_recv()
    for k in range(8):
        qkv_part[k, c] = low(wide(qkv_part[k, c]) + wide(qkv_core[k]))
    qkv_moves = [
        sent(qkv_part.at[goal, c], qkv_in.at[step - 1], device)
        for step, (device, goal) in ((step, dp_partner(step)) for step in range(1, 8))
    ]
    for k in range(4):
        dq_copy(k).wait_recv()
    exchanged.wait_recv()
    weight_load.wait()
    weight_other_load.wait()

    def partial(block_z):
        theirs = jnp.concatenate([dq_in[block_z], dkv_in[block_z]], axis=1)
        return times_transposed(
            dp[lines(mine + block_z * 192, 192), :], weight_ref[...]
        ) + times_transposed(theirs, weight_other_ref[...])

    far_out[...] = low(partial(opposite))
    far = [
        sent(far_out.at[pl.ds(0, 96)], far_a, right),
        sent(far_out.at[pl.ds(96, 96)], far_b, left),
    ]
    to_right, to_left = partial(after), partial(before)
    arrived(far)
    near_out[0, 0:96] = low(to_right[0:96] + wide(far_a[...]))
    near_out[0, 96:192] = low(to_right[96:192])
    near_out[1, 0:96] = low(to_left[0:96])
    near_out[1, 96:192] = low(to_left[96:192] + wide(far_b[...]))
    near = [
        sent(near_out.at[0], from_left, right),
        sent(near_out.at[1], from_right, left),
    ]
    own = partial(z)
    arrived(out_second)
    own_cols = columns(x * 384, 384)
    for k in range(8):
        total = wide(out_part[k, :, own_cols]) + wide(out_from_left[k]) + wide(out_from_right[k])
        out_sum[k, 0] = low(total[:, 0:192])
        out_sum[k, 1] = low(total[:, 192:384])
    out_moves = []
    for step in range(8):
        place_yh = tensor_partner(step)
        for side in range(2):
            if step + side > 0:
                goal_yl = yl if side == 0 else 1 - yl
                out_moves.append(
                    sent(
                        out_sum.at[step, goal_yl],
                        out_shards.at[step * 2 + side - 1],
                        {**place_yh, "yl": goal_yl},
                    )
                )
    arrived(feed_second)
    middle_load.wait()
    mixed_ref[...] = low(
        middle_ref[...] + wide(feeds[2]) + wide(feed_from_left[...]) + wide(feed_from_right[...])
    )
    arrived(qkv_moves)
    qkv_final = wide(qkv_part[x * 2 + yl, c])
    for k in range(7):
        qkv_final = qkv_final + wide(qkv_in[k])
    qkv_grad_ref[...] = qkv_final
    arrived(ffn_moves)
    ffn_final = ffn_grad_ref[...]
    for k in range(3):
        ffn_final = ffn_final + wide(ffn_in[k])
    ffn_grad_ref[...] = ffn_final
    rows_load.wait()
    gain_one = jnp.sum(
        qkv_final * wide(weight_ref[lines(place * 96, 96), :]), axis=1, keepdims=True
    )
    gain_two = jnp.sum(
        ffn_final[0] * wide(gate_up_rows[0]) + ffn_final[1] * wide(gate_up_rows[1]),
        axis=1,
        keepdims=True,
    )
    lanes = lax.broadcasted_iota(jnp.int32, (96, 128), 1)
    gain_out[...] = jnp.where(lanes == 0, gain_one, jnp.where(lanes == 1, gain_two, 0.0))
    gain_shared = [
        sent(gain_out, gain_in.at[step - 1], tensor_partner(step)) for step in range(1, 8)
    ]
    arrived(out_moves)
    out_final = wide(out_sum[0, yl])
    for k in range(15):
        out_final = out_final + wide(out_shards[k])
    out_swap[...] = low(jnp.where(c == 0, out_final[:, 96:192], out_final[:, 0:96]))
    out_swapped = sent(out_swap, out_swap_in, core)
    out_mine = jnp.where(c == 0, out_final[:, 0:96], out_final[:, 96:192])
    out_grad_ref[lines(c * 96, 96), :] = out_mine
    arrived(near)
    dn = own + wide(from_left[...]) + wide(from_right[...])
    tokens_load.wait()
    hidden = wide(tokens_ref[...])
    scale = lax.rsqrt(jnp.mean(hidden * hidden, axis=1, keepdims=True) + EPSILON)
    unit = hidden * scale
    scaled = dn * gain_ref[0:1, :]
    dh_load.wait()
    input_grad_ref[...] = dh_ref[...] + scale * (
        scaled - unit * jnp.mean(scaled * unit, axis=1, keepdims=True)
    )
    out_swapped.wait_recv()
    out_grad_ref[lines((1 - c) * 96, 96), :] = wide(out_swap_in[...])
    arrived(gain_shared)
    total = gain_out[...]
    for k in range(7):
        total = total + gain_in[k]
    gains_ref[...] = total
    for copy in copies:
        copy.wait_send()
    for k in range(4):
        dq_copy(k).wait_send()


SLOTS = 72
BACK_LOCALS = 23


def finished_back(*arguments):
    def shape(dims, kind=jnp.float32):
        return jax.ShapeDtypeStruct(dims, kind)

    def room(*dims):
        return pltpu.VMEM(dims, jnp.bfloat16)

    return pl.pallas_call(
        back_kernel,
        out_shape=(
            shape((192, 1536), jnp.bfloat16),
            shape((192, 1536)),
            shape((96, 512)),
            shape((192, 96)),
            shape((3, 96, 512)),
            shape((96, 128)),
        ),
        in_specs=[IN_VMEM] * 2 + [pl.BlockSpec(memory_space=pltpu.SMEM)] + [ANY] * 22,
        out_specs=(IN_VMEM,) * 6,
        scratch_shapes=[
            room(8, 192, 192),
            pltpu.VMEM((1536, 128), jnp.float32),
            pltpu.VMEM((1536, 128), jnp.float32),
            room(1536, 512),
            room(1536, 1536),
            room(3, 2, 96, 1024),
            room(3, 192, 1536),
            room(96, 1536),
            room(96, 1536),
            room(192, 1536),
            room(192, 1536),
            room(2, 2, 96, 1024),
            room(2, 2, 96, 1024),
            room(3, 3, 96, 512),
            room(3, 3, 96, 512),
            room(8, 96, 1536),
            room(8, 96, 1536),
            room(4, 96, 384),
            room(4, 96, 384),
            room(8, 96, 384),
            room(8, 96, 384),
            room(8, 2, 96, 192),
            room(15, 96, 192),
            room(96, 96),
            room(96, 96),
            room(8, 2, 96, 512),
            room(8, 96, 512),
            room(7, 96, 512),
            room(192, 1536),
            room(2, 192, 1536),
            room(96, 1536),
            room(96, 1536),
            room(192, 1536),
            room(192, 1536),
            room(4, 192, 192),
            room(4, 192, 192),
            room(4, 192, 192),
            room(4, 192, 192),
            pltpu.VMEM((96, 128), jnp.float32),
            pltpu.VMEM((7, 96, 128), jnp.float32),
            room(2, 96, 512),
            pltpu.VMEM((192, 1536), jnp.float32),
            pltpu.VMEM((192, 1536), jnp.float32),
            room(8, 384, 128),
            room(1536, 128),
            room(1536, 128),
            room(8, 384, 128),
            pltpu.VMEM((1536, 128), jnp.float32),
            pltpu.VMEM((1536, 128), jnp.float32),
            room(1536, 512),
            room(1536, 384),
            room(192, 1536),
            pltpu.SemaphoreType.DMA((SLOTS,)),
            pltpu.SemaphoreType.DMA((SLOTS,)),
            pltpu.SemaphoreType.DMA((BACK_LOCALS,)),
        ],
        compiler_params=pltpu.CompilerParams(
            collective_id=2, has_side_effects=True, vmem_limit_bytes=63 * 2**20
        ),
        name="back",
    )(*arguments)


def finish_kernel(
    mixed_in,
    input_in,
    qkv_in,
    out_in,
    ffn_in,
    gains_in,
    gain_ref,
    mixed_ref,
    input_ref,
    qkv_ref,
    out_ref,
    gate_up_ref,
    down_ref,
    gains_ref,
    mixed_room,
    input_room,
    ffn_room,
    out_room,
    qkv_room,
    gains_room,
    gain_room,
    qkv_out,
    gains_out,
    sem,
):
    sources = (qkv_in, gains_in, gain_ref, input_in, ffn_in, mixed_in, out_in)
    rooms = (qkv_room, gains_room, gain_room, input_room, ffn_room, mixed_room, out_room)
    arriving, copies = [], []
    for k, (source, room) in enumerate(zip(sources, rooms)):
        arriving.append(pltpu.make_async_copy(source, room, sem.at[k]))
        arriving[-1].start()

    def leave(source, goal):
        copies.append(pltpu.make_async_copy(source, goal, sem.at[7 + len(copies)]))
        copies[-1].start()

    for arrival in arriving[0:3]:
        arrival.wait()
    qkv_out[...] = jnp.concatenate(
        [packed(qkv_room[:, head * 128 : head * 128 + 128]) for head in range(4)], axis=1
    )
    leave(qkv_out, qkv_ref)
    place = (lax.axis_index("x") * 2 + lax.axis_index("yl")) * 2 + lax.axis_index("c")
    gains = jnp.transpose(gains_room[...])[0:2]
    rows = jnp.zeros((2, 96), jnp.float32)
    for k in range(16):
        rows = jnp.where(place == k, gain_room[:, k * 96 : k * 96 + 96], rows)
    gains_out[...] = gains / rows
    leave(gains_out, gains_ref)
    arriving[3].wait()
    leave(input_room, input_ref)
    arriving[4].wait()
    leave(ffn_room.at[pl.ds(0, 2)], gate_up_ref)
    leave(ffn_room.at[2], down_ref)
    arriving[5].wait()
    leave(mixed_room, mixed_ref)
    arriving[6].wait()
    leave(out_room, out_ref)
    for copy in copies:
        copy.wait()


def finished(*arguments):
    def shape(*dims):
        return jax.ShapeDtypeStruct(dims, jnp.float32)

    return pl.pallas_call(
        finish_kernel,
        out_shape=(
            jax.ShapeDtypeStruct((192, 1536), jnp.bfloat16),
            shape(192, 1536),
            shape(96, 384),
            shape(192, 96),
            shape(2, 96, 512),
            shape(96, 512),
            shape(2, 96),
        ),
        in_specs=[ANY] * 7,
        out_specs=(ANY,) * 7,
        scratch_shapes=[
            pltpu.VMEM((192, 1536), jnp.bfloat16),
            pltpu.VMEM((192, 1536), jnp.float32),
            pltpu.VMEM((3, 96, 512), jnp.float32),
            pltpu.VMEM((192, 96), jnp.float32),
            pltpu.VMEM((96, 512), jnp.float32),
            pltpu.VMEM((96, 128), jnp.float32),
            pltpu.VMEM((2, 1536), jnp.float32),
            pltpu.VMEM((96, 384), jnp.float32),
            pltpu.VMEM((2, 96), jnp.float32),
            pltpu.SemaphoreType.DMA((14,)),
        ],
        compiler_params=pltpu.CompilerParams(vmem_limit_bytes=63 * 2**20),
        name="finish",
    )(*arguments)


def per_device(
    tokens,
    seq_lens,
    query_key_value_weight,
    out_weight,
    gate_up_weight,
    down_weight,
    norm_gains,
    cotangent,
):
    (
        normed_half,
        normed_first,
        weight_wide,
        weight_other,
        out_all,
        gate_up_other,
        down_other,
        upstream_all,
        normed_two_all,
        activated,
        grad_gate_up,
        middle,
        attended_here,
        queries,
        keys_all,
        values_all,
        heads,
        cos_part,
        sin_part,
        dn_part,
        log_sums,
    ) = fronted(
        tokens,
        seq_lens,
        norm_gains,
        query_key_value_weight,
        out_weight,
        gate_up_weight,
        down_weight,
        cotangent,
    )
    (
        grad_middle,
        grad_heads,
        out_half,
        ffn_right,
        ffn_left,
        ffn_own,
        gate_own,
        feeds,
        normed_second,
    ) = middled(
        grad_gate_up,
        activated,
        normed_two_all,
        upstream_all,
        normed_half,
        dn_part,
        gate_up_weight,
        gate_up_other,
        down_weight,
        down_other,
        out_all,
        attended_here,
        middle,
        cotangent,
        norm_gains,
    )
    mixed, input_grad, qkv_grad, out_grad, ffn_grad, gains_grad = finished_back(
        norm_gains,
        log_sums,
        seq_lens,
        grad_middle,
        middle,
        grad_heads,
        out_half,
        queries,
        keys_all,
        values_all,
        heads,
        cos_part,
        sin_part,
        weight_wide,
        weight_other,
        tokens,
        normed_half.reshape(768, 1536),
        normed_first.reshape(384, 1536),
        normed_second.reshape(384, 1536),
        ffn_right,
        ffn_left,
        ffn_own,
        gate_own,
        feeds,
        gate_up_weight,
    )
    mixed, input_grad, qkv_grad, out_grad, gate_up_grad, down_grad, gains_grad = finished(
        mixed, input_grad, qkv_grad, out_grad, ffn_grad, gains_grad, norm_gains
    )
    return mixed, input_grad, qkv_grad, out_grad, gate_up_grad, down_grad.T, gains_grad


def solution(mesh):
    split = Mesh(mesh.devices.reshape(4, 2, 2, 2, 4), ALL)
    placed = (
        P(ALL, None),
        P(DP, None),
        P(None, TENSOR),
        P(TENSOR, None),
        P(None, None, TENSOR),
        P(TENSOR, None),
        P(),
        P(ALL, None),
    )
    return jax.shard_map(
        per_device,
        mesh=split,
        in_specs=placed,
        out_specs=(
            P(ALL, None),
            P(ALL, None),
            P(DP, TENSOR),
            P(TENSOR, DP),
            P(None, DP, TENSOR),
            P(TENSOR, DP),
            P(None, DP),
        ),
        check_vma=False,
    )
```

```python
import functools

import jax
import jax.numpy as jnp
import numpy as np
from jax import lax
from jax.experimental import pallas as pl
from jax.experimental.pallas import tpu as pltpu
from jax.sharding import Mesh
from jax.sharding import PartitionSpec as P

HEAD_SIZE = 96
BLOCK = 128
DP = ("x", "yl", "c")
TENSOR = ("yh", "z")
ALL = DP + TENSOR
MESH = pl.DeviceIdType.MESH

EPSILON = 1e-05
THETA = 100000.0
masked_score = -1e30


def times_transposed(left, right):
    return lax.dot_general(
        left, right, (((1,), (1,)), ((), ())), preferred_element_type=jnp.float32
    )


def transposed_times(left, right):
    return lax.dot_general(
        left, right, (((0,), (0,)), ((), ())), preferred_element_type=jnp.float32
    )


def barrier_with(partners):
    barrier = pltpu.get_barrier_semaphore()
    for partner in partners:
        pl.semaphore_signal(barrier, inc=1, device_id=partner, device_id_type=MESH)
    pl.semaphore_wait(barrier, len(partners))


def kernel_copies(send_sem, recv_sem):
    def sent(slot, source, goal, device):
        copy = pltpu.make_async_remote_copy(
            src_ref=source,
            dst_ref=goal,
            send_sem=send_sem.at[slot],
            recv_sem=recv_sem.at[slot],
            device_id=device,
            device_id_type=MESH,
        )
        copy.start()
        return copy

    return sent


def tensor_partner(step):
    goal = lax.rem(lax.axis_index("yh") * 4 + lax.axis_index("z") + step, 8)
    return {"yh": lax.div(goal, 4), "z": lax.rem(goal, 4)}


def spread(values):
    gap = jnp.zeros((values.shape[0], 16), values.dtype)
    return jnp.concatenate([values[:, :48], gap, values[:, 48:], gap], axis=1)


def packed(values):
    return jnp.concatenate([values[:, :48], values[:, 64:112]], axis=1)


KEYS = 256


ANY = pl.BlockSpec(memory_space=pl.ANY)
IN_VMEM = pl.BlockSpec(memory_space=pltpu.VMEM)


def static_score(key_block, query_block, first_row, key_start, queries, query_start):
    scores = times_transposed(key_block, query_block) * (HEAD_SIZE ** (-0.5))
    keys = key_start + lax.broadcasted_iota(jnp.int32, scores.shape, 0)
    allowed = keys >= first_row
    if key_start + scores.shape[0] > query_start:
        allowed = allowed & (keys <= queries)
    return scores, allowed


def block_queries(block, starts, ends):
    queries = lax.broadcasted_iota(jnp.int32, (1, 384), 1)
    queries = block * 192 + jnp.where(queries >= 192, queries - 192, queries)
    first_row = queries
    for slot in range(4):
        within = (starts[slot] <= queries) & (queries < ends[slot])
        first_row = jnp.where(within, starts[slot], first_row)
    return queries, first_row


def sequences(lens_ref):
    starts, ends = [], []
    start = jnp.int32(0)
    for slot in range(4):
        length = lens_ref[0, slot]
        starts.append(start)
        ends.append(start + length)
        start = start + lax.div(length + (BLOCK - 1), BLOCK) * BLOCK
    return starts, ends


def columns(start, size):
    return pl.ds(pl.multiple_of(start, 128), size)


def lines(start, size):
    return pl.ds(pl.multiple_of(start, 16), size)


def wide(value):
    return value.astype(jnp.float32)


def low(value):
    return value.astype(jnp.bfloat16)


def front_kernel(
    tokens_ref,
    lens_ref,
    gain_ref,
    qkv_ref,
    out_weight_ref,
    gate_up_ref,
    down_ref,
    cotangent_ref,
    cos_table_ref,
    sin_table_ref,
    normed_ref,
    normed_other_ref,
    weight_out_ref,
    weight_other_out_ref,
    out_out_ref,
    gate_up_out_ref,
    down_out_ref,
    upstream_ref,
    normed_two_ref,
    act_ref,
    dgu_ref,
    middle_out_ref,
    here_out_ref,
    q_out_ref,
    k_out_ref,
    v_out_ref,
    o_out_ref,
    cos_out_ref,
    sin_out_ref,
    dn_out_ref,
    lse_ref,
    landed,
    raw,
    raw_other,
    weight,
    weight_other,
    projected_out,
    projected_in,
    tables,
    out_all,
    gate_up,
    down,
    upstream,
    normed_two,
    act,
    dgu,
    dact,
    scores,
    outgoing,
    middle_ref,
    here_ref,
    q_ref,
    k_ref,
    v_ref,
    o_ref,
    cos_ref,
    sin_ref,
    dn_part,
    send_sem,
    recv_sem,
    local_sem,
):
    x, yl, c = lax.axis_index("x"), lax.axis_index("yl"), lax.axis_index("c")
    yh, z = lax.axis_index("yh"), lax.axis_index("z")
    me = yh * 4 + z
    after, before, opposite = lax.rem(z + 1, 4), lax.rem(z + 3, 4), lax.rem(z + 2, 4)
    other = 1 - yh
    right, left, across = {"z": after}, {"z": before}, {"yh": other}
    x_after, x_before, x_far = lax.rem(x + 1, 4), lax.rem(x + 3, 4), lax.rem(x + 2, 4)
    x_right, x_left, core = {"x": x_after}, {"x": x_before}, {"c": 1 - c}

    def crossed(step):
        place = tensor_partner(step)
        return {**place, "yl": lax.rem(yl + yh + place["yh"], 2)}

    tensor_partners = [tensor_partner(step) for step in range(1, 8)]
    cross_partners = [{"yl": 1 - yl, "yh": other, "z": lax.rem(z + k, 4)} for k in range(4)]
    partners = tensor_partners + cross_partners + [x_right, x_left, core]
    barrier = pltpu.get_barrier_semaphore()
    for partner in partners:
        pl.semaphore_signal(barrier, inc=1, device_id=partner, device_id_type=MESH)

    stores = []
    local_slots = iter(range(FRONT_LOCALS))

    def moved(source, goal):
        copy = pltpu.make_async_copy(source, goal, local_sem.at[next(local_slots)])
        copy.start()
        return copy

    def stored(source, goal):
        stores.append(moved(source, goal))

    qkv_load = moved(qkv_ref, raw)
    cos_load = moved(cos_table_ref, tables.at[0])
    sin_load = moved(sin_table_ref, tables.at[1])
    hidden = wide(tokens_ref[...])
    scale = lax.rsqrt(jnp.mean(hidden * hidden, axis=1, keepdims=True) + EPSILON)
    landed[z] = low(hidden * scale * gain_ref[0:1, :])
    pl.semaphore_wait(barrier, len(partners))

    raw_sent = kernel_copies(send_sem, recv_sem)
    copies = []
    slots = iter(range(FRONT_SLOTS))

    def sent(source, goal, device):
        copy = raw_sent(next(slots), source, goal, device)
        copies.append(copy)
        return copy

    lower, upper = pl.ds(0, 96), pl.ds(96, 96)

    def shard(block_z, rows, device):
        spot = landed.at[block_z, rows]
        return sent(spot, spot, device)

    def qkv_part(quarter, half, part=pl.ds(0, 192)):
        return raw_other.at[lines(quarter * 384 + half * 192 + part.start, part.size), :]

    def gate_up_part(quarter, half, part=pl.ds(0, 2)):
        rows = lines(quarter * 384, 384)
        return gate_up.at[1, part, rows, columns(half * 256, 256)]

    def down_part(quarter, half, part=pl.ds(0, 128)):
        rows = lines(quarter * 128 + part.start, part.size)
        return down.at[1, rows, columns(half * 768, 768)]

    def out_part(quarter, half, part=pl.ds(1, 7)):
        return out_all.at[part, lines(quarter * 48, 48), columns(half * 768, 768)]

    to_right = [shard(z, lower, right), shard(z, upper, right)]
    to_left = [shard(z, upper, left), shard(z, lower, left)]
    qkv_cross = sent(
        qkv_ref.at[lines(x * 384 + c * 192, 192), :], qkv_part(x, c), crossed(4)
    )
    out_cross = []
    piece = out_weight_ref.at[lines(x * 48, 48), columns(c * 768, 768)]
    for step in range(1, 8):
        goal = out_all.at[8 - step, lines(x * 48, 48), columns(c * 768, 768)]
        out_cross.append(sent(piece, goal, crossed(step)))
    gate_up_cross = sent(
        gate_up_ref.at[:, lines(x * 384, 384), columns(c * 256, 256)],
        gate_up_part(x, c),
        crossed(4),
    )
    down_cross = sent(
        down_ref.at[lines(x * 128, 128), columns(c * 768, 768)], down_part(x, c), crossed(4)
    )
    upstream_load = moved(cotangent_ref, upstream.at[z])
    out_load = moved(out_weight_ref, out_all.at[0])
    gate_up_load = moved(gate_up_ref, gate_up.at[0])
    down_load = moved(down_ref, down.at[0])

    starts, ends = sequences(lens_ref)
    cos_load.wait()
    sin_load.wait()
    for block in range(12):
        begin, end = jnp.int32(0), jnp.int32(0)
        for slot in range(4):
            within = (starts[slot] <= block * BLOCK) & (block * BLOCK < ends[slot])
            begin = jnp.where(within, starts[slot], begin)
            end = jnp.where(within, ends[slot], end)
        used = block - lax.div(begin, BLOCK)
        rows = pl.ds(block * BLOCK, BLOCK)
        token = block * BLOCK + lax.broadcasted_iota(jnp.int32, (BLOCK, 128), 0)
        cos_ref[rows, :] = jnp.where(token < end, tables[0, used], tables[0, block])
        sin_ref[rows, :] = jnp.where(token < end, tables[1, used], tables[1, block])
    qkv_load.wait()
    for head in range(4):
        weight[:, head * 128 : head * 128 + 128] = spread(raw[:, head * 96 : head * 96 + 96])
    stored(weight, weight_out_ref)
    stored(cos_ref, cos_out_ref)
    stored(sin_ref, sin_out_ref)

    def projected(block_z, weights):
        values = jnp.dot(landed[block_z], weights[...], preferred_element_type=jnp.float32)
        rows = lines((yh * 4 + block_z) * 192, 192)
        cos_part, sin_part = cos_ref[rows, :], sin_ref[rows, :]
        heads = [values[:, head * 128 : head * 128 + 128] for head in range(4)]
        for head in range(3):
            heads[head] = heads[head] * cos_part + pltpu.roll(heads[head], 64, 1) * sin_part
        return heads

    def kept(block, heads):
        rows = lines(block * 192, 192)
        q_ref[block, 0:192, :] = heads[0]
        q_ref[block, 192:384, :] = heads[1]
        k_ref[rows, :] = heads[2]
        v_ref[rows, :] = heads[3]

    def project_own(block_z):
        kept(yh * 4 + block_z, [low(head) for head in projected(block_z, weight)])

    exchanged = []

    def project_other(k, block_z):
        heads = [packed(head) for head in projected(block_z, weight_other)]
        projected_out[k] = low(jnp.concatenate(heads, axis=1))
        exchanged.append(sent(projected_out.at[k], projected_in.at[block_z], across))

    def spread_out(part, halves, awaited):
        goal = part(x, c)
        awaited.append(sent(goal, goal, core))
        return [sent(goal, goal, x_right), sent(goal, goal, x_left)]

    def pass_on(part, halves, awaited, arriving):
        arriving[0].wait_recv()
        first, second = part(x_before, c), part(x_before, c, halves[0])
        far = [sent(second, second, x_right)]
        awaited.append(sent(first, first, core))
        arriving[1].wait_recv()
        first, second = part(x_after, c), part(x_after, c, halves[1])
        far.append(sent(second, second, x_left))
        awaited.append(sent(first, first, core))
        return far

    def forward(part, halves, awaited, far):
        for k in range(2):
            far[k].wait_recv()
            goal = part(x_far, c, halves[k])
            awaited.append(sent(goal, goal, core))

    def settle(part, halves, awaited):
        for copy in awaited:
            copy.wait_recv()

    gate_up_plan = (gate_up_part, (pl.ds(0, 1), pl.ds(1, 1)), [])
    down_plan = (down_part, (pl.ds(0, 64), pl.ds(64, 64)), [])
    out_plan = (out_part, (pl.ds(1, 4), pl.ds(5, 3)), [])
    qkv_plan = (qkv_part, (pl.ds(0, 96), pl.ds(96, 96)), [])

    project_own(z)
    qkv_cross.wait_recv()
    qkv_moves = spread_out(*qkv_plan)
    qkv_far = pass_on(*qkv_plan, qkv_moves)
    to_right[0].wait_recv()
    last_right = shard(before, lower, right)
    to_left[0].wait_recv()
    last_left = shard(after, upper, left)
    forward(*qkv_plan, qkv_far)
    settle(*qkv_plan)
    for head in range(4):
        weight_other[:, head * 128 : head * 128 + 128] = spread(
            raw_other[:, head * 96 : head * 96 + 96]
        )
    stored(raw_other, weight_other_out_ref)
    to_right[1].wait_recv()
    to_left[1].wait_recv()
    project_other(0, z)
    project_other(1, before)
    project_other(2, after)
    project_own(before)
    project_own(after)
    for copy in out_cross:
        copy.wait_recv()
    out_moves = spread_out(*out_plan)
    last_right.wait_recv()
    last_left.wait_recv()
    project_other(3, opposite)
    project_own(opposite)
    upstream_load.wait()
    upstream_right = sent(upstream.at[z], upstream.at[z], right)
    upstream_left = sent(upstream.at[z], upstream.at[z], left)
    stored(landed, normed_ref)
    for copy in exchanged:
        copy.wait_recv()
    for block_z in range(4):
        arrived = projected_in[block_z]
        kept(
            other * 4 + block_z,
            [spread(arrived[:, head * 96 : head * 96 + 96]) for head in range(4)],
        )
    out_far = pass_on(*out_plan, out_moves)
    down_cross.wait_recv()
    down_moves = spread_out(*down_plan)
    gate_up_cross.wait_recv()
    gate_up_moves = spread_out(*gate_up_plan)
    stored(q_ref, q_out_ref)
    stored(k_ref, k_out_ref)
    stored(v_ref, v_out_ref)

    def outgoing_copy(block, step):
        return pltpu.make_async_remote_copy(
            src_ref=outgoing.at[block],
            dst_ref=here_ref.at[8 - step],
            send_sem=send_sem.at[FRONT_SLOTS + step],
            recv_sem=recv_sem.at[FRONT_SLOTS + step],
            device_id={"yh": lax.div(block, 4), "z": lax.rem(block, 4)},
            device_id_type=MESH,
        )

    here_sem = local_sem.at[FRONT_LOCALS]

    def attend(block):
        query_block = q_ref[block]
        queries, first_row = block_queries(block, starts, ends)
        count = (192 * (block + 1) + KEYS - 1) // KEYS
        peak = jnp.full((8, 384), masked_score, jnp.float32)
        for j in range(count):
            rows = pl.ds(j * KEYS, KEYS)
            part, allowed = static_score(
                k_ref[rows, :], query_block, first_row, j * KEYS, queries, block * 192
            )
            part = jnp.where(allowed, part, masked_score)
            scores[rows, :] = part
            peak = jnp.maximum(peak, jnp.max(part.reshape(KEYS // 8, 8, 384), axis=0))
        peak = jnp.max(peak, axis=0, keepdims=True)
        total = jnp.zeros((8, 384), jnp.float32)
        out = jnp.zeros((384, 128), jnp.float32)
        for j in range(count):
            rows = pl.ds(j * KEYS, KEYS)
            weights = jnp.exp(scores[rows, :] - peak)
            total = total + jnp.sum(weights.reshape(KEYS // 8, 8, 384), axis=0)
            out = out + transposed_times(low(weights), v_ref[rows, :])
        total = jnp.sum(total, axis=0, keepdims=True)
        lse_ref[block] = peak + jnp.log(total)
        out = out * jnp.transpose(jnp.broadcast_to(1.0 / total, (128, 384)))
        o_ref[block] = low(out)
        outgoing[block] = low(
            jnp.concatenate([packed(out[0:192]), packed(out[192:384])], axis=1)
        )
        step = lax.rem(block - me + 8, 8)

        @pl.when(step != 0)
        def _():
            outgoing_copy(block, step).start()

        @pl.when(step == 0)
        def _():
            pltpu.make_async_copy(outgoing.at[block], here_ref.at[0], here_sem).start()

    for block in range(6):
        attend(block)
    forward(*out_plan, out_far)
    for block in range(6, 8):
        attend(block)
    settle(*out_plan)
    upstream_right.wait_recv()
    upstream_last = [sent(upstream.at[before, lower], upstream.at[before, lower], right)]
    upstream_left.wait_recv()
    upstream_last.append(sent(upstream.at[after, upper], upstream.at[after, upper], left))
    out_load.wait()

    pltpu.make_async_copy(outgoing.at[me], here_ref.at[0], here_sem).wait()
    middle = wide(tokens_ref[...]) + jnp.dot(
        here_ref[0], out_all[0], preferred_element_type=jnp.float32
    )
    for step in range(7, 0, -1):
        outgoing_copy(lax.rem(me + step, 8), step).wait_recv()
        middle += jnp.dot(here_ref[8 - step], out_all[8 - step], preferred_element_type=jnp.float32)
    middle_ref[...] = middle
    stored(middle_ref, middle_out_ref)
    stored(here_ref, here_out_ref)
    stored(o_ref, o_out_ref)
    scale = lax.rsqrt(jnp.mean(middle * middle, axis=1, keepdims=True) + EPSILON)
    normed_two[z] = low(middle * scale * gain_ref[1:2, :])
    two_right = [
        sent(normed_two.at[z, rows], normed_two.at[z, rows], right) for rows in (lower, upper)
    ]
    two_left = [
        sent(normed_two.at[z, rows], normed_two.at[z, rows], left) for rows in (upper, lower)
    ]
    normed_across = [sent(landed.at[k], normed_other_ref.at[k], across) for k in range(2)]
    stored(out_all, out_out_ref)
    gate_up_load.wait()
    down_load.wait()

    def act_back(block, side):
        dact[block, side] = times_transposed(upstream[block], down[side])

    def feed(block, side):
        cols = pl.ds(side * 512, 512)
        gate = jnp.dot(normed_two[block], gate_up[side, 0], preferred_element_type=jnp.float32)
        up = jnp.dot(normed_two[block], gate_up[side, 1], preferred_element_type=jnp.float32)
        sigmoid = 1.0 / (1.0 + jnp.exp(-gate))
        silu = gate * sigmoid
        act[block, :, cols] = low(silu * up)
        grad = dact[block, side]
        dgu[0, block, :, cols] = low(grad * up * sigmoid * (1.0 + gate * (1.0 - sigmoid)))
        dgu[1, block, :, cols] = low(grad * silu)

    def partial(block):
        total = jnp.zeros((192, 1536), jnp.float32)
        for kind in range(2):
            for side in range(2):
                total = total + times_transposed(
                    dgu[kind, block, :, pl.ds(side * 512, 512)], gate_up[side, kind]
                )
        dn_part[...] = low(total)

    act_back(z, 0)
    feed(z, 0)
    act_back(before, 0)
    act_back(after, 0)
    down_far = pass_on(*down_plan, down_moves)
    gate_up_far = pass_on(*gate_up_plan, gate_up_moves)
    two_right[0].wait_recv()
    two_last = [sent(normed_two.at[before, lower], normed_two.at[before, lower], right)]
    two_left[0].wait_recv()
    two_last.append(sent(normed_two.at[after, upper], normed_two.at[after, upper], left))
    forward(*down_plan, down_far)
    settle(*down_plan)
    stored(down.at[1], down_out_ref)
    act_back(z, 1)
    act_back(before, 1)
    act_back(after, 1)
    forward(*gate_up_plan, gate_up_far)
    two_right[1].wait_recv()
    two_left[1].wait_recv()
    feed(before, 0)
    feed(after, 0)
    settle(*gate_up_plan)
    stored(gate_up.at[1], gate_up_out_ref)
    feed(z, 1)
    feed(before, 1)
    feed(after, 1)
    for copy in upstream_last:
        copy.wait_recv()
    stored(upstream, upstream_ref)
    act_back(opposite, 0)
    act_back(opposite, 1)
    for copy in two_last:
        copy.wait_recv()
    stored(normed_two, normed_two_ref)
    feed(opposite, 0)
    feed(opposite, 1)
    stored(act, act_ref)
    stored(dgu, dgu_ref)
    partial(opposite)
    stored(dn_part, dn_out_ref)
    for copy in normed_across:
        copy.wait_recv()
    for copy in copies:
        copy.wait_send()
    for step in range(1, 8):
        outgoing_copy(lax.rem(me + step, 8), step).wait_send()
    for copy in stores:
        copy.wait()


FRONT_SLOTS = 77
FRONT_LOCALS = 26


def rotation_tables():
    inverse = np.float32(THETA) ** (-np.arange(0, HEAD_SIZE, 2, dtype=np.float32) / HEAD_SIZE)
    phases = np.arange(1536, dtype=np.float32)[:, None] * inverse.astype(np.float32)[None, :]
    cosine, sine = np.zeros((1536, 128), np.float32), np.zeros((1536, 128), np.float32)
    cosine[:, 0:48] = cosine[:, 64:112] = np.cos(phases)
    sine[:, 64:112] = np.sin(phases)
    sine[:, 0:48] = -sine[:, 64:112]
    return cosine.reshape(12, BLOCK, 128), sine.reshape(12, BLOCK, 128)


def fronted(tokens, lens, gains, qkv, out_weight, gate_up, down, cotangent):
    def shape(dims, kind=jnp.bfloat16):
        return jax.ShapeDtypeStruct(dims, kind)

    def room(*dims):
        return pltpu.VMEM(dims, jnp.bfloat16)

    cosine, sine = rotation_tables()
    return pl.pallas_call(
        front_kernel,
        out_shape=(
            shape((4, 192, 1536)),
            shape((2, 192, 1536)),
            shape((1536, 512)),
            shape((1536, 384)),
            shape((8, 192, 1536)),
            shape((2, 1536, 512)),
            shape((512, 1536)),
            shape((4, 192, 1536)),
            shape((4, 192, 1536)),
            shape((4, 192, 1024)),
            shape((2, 4, 192, 1024)),
            shape((192, 1536), jnp.float32),
            shape((8, 192, 192)),
            shape((8, 384, 128)),
            shape((1536, 128)),
            shape((1536, 128)),
            shape((8, 384, 128)),
            shape((1536, 128), jnp.float32),
            shape((1536, 128), jnp.float32),
            shape((192, 1536)),
            shape((8, 1, 384), jnp.float32),
        ),
        in_specs=[IN_VMEM, pl.BlockSpec(memory_space=pltpu.SMEM), IN_VMEM] + [ANY] * 7,
        out_specs=(ANY,) * 20 + (IN_VMEM,),
        scratch_shapes=[
            room(4, 192, 1536),
            room(1536, 384),
            room(1536, 384),
            room(1536, 512),
            room(1536, 512),
            room(4, 192, 384),
            room(4, 192, 384),
            pltpu.VMEM((2, 12, BLOCK, 128), jnp.float32),
            room(8, 192, 1536),
            room(2, 2, 1536, 512),
            room(2, 512, 1536),
            room(4, 192, 1536),
            room(4, 192, 1536),
            room(4, 192, 1024),
            room(2, 4, 192, 1024),
            pltpu.VMEM((4, 2, 192, 512), jnp.float32),
            pltpu.VMEM((1536, 384), jnp.float32),
            room(8, 192, 192),
            pltpu.VMEM((192, 1536), jnp.float32),
            room(8, 192, 192),
            room(8, 384, 128),
            room(1536, 128),
            room(1536, 128),
            room(8, 384, 128),
            pltpu.VMEM((1536, 128), jnp.float32),
            pltpu.VMEM((1536, 128), jnp.float32),
            room(192, 1536),
            pltpu.SemaphoreType.DMA((FRONT_SLOTS + 8,)),
            pltpu.SemaphoreType.DMA((FRONT_SLOTS + 8,)),
            pltpu.SemaphoreType.DMA((FRONT_LOCALS + 1,)),
        ],
        compiler_params=pltpu.CompilerParams(
            collective_id=1, has_side_effects=True, vmem_limit_bytes=62 * 2**20
        ),
        name="front",
    )(
        tokens,
        lens,
        gains,
        qkv,
        out_weight,
        gate_up,
        down,
        cotangent,
        jnp.asarray(cosine),
        jnp.asarray(sine),
    )


def mid_kernel(
    dgu_ref,
    act_ref,
    normed_two_ref,
    upstream_ref,
    normed_ref,
    part_ref,
    gate_up_ref,
    gate_up_other_ref,
    down_ref,
    down_other_ref,
    out_in_ref,
    here_in_ref,
    middle_in_ref,
    cotangent_in_ref,
    gain_ref,
    dh_ref,
    landed_ref,
    out_grad_ref,
    ffn_right_ref,
    ffn_left_ref,
    ffn_own_ref,
    gate_own_ref,
    feeds_ref,
    normed_other_ref,
    dgu,
    act,
    normed,
    upstream,
    own,
    gate_up,
    down,
    turned,
    grads,
    grads_core,
    grads_a,
    grads_b,
    gate_left,
    gate_right,
    near_out,
    far_a,
    far_b,
    from_left,
    from_right,
    feeds,
    out_all,
    here,
    middle_room,
    cotangent,
    outgoing,
    landed,
    dhb,
    out_part,
    send_sem,
    recv_sem,
    local_sem,
):
    x, c = lax.axis_index("x"), lax.axis_index("c")
    z = lax.axis_index("z")
    after, before, opposite = lax.rem(z + 1, 4), lax.rem(z + 3, 4), lax.rem(z + 2, 4)
    x_after, x_before, x_far = lax.rem(x + 1, 4), lax.rem(x + 3, 4), lax.rem(x + 2, 4)
    right, left, across = {"z": after}, {"z": before}, {"yh": 1 - lax.axis_index("yh")}
    x_right, x_left, core = {"x": x_after}, {"x": x_before}, {"c": 1 - c}
    partners = [tensor_partner(step) for step in range(1, 8)] + [x_right, x_left, core]
    barrier = pltpu.get_barrier_semaphore()
    for partner in partners:
        pl.semaphore_signal(barrier, inc=1, device_id=partner, device_id_type=MESH)
    local_slots, slots = iter(range(MID_LOCALS)), iter(range(MID_SLOTS))
    stores, copies = [], []
    raw_sent = kernel_copies(send_sem, recv_sem)

    def moved(source, goal):
        copy = pltpu.make_async_copy(source, goal, local_sem.at[next(local_slots)])
        copy.start()
        return copy

    def stored(source, goal):
        stores.append(moved(source, goal))

    def sent(source, goal, device):
        copy = raw_sent(next(slots), source, goal, device)
        copies.append(copy)
        return copy

    def arrived(pair):
        for copy in pair:
            copy.wait_recv()

    dgu_load = moved(dgu_ref, dgu)
    gate_up_loads = [
        moved(gate_up_ref, gate_up.at[0]),
        moved(gate_up_other_ref, gate_up.at[1]),
    ]
    normed_load = moved(normed_two_ref, normed)
    upstream_load = moved(upstream_ref, upstream)
    act_load = moved(act_ref, act)
    down_loads = [moved(down_ref, down.at[0]), moved(down_other_ref, down.at[1])]
    middle_load = moved(middle_in_ref, middle_room)
    cotangent_load = moved(cotangent_in_ref, cotangent)
    out_load = moved(out_in_ref, out_all)
    here_load = moved(here_in_ref, here)
    pl.semaphore_wait(barrier, len(partners))

    far = [
        sent(part_ref.at[pl.ds(0, 96)], far_a, right),
        sent(part_ref.at[pl.ds(96, 96)], far_b, left),
    ]
    normed_across = [
        sent(normed_ref.at[2 + k], normed_other_ref.at[k], across) for k in range(2)
    ]

    def add_core(kind):
        cored[kind].wait_recv()
        for k in range(8):
            grads[kind, k, c] = low(wide(grads[kind, k, c]) + wide(grads_core[kind, k]))
        spot = grads.at[kind, pl.ds(x_far * 2, 2), c]
        return [
            sent(spot.at[:, :, pl.ds(0, 512)], grads_a.at[kind], x_right),
            sent(spot.at[:, :, pl.ds(512, 512)], grads_b.at[kind], x_left),
        ]

    def grad(kind, right_side):
        for side in range(2):
            cols = pl.ds(side * 512, 512)
            value = jnp.dot(turned[...], right_side(cols), preferred_element_type=jnp.float32)
            grads[kind, :, :, :, cols] = low(value).reshape(8, 2, 96, 512)
        cored.append(sent(grads.at[kind, :, 1 - c], grads_core.at[kind], core))

    cored = []

    def add_x(kind):
        arrived(round_x[kind])
        for k in range(2):
            spot = grads[kind, x_after * 2 + k, c, :, 0:512]
            grads[kind, x_after * 2 + k, c, :, 0:512] = low(wide(spot) + wide(grads_a[kind, k]))
            spot = grads[kind, x_before * 2 + k, c, :, 512:1024]
            grads[kind, x_before * 2 + k, c, :, 512:1024] = low(
                wide(spot) + wide(grads_b[kind, k])
            )

    def partial(block):
        total = jnp.zeros((192, 1536), jnp.float32)
        for kind in range(2):
            for side in range(2):
                total = total + times_transposed(
                    dgu[kind, block, :, pl.ds(side * 512, 512)], gate_up[side, kind]
                )
        return total


    dgu_load.wait()
    for load in gate_up_loads:
        load.wait()
    to_right, to_left = partial(after), partial(before)
    normed_load.wait()
    turned[...] = jnp.transpose(normed[...].reshape(768, 1536))
    grad(0, lambda cols: dgu[0, :, :, cols].reshape(768, 512))
    arrived(far)
    near_out[0, 0:96] = low(to_right[0:96] + wide(far_a[...]))
    near_out[0, 96:192] = low(to_right[96:192])
    near_out[1, 0:96] = low(to_left[0:96])
    near_out[1, 96:192] = low(to_left[96:192] + wide(far_b[...]))
    near = [
        sent(near_out.at[0], from_left, right),
        sent(near_out.at[1], from_right, left),
    ]
    grad(1, lambda cols: dgu[1, :, :, cols].reshape(768, 512))
    round_x = [add_core(0)]
    upstream_load.wait()
    act_load.wait()
    turned[...] = jnp.transpose(upstream[...].reshape(768, 1536))
    grad(2, lambda cols: act[:, :, cols].reshape(768, 512))
    round_x.append(add_core(1))

    round_x.append(add_core(2))
    stored(grads.at[pl.ds(1, 2), pl.ds(x * 2, 2), c], ffn_own_ref)
    own[...] = partial(z)
    add_x(0)
    gate_second = [
        sent(grads.at[0, pl.ds(x_after * 2, 2), c], gate_left, x_right),
        sent(grads.at[0, pl.ds(x_before * 2, 2), c], gate_right, x_left),
    ]
    middle_load.wait()
    cotangent_load.wait()
    out_load.wait()
    middle = middle_room[...]
    scale = lax.rsqrt(jnp.mean(middle * middle, axis=1, keepdims=True) + EPSILON)
    unit = middle * scale
    arrived(near)
    dn = own[...] + wide(from_left[...]) + wide(from_right[...])
    scaled = dn * gain_ref[1:2, :]
    dh = wide(cotangent[...]) + scale * (
        scaled - unit * jnp.mean(scaled * unit, axis=1, keepdims=True)
    )
    dh_ref[...] = dh
    dhb[...] = low(dh)
    do_moves = []
    for step in range(1, 8):
        outgoing[step] = low(times_transposed(dhb[...], out_all[step]))
        do_moves.append(sent(outgoing.at[step], landed.at[8 - step], tensor_partner(step)))
    landed[0] = low(times_transposed(dhb[...], out_all[0]))
    here_load.wait()
    for k in range(8):
        out_part[k] = low(transposed_times(here[k], dhb[...]))
    stored(out_part, out_grad_ref)
    for load in down_loads:
        load.wait()

    def feed(block):
        return jnp.dot(
            act[block, :, 0:512], down[0], preferred_element_type=jnp.float32
        ) + jnp.dot(act[block, :, 512:1024], down[1], preferred_element_type=jnp.float32)

    feeds[3] = low(feed(opposite))
    feeds[0], feeds[1], feeds[2] = low(feed(after)), low(feed(before)), low(feed(z))
    stored(feeds, feeds_ref)
    add_x(1)
    add_x(2)
    stored(grads.at[pl.ds(1, 2), pl.ds(x_after * 2, 2), c], ffn_right_ref)
    stored(grads.at[pl.ds(1, 2), pl.ds(x_before * 2, 2), c], ffn_left_ref)
    arrived(gate_second)
    for k in range(2):
        gate_left[k] = low(
            wide(grads[0, x * 2 + k, c]) + wide(gate_left[k]) + wide(gate_right[k])
        )
    stored(gate_left, gate_own_ref)
    arrived(do_moves)
    stored(landed, landed_ref)
    arrived(normed_across)
    for copy in copies:
        copy.wait_send()
    for copy in stores:
        copy.wait()


MID_SLOTS = 26
MID_LOCALS = 25


def middled(*arguments):
    def shape(dims, kind=jnp.bfloat16):
        return jax.ShapeDtypeStruct(dims, kind)

    def room(*dims):
        return pltpu.VMEM(dims, jnp.bfloat16)

    return pl.pallas_call(
        mid_kernel,
        out_shape=(
            shape((192, 1536), jnp.float32),
            shape((8, 192, 192)),
            shape((8, 192, 1536)),
            shape((2, 2, 96, 1024)),
            shape((2, 2, 96, 1024)),
            shape((2, 2, 96, 1024)),
            shape((2, 96, 1024)),
            shape((4, 192, 1536)),
            shape((2, 192, 1536)),
        ),
        in_specs=[ANY] * 14 + [IN_VMEM],
        out_specs=(IN_VMEM,) + (ANY,) * 8,
        scratch_shapes=[
            room(2, 4, 192, 1024),
            room(4, 192, 1024),
            room(4, 192, 1536),
            room(4, 192, 1536),
            pltpu.VMEM((192, 1536), jnp.float32),
            room(2, 2, 1536, 512),
            room(2, 512, 1536),
            room(1536, 768),
            room(3, 8, 2, 96, 1024),
            room(3, 8, 96, 1024),
            room(3, 2, 96, 512),
            room(3, 2, 96, 512),
            room(2, 96, 1024),
            room(2, 96, 1024),
            room(2, 192, 1536),
            room(96, 1536),
            room(96, 1536),
            room(192, 1536),
            room(192, 1536),
            room(4, 192, 1536),
            room(8, 192, 1536),
            room(8, 192, 192),
            pltpu.VMEM((192, 1536), jnp.float32),
            room(192, 1536),
            room(8, 192, 192),
            room(8, 192, 192),
            room(192, 1536),
            room(8, 192, 1536),
            pltpu.SemaphoreType.DMA((MID_SLOTS,)),
            pltpu.SemaphoreType.DMA((MID_SLOTS,)),
            pltpu.SemaphoreType.DMA((MID_LOCALS,)),
        ],
        compiler_params=pltpu.CompilerParams(
            collective_id=3, has_side_effects=True, vmem_limit_bytes=62 * 2**20
        ),
        name="mid",
    )(*arguments)


def back_kernel(
    gain_ref,
    lse_ref,
    lens_ref,
    dh_in_ref,
    middle_in_ref,
    grads_in_ref,
    out_in_ref,
    q_in_ref,
    k_in_ref,
    v_in_ref,
    o_in_ref,
    cos_in_ref,
    sin_in_ref,
    weight_in_ref,
    weight_other_in_ref,
    tokens_in_ref,
    normed_ref,
    normed_first_ref,
    normed_second_ref,
    ffn_right_ref,
    ffn_left_ref,
    ffn_own_ref,
    gate_own_ref,
    feeds_ref,
    gate_up_ref,
    mixed_ref,
    input_grad_ref,
    qkv_grad_ref,
    out_grad_ref,
    ffn_grad_ref,
    gains_ref,
    landed,
    dk_sum,
    dv_sum,
    dp,
    normed,
    ffn_own,
    feeds,
    feed_a,
    feed_b,
    feed_from_left,
    feed_from_right,
    ffn_from_left,
    ffn_from_right,
    ffn_out,
    ffn_in,
    out_part,
    out_core,
    out_far_a,
    out_far_b,
    out_from_left,
    out_from_right,
    out_sum,
    out_shards,
    out_swap,
    out_swap_in,
    qkv_part,
    qkv_core,
    qkv_in,
    far_out,
    near_out,
    far_a,
    far_b,
    from_left,
    from_right,
    dq_out,
    dq_in,
    dkv_out,
    dkv_in,
    gain_out,
    gain_in,
    gate_up_rows,
    dh_ref,
    middle_ref,
    q_ref,
    k_ref,
    v_ref,
    o_ref,
    cos_ref,
    sin_ref,
    weight_ref,
    weight_other_ref,
    tokens_ref,
    send_sem,
    recv_sem,
    local_sem,
):
    x, yl, c = lax.axis_index("x"), lax.axis_index("yl"), lax.axis_index("c")
    yh, z = lax.axis_index("yh"), lax.axis_index("z")
    me = yh * 4 + z
    place = (x * 2 + yl) * 2 + c
    after, before, opposite = lax.rem(z + 1, 4), lax.rem(z + 3, 4), lax.rem(z + 2, 4)
    x_after, x_before, x_far = lax.rem(x + 1, 4), lax.rem(x + 3, 4), lax.rem(x + 2, 4)
    right, left, across = {"z": after}, {"z": before}, {"yh": 1 - yh}
    x_right, x_left = {"x": x_after}, {"x": x_before}
    core, other_yl, cross = {"c": 1 - c}, {"yl": 1 - yl}, {"yl": 1 - yl, "yh": 1 - yh}
    def dp_partner(step):
        goal = lax.rem(x * 2 + yl + step, 8)
        return {"x": lax.div(goal, 2), "yl": lax.rem(goal, 2)}, goal

    partners = [tensor_partner(step) for step in range(1, 8)]
    partners += [{**tensor_partner(step), "yl": 1 - yl} for step in range(1, 8)]
    partners += [core] + [dp_partner(step)[0] for step in range(1, 8)]
    barrier = pltpu.get_barrier_semaphore()
    for partner in partners:
        pl.semaphore_signal(barrier, inc=1, device_id=partner, device_id_type=MESH)
    raw_sent = kernel_copies(send_sem, recv_sem)
    copies = []
    slots = iter(range(SLOTS))

    def sent(source, goal, device):
        copy = raw_sent(next(slots), source, goal, device)
        copies.append(copy)
        return copy

    def arrived(pair):
        for copy in pair:
            copy.wait_recv()

    local_slots = iter(range(BACK_LOCALS))

    def fetched(source, goal):
        copy = pltpu.make_async_copy(source, goal, local_sem.at[next(local_slots)])
        copy.start()
        return copy

    attend_loads = [
        fetched(source, goal)
        for source, goal in (
            (grads_in_ref, landed),
            (q_in_ref, q_ref),
            (k_in_ref, k_ref),
            (v_in_ref, v_ref),
            (o_in_ref, o_ref),
            (cos_in_ref, cos_ref),
            (sin_in_ref, sin_ref),
        )
    ]
    out_load = fetched(out_in_ref.at[:, lines(c * 96, 96), :], out_part)
    weight_load = fetched(weight_in_ref, weight_ref)
    weight_other_load = fetched(weight_other_in_ref, weight_other_ref)
    normed_loads = [
        fetched(normed_ref, normed.at[lines(yh * 768, 768), :]),
        fetched(normed_first_ref, normed.at[lines((1 - yh) * 768, 384), :]),
        fetched(normed_second_ref, normed.at[lines((1 - yh) * 768 + 384, 384), :]),
    ]
    ffn_loads = [
        fetched(gate_own_ref, ffn_own.at[0]),
        fetched(ffn_own_ref, ffn_own.at[pl.ds(1, 2)]),
    ]
    feed_load = fetched(feeds_ref.at[pl.ds(0, 3)], feeds)
    tokens_load = fetched(tokens_in_ref, tokens_ref)
    middle_load = fetched(middle_in_ref, middle_ref)
    dh_load = fetched(dh_in_ref, dh_ref)
    rows_load = fetched(gate_up_ref.at[:, lines(place * 96, 96), :], gate_up_rows)

    pl.semaphore_wait(barrier, len(partners))
    out_cored = sent(out_in_ref.at[:, lines((1 - c) * 96, 96), :], out_core, core)
    ffn_second = [
        sent(ffn_right_ref, ffn_from_left, x_right),
        sent(ffn_left_ref, ffn_from_right, x_left),
    ]
    feed_far = [
        sent(feeds_ref.at[3, pl.ds(0, 96)], feed_a, right),
        sent(feeds_ref.at[3, pl.ds(96, 96)], feed_b, left),
    ]
    starts, ends = sequences(lens_ref)
    dk_sum[...] = jnp.zeros_like(dk_sum)
    dv_sum[...] = jnp.zeros_like(dv_sum)

    def unturned(values, rows):
        return values * cos_ref[rows, :] - pltpu.roll(values, 64, 1) * sin_ref[rows, :]

    dq_slot = [next(slots) for _ in range(4)][0]

    def dq_copy(block):
        return pltpu.make_async_remote_copy(
            src_ref=dq_out.at[block % 4],
            dst_ref=dq_in.at[block % 4],
            send_sem=send_sem.at[dq_slot + block % 4],
            recv_sem=recv_sem.at[dq_slot + block % 4],
            device_id=across,
            device_id_type=MESH,
        )

    def back(block):
        step = lax.rem(block - me + 8, 8)
        grads = landed[step]
        grad_block = jnp.concatenate([spread(grads[:, 0:96]), spread(grads[:, 96:192])], axis=0)
        query_block = q_ref[block]
        queries, first_row = block_queries(block, starts, ends)
        lse = lse_ref[block]
        centered = wide(grad_block) * wide(o_ref[block])
        centered = jnp.sum(jnp.transpose(centered), axis=0, keepdims=True)
        dq = jnp.zeros((384, 128), jnp.float32)
        for j in range((192 * (block + 1) + KEYS - 1) // KEYS):
            rows = pl.ds(j * KEYS, KEYS)
            key_block, value_block = k_ref[rows, :], v_ref[rows, :]
            scores, allowed = static_score(
                key_block, query_block, first_row, j * KEYS, queries, block * 192
            )
            weights = jnp.where(allowed, jnp.exp(scores - lse), 0.0)
            grad_weights = times_transposed(value_block, grad_block)
            grad_scores = low(weights * (grad_weights - centered))
            dv_sum[rows, :] += jnp.dot(
                low(weights), grad_block, preferred_element_type=jnp.float32
            )
            dk_sum[rows, :] += jnp.dot(
                grad_scores, query_block, preferred_element_type=jnp.float32
            )
            dq = dq + transposed_times(grad_scores, key_block)
        dq = dq * (HEAD_SIZE ** (-0.5))
        rows = pl.ds(block * 192, 192)
        first, second = unturned(dq[0:192], rows), unturned(dq[192:384], rows)
        dp[rows, 0:128] = low(first)
        dp[rows, 128:256] = low(second)

        @pl.when(yh != block // 4)
        def _():
            dq_out[block % 4] = low(jnp.concatenate([packed(first), packed(second)], axis=1))
            dq_copy(block).start()

    for load in attend_loads:
        load.wait()
    for block in range(4):
        back(block)
    out_load.wait()
    out_cored.wait_recv()
    for k in range(8):
        out_part[k] = low(wide(out_part[k]) + wide(out_core[k]))
    out_first = [
        sent(out_part.at[pl.ds(0, 4), :, columns(x_far * 384, 384)], out_far_a, x_right),
        sent(out_part.at[pl.ds(4, 4), :, columns(x_far * 384, 384)], out_far_b, x_left),
    ]
    for block in range(4, 6):
        back(block)
    arrived(feed_far)
    feed_load.wait()
    feeds[0, 0:96] = low(wide(feeds[0, 0:96]) + wide(feed_a[...]))
    feeds[1, 96:192] = low(wide(feeds[1, 96:192]) + wide(feed_b[...]))
    feed_second = [
        sent(feeds.at[0], feed_from_left, right),
        sent(feeds.at[1], feed_from_right, left),
    ]
    back(6)
    back(7)
    for block in range(8):
        rows = pl.ds(block * 192, 192)
        dp[rows, 256:384] = low(unturned(dk_sum[rows, :] * (HEAD_SIZE ** (-0.5)), rows))
        dp[rows, 384:512] = low(dv_sum[rows, :])

    mine = yh * 768
    for k in range(4):
        rows = lines((1 - yh) * 768 + k * 192, 192)
        dkv_out[k] = jnp.concatenate(
            [packed(dp[rows, 256:384]), packed(dp[rows, 384:512])], axis=1
        )
    exchanged = sent(dkv_out, dkv_in, across)
    for load in normed_loads:
        load.wait()
    for part in range(4):
        features = pl.ds(part * 384, 384)
        grad = transposed_times(normed[:, features], dp[...])
        qkv_part[part * 2 : part * 2 + 2] = low(grad).reshape(2, 2, 96, 512)
    qkv_cored = sent(qkv_part.at[:, 1 - c], qkv_core, core)
    arrived(ffn_second)
    for load in ffn_loads:
        load.wait()
    for kind in range(2):
        ffn_own[kind + 1] = low(
            wide(ffn_own[kind + 1]) + wide(ffn_from_left[kind]) + wide(ffn_from_right[kind])
        )
    ffn_sum = wide(ffn_own[...])
    flipped = jnp.where(yl == 0, ffn_sum[:, 1], ffn_sum[:, 0])
    kept = jnp.where(yl == 0, ffn_sum[:, 0], ffn_sum[:, 1])
    ffn_out[0] = low(flipped[..., 0:512])
    ffn_out[1] = low(flipped[..., 512:1024])
    ffn_out[2] = low(kept[..., 512:1024])
    ffn_moves = [
        sent(ffn_out.at[k], ffn_in.at[k], device)
        for k, device in enumerate((other_yl, cross, across))
    ]
    ffn_grad_ref[...] = kept[..., 0:512]
    out_cols = [columns(place_x * 384, 384) for place_x in (x_after, x_before)]
    arrived(out_first)
    for k in range(4):
        out_part[k, :, out_cols[0]] = low(wide(out_part[k, :, out_cols[0]]) + wide(out_far_a[k]))
        out_part[4 + k, :, out_cols[1]] = low(
            wide(out_part[4 + k, :, out_cols[1]]) + wide(out_far_b[k])
        )
    out_second = [
        sent(out_part.at[:, :, out_cols[0]], out_from_left, x_right),
        sent(out_part.at[:, :, out_cols[1]], out_from_right, x_left),
    ]
    qkv_cored.wait_recv()
    for k in range(8):
        qkv_part[k, c] = low(wide(qkv_part[k, c]) + wide(qkv_core[k]))
    qkv_moves = [
        sent(qkv_part.at[goal, c], qkv_in.at[step - 1], device)
        for step, (device, goal) in ((step, dp_partner(step)) for step in range(1, 8))
    ]
    for k in range(4):
        dq_copy(k).wait_recv()
    exchanged.wait_recv()
    weight_load.wait()
    weight_other_load.wait()

    def partial(block_z):
        theirs = jnp.concatenate([dq_in[block_z], dkv_in[block_z]], axis=1)
        return times_transposed(
            dp[lines(mine + block_z * 192, 192), :], weight_ref[...]
        ) + times_transposed(theirs, weight_other_ref[...])

    far_out[...] = low(partial(opposite))
    far = [
        sent(far_out.at[pl.ds(0, 96)], far_a, right),
        sent(far_out.at[pl.ds(96, 96)], far_b, left),
    ]
    to_right, to_left = partial(after), partial(before)
    arrived(far)
    near_out[0, 0:96] = low(to_right[0:96] + wide(far_a[...]))
    near_out[0, 96:192] = low(to_right[96:192])
    near_out[1, 0:96] = low(to_left[0:96])
    near_out[1, 96:192] = low(to_left[96:192] + wide(far_b[...]))
    near = [
        sent(near_out.at[0], from_left, right),
        sent(near_out.at[1], from_right, left),
    ]
    own = partial(z)
    arrived(out_second)
    own_cols = columns(x * 384, 384)
    for k in range(8):
        total = wide(out_part[k, :, own_cols]) + wide(out_from_left[k]) + wide(out_from_right[k])
        out_sum[k, 0] = low(total[:, 0:192])
        out_sum[k, 1] = low(total[:, 192:384])
    out_moves = []
    for step in range(8):
        place_yh = tensor_partner(step)
        for side in range(2):
            if step + side > 0:
                goal_yl = yl if side == 0 else 1 - yl
                out_moves.append(
                    sent(
                        out_sum.at[step, goal_yl],
                        out_shards.at[step * 2 + side - 1],
                        {**place_yh, "yl": goal_yl},
                    )
                )
    arrived(feed_second)
    middle_load.wait()
    mixed_ref[...] = low(
        middle_ref[...] + wide(feeds[2]) + wide(feed_from_left[...]) + wide(feed_from_right[...])
    )
    arrived(qkv_moves)
    qkv_final = wide(qkv_part[x * 2 + yl, c])
    for k in range(7):
        qkv_final = qkv_final + wide(qkv_in[k])
    qkv_grad_ref[...] = qkv_final
    arrived(ffn_moves)
    ffn_final = ffn_grad_ref[...]
    for k in range(3):
        ffn_final = ffn_final + wide(ffn_in[k])
    ffn_grad_ref[...] = ffn_final
    rows_load.wait()
    gain_one = jnp.sum(
        qkv_final * wide(weight_ref[lines(place * 96, 96), :]), axis=1, keepdims=True
    )
    gain_two = jnp.sum(
        ffn_final[0] * wide(gate_up_rows[0]) + ffn_final[1] * wide(gate_up_rows[1]),
        axis=1,
        keepdims=True,
    )
    lanes = lax.broadcasted_iota(jnp.int32, (96, 128), 1)
    gain_out[...] = jnp.where(lanes == 0, gain_one, jnp.where(lanes == 1, gain_two, 0.0))
    gain_shared = [
        sent(gain_out, gain_in.at[step - 1], tensor_partner(step)) for step in range(1, 8)
    ]
    arrived(out_moves)
    out_final = wide(out_sum[0, yl])
    for k in range(15):
        out_final = out_final + wide(out_shards[k])
    out_swap[...] = low(jnp.where(c == 0, out_final[:, 96:192], out_final[:, 0:96]))
    out_swapped = sent(out_swap, out_swap_in, core)
    out_mine = jnp.where(c == 0, out_final[:, 0:96], out_final[:, 96:192])
    out_grad_ref[lines(c * 96, 96), :] = out_mine
    arrived(near)
    dn = own + wide(from_left[...]) + wide(from_right[...])
    tokens_load.wait()
    hidden = wide(tokens_ref[...])
    scale = lax.rsqrt(jnp.mean(hidden * hidden, axis=1, keepdims=True) + EPSILON)
    unit = hidden * scale
    scaled = dn * gain_ref[0:1, :]
    dh_load.wait()
    input_grad_ref[...] = dh_ref[...] + scale * (
        scaled - unit * jnp.mean(scaled * unit, axis=1, keepdims=True)
    )
    out_swapped.wait_recv()
    out_grad_ref[lines((1 - c) * 96, 96), :] = wide(out_swap_in[...])
    arrived(gain_shared)
    total = gain_out[...]
    for k in range(7):
        total = total + gain_in[k]
    gains_ref[...] = total
    for copy in copies:
        copy.wait_send()
    for k in range(4):
        dq_copy(k).wait_send()


SLOTS = 72
BACK_LOCALS = 23


def finished_back(*arguments):
    def shape(dims, kind=jnp.float32):
        return jax.ShapeDtypeStruct(dims, kind)

    def room(*dims):
        return pltpu.VMEM(dims, jnp.bfloat16)

    return pl.pallas_call(
        back_kernel,
        out_shape=(
            shape((192, 1536), jnp.bfloat16),
            shape((192, 1536)),
            shape((96, 512)),
            shape((192, 96)),
            shape((3, 96, 512)),
            shape((96, 128)),
        ),
        in_specs=[IN_VMEM] * 2 + [pl.BlockSpec(memory_space=pltpu.SMEM)] + [ANY] * 22,
        out_specs=(IN_VMEM,) * 6,
        scratch_shapes=[
            room(8, 192, 192),
            pltpu.VMEM((1536, 128), jnp.float32),
            pltpu.VMEM((1536, 128), jnp.float32),
            room(1536, 512),
            room(1536, 1536),
            room(3, 2, 96, 1024),
            room(3, 192, 1536),
            room(96, 1536),
            room(96, 1536),
            room(192, 1536),
            room(192, 1536),
            room(2, 2, 96, 1024),
            room(2, 2, 96, 1024),
            room(3, 3, 96, 512),
            room(3, 3, 96, 512),
            room(8, 96, 1536),
            room(8, 96, 1536),
            room(4, 96, 384),
            room(4, 96, 384),
            room(8, 96, 384),
            room(8, 96, 384),
            room(8, 2, 96, 192),
            room(15, 96, 192),
            room(96, 96),
            room(96, 96),
            room(8, 2, 96, 512),
            room(8, 96, 512),
            room(7, 96, 512),
            room(192, 1536),
            room(2, 192, 1536),
            room(96, 1536),
            room(96, 1536),
            room(192, 1536),
            room(192, 1536),
            room(4, 192, 192),
            room(4, 192, 192),
            room(4, 192, 192),
            room(4, 192, 192),
            pltpu.VMEM((96, 128), jnp.float32),
            pltpu.VMEM((7, 96, 128), jnp.float32),
            room(2, 96, 512),
            pltpu.VMEM((192, 1536), jnp.float32),
            pltpu.VMEM((192, 1536), jnp.float32),
            room(8, 384, 128),
            room(1536, 128),
            room(1536, 128),
            room(8, 384, 128),
            pltpu.VMEM((1536, 128), jnp.float32),
            pltpu.VMEM((1536, 128), jnp.float32),
            room(1536, 512),
            room(1536, 384),
            room(192, 1536),
            pltpu.SemaphoreType.DMA((SLOTS,)),
            pltpu.SemaphoreType.DMA((SLOTS,)),
            pltpu.SemaphoreType.DMA((BACK_LOCALS,)),
        ],
        compiler_params=pltpu.CompilerParams(
            collective_id=2, has_side_effects=True, vmem_limit_bytes=63 * 2**20
        ),
        name="back",
    )(*arguments)


def finish_kernel(
    mixed_in,
    input_in,
    qkv_in,
    out_in,
    ffn_in,
    gains_in,
    gain_ref,
    mixed_ref,
    input_ref,
    qkv_ref,
    out_ref,
    gate_up_ref,
    down_ref,
    gains_ref,
    mixed_room,
    input_room,
    ffn_room,
    out_room,
    qkv_room,
    gains_room,
    gain_room,
    qkv_out,
    gains_out,
    sem,
):
    sources = (qkv_in, gains_in, gain_ref, input_in, ffn_in, mixed_in, out_in)
    rooms = (qkv_room, gains_room, gain_room, input_room, ffn_room, mixed_room, out_room)
    arriving, copies = [], []
    for k, (source, room) in enumerate(zip(sources, rooms)):
        arriving.append(pltpu.make_async_copy(source, room, sem.at[k]))
        arriving[-1].start()

    def leave(source, goal):
        copies.append(pltpu.make_async_copy(source, goal, sem.at[7 + len(copies)]))
        copies[-1].start()

    for arrival in arriving[0:3]:
        arrival.wait()
    qkv_out[...] = jnp.concatenate(
        [packed(qkv_room[:, head * 128 : head * 128 + 128]) for head in range(4)], axis=1
    )
    leave(qkv_out, qkv_ref)
    place = (lax.axis_index("x") * 2 + lax.axis_index("yl")) * 2 + lax.axis_index("c")
    gains = jnp.transpose(gains_room[...])[0:2]
    rows = jnp.zeros((2, 96), jnp.float32)
    for k in range(16):
        rows = jnp.where(place == k, gain_room[:, k * 96 : k * 96 + 96], rows)
    gains_out[...] = gains / rows
    leave(gains_out, gains_ref)
    arriving[3].wait()
    leave(input_room, input_ref)
    arriving[4].wait()
    leave(ffn_room.at[pl.ds(0, 2)], gate_up_ref)
    leave(ffn_room.at[2], down_ref)
    arriving[5].wait()
    leave(mixed_room, mixed_ref)
    arriving[6].wait()
    leave(out_room, out_ref)
    for copy in copies:
        copy.wait()


def finished(*arguments):
    def shape(*dims):
        return jax.ShapeDtypeStruct(dims, jnp.float32)

    return pl.pallas_call(
        finish_kernel,
        out_shape=(
            jax.ShapeDtypeStruct((192, 1536), jnp.bfloat16),
            shape(192, 1536),
            shape(96, 384),
            shape(192, 96),
            shape(2, 96, 512),
            shape(96, 512),
            shape(2, 96),
        ),
        in_specs=[ANY] * 7,
        out_specs=(ANY,) * 7,
        scratch_shapes=[
            pltpu.VMEM((192, 1536), jnp.bfloat16),
            pltpu.VMEM((192, 1536), jnp.float32),
            pltpu.VMEM((3, 96, 512), jnp.float32),
            pltpu.VMEM((192, 96), jnp.float32),
            pltpu.VMEM((96, 512), jnp.float32),
            pltpu.VMEM((96, 128), jnp.float32),
            pltpu.VMEM((2, 1536), jnp.float32),
            pltpu.VMEM((96, 384), jnp.float32),
            pltpu.VMEM((2, 96), jnp.float32),
            pltpu.SemaphoreType.DMA((14,)),
        ],
        compiler_params=pltpu.CompilerParams(vmem_limit_bytes=63 * 2**20),
        name="finish",
    )(*arguments)


def per_device(
    tokens,
    seq_lens,
    query_key_value_weight,
    out_weight,
    gate_up_weight,
    down_weight,
    norm_gains,
    cotangent,
):
    (
        normed_half,
        normed_first,
        weight_wide,
        weight_other,
        out_all,
        gate_up_other,
        down_other,
        upstream_all,
        normed_two_all,
        activated,
        grad_gate_up,
        middle,
        attended_here,
        queries,
        keys_all,
        values_all,
        heads,
        cos_part,
        sin_part,
        dn_part,
        log_sums,
    ) = fronted(
        tokens,
        seq_lens,
        norm_gains,
        query_key_value_weight,
        out_weight,
        gate_up_weight,
        down_weight,
        cotangent,
    )
    (
        grad_middle,
        grad_heads,
        out_half,
        ffn_right,
        ffn_left,
        ffn_own,
        gate_own,
        feeds,
        normed_second,
    ) = middled(
        grad_gate_up,
        activated,
        normed_two_all,
        upstream_all,
        normed_half,
        dn_part,
        gate_up_weight,
        gate_up_other,
        down_weight,
        down_other,
        out_all,
        attended_here,
        middle,
        cotangent,
        norm_gains,
    )
    mixed, input_grad, qkv_grad, out_grad, ffn_grad, gains_grad = finished_back(
        norm_gains,
        log_sums,
        seq_lens,
        grad_middle,
        middle,
        grad_heads,
        out_half,
        queries,
        keys_all,
        values_all,
        heads,
        cos_part,
        sin_part,
        weight_wide,
        weight_other,
        tokens,
        normed_half.reshape(768, 1536),
        normed_first.reshape(384, 1536),
        normed_second.reshape(384, 1536),
        ffn_right,
        ffn_left,
        ffn_own,
        gate_own,
        feeds,
        gate_up_weight,
    )
    mixed, input_grad, qkv_grad, out_grad, gate_up_grad, down_grad, gains_grad = finished(
        mixed, input_grad, qkv_grad, out_grad, ffn_grad, gains_grad, norm_gains
    )
    return mixed, input_grad, qkv_grad, out_grad, gate_up_grad, down_grad.T, gains_grad


def solution(mesh):
    split = Mesh(mesh.devices.reshape(4, 2, 2, 2, 4), ALL)
    placed = (
        P(ALL, None),
        P(DP, None),
        P(None, TENSOR),
        P(TENSOR, None),
        P(None, None, TENSOR),
        P(TENSOR, None),
        P(),
        P(ALL, None),
    )
    return jax.shard_map(
        per_device,
        mesh=split,
        in_specs=placed,
        out_specs=(
            P(ALL, None),
            P(ALL, None),
            P(DP, TENSOR),
            P(TENSOR, DP),
            P(None, DP, TENSOR),
            P(TENSOR, DP),
            P(None, DP),
        ),
        check_vma=False,
    )
```
